128 devices in a mesh: seq: 64 (over x_lo, y, z, core), mp: 2 (over x_hi).
Axes of the slice: x: 4 (x_hi: 2, x_lo: 2; x = x_hi * 2 + x_lo), y: 4, z: 4, core: 2. Of those that a mesh axis runs over, the one named last changes fastest.
Arguments:
- tokens: bfloat16 [16384, 2048], P('seq'), may hold values from -16 to 16
- cotangent: bfloat16 [16384, 2048], P('seq'), may hold values from -16 to 16
- next_kv_grad: bfloat16 [16384, 256], P('seq'), may hold values from -6 to 6
- seq_lengths: int32 [6], replicated, may hold values from 1024 to 4096, as said below
- pad_counts: int32 [6], replicated, may hold values from 0 to 1024, as said below
- norm_attn: float32 [2048], replicated, may hold values from 0.1 to 1.9
- norm_ffn: float32 [2048], replicated, may hold values from 0.1 to 1.9
- w_query: bfloat16 [2048, 2048], P(None, 'mp'), may hold values from -0.125 to 0.125
- w_keyval: bfloat16 [2048, 256], replicated, may hold values from -0.125 to 0.125
- w_out: bfloat16 [2048, 2048], P('mp'), may hold values from -0.5 to 0.5
- w_gate: bfloat16 [2048, 5632], P(None, 'mp'), may hold values from -0.125 to 0.125
- w_up: bfloat16 [2048, 5632], P(None, 'mp'), may hold values from -0.125 to 0.125
- w_down: bfloat16 [5632, 2048], P('mp'), may hold values from -0.078125 to 0.078125
Outputs:
- mixed: bfloat16 [16384, 2048], P('seq')
- input_grad: bfloat16 [16384, 2048], P('seq')
- shared_kv: bfloat16 [16384, 256], P('seq')
- shared_grad: float32 [16384, 256], P('seq')
- grad_norm_attn: float32 [2048], P('seq')
- grad_norm_ffn: float32 [2048], P('seq')
- grad_query: float32 [2048, 2048], P('seq', 'mp')
- grad_keyval: float32 [2048, 256], P('seq')
- grad_out: float32 [2048, 2048], P('mp', 'seq')
- grad_gate: float32 [2048, 5632], P('seq', 'mp')
- grad_up: float32 [2048, 5632], P('seq', 'mp')
- grad_down: float32 [5632, 2048], P('mp', 'seq')
The draws below stay inside these ranges and needn't reach their ends.
Inputs may be any that keep to these rules, and one draw needn't show every extreme that they name: `seq_lengths`: 6 lengths in token order, summing to 16384, each at least min(1024, 4096); one is exactly 4096. `pad_counts`: at most a quarter of the sequence's length, rounded down; a sequence of length 4096 has exactly 1024.
All inputs are finite; a program needn't handle non-finite values.
Results may differ from the reference program's by a relative error of at most 0.017.
Values may be sent and summed in bfloat16 or wider, within the bound.
No kernel may reach another device: no remote copies, remote signals or barrier semaphores. Data moves between devices by JAX's collectives and lax.ppermute only.
A program may use at most 320 MiB of HBM per device.

```python
from functools import partial
import jax
import jax.numpy as jnp
from jax import lax

D = 2048
HEADS = 16
HD = 128
FF = 5632
WINDOW = 512
LMIN = 1024
TOKENS = 16384
LONGEST = 4096
NSEQ = 6


def make_lengths(key):
    count = NSEQ
    longest = LONGEST
    if count == 1:
        return jnp.full((1,), TOKENS, jnp.int32)
    rest = TOKENS - longest - (count - 1) * LMIN
    share = rest // (count - 1)
    extra = rest - share * (count - 1)
    room = max(min(share, longest - LMIN - share - extra), 0)
    key_wobble, key_place = jax.random.split(key)
    wobble = jax.random.randint(key_wobble, (count - 1,), 0, room + 1).astype(jnp.int32)
    others = LMIN + share + wobble - jnp.roll(wobble, 1)
    others = others.at[0].add(extra)
    whole = jnp.concatenate([others.astype(jnp.int32), jnp.full((1,), longest, jnp.int32)])
    return jnp.roll(whole, jax.random.randint(key_place, (), 0, count)).astype(jnp.int32)


def draw_seq_lengths(key, part):
    return make_lengths(key)


def draw_pad_counts(key, part):
    lengths = make_lengths(key)
    key = jax.random.fold_in(key, 7)
    bits = jax.random.randint(key, (NSEQ,), 0, 1 << 20).astype(jnp.int32)
    drawn = (bits % (lengths // 4 + 1)).astype(jnp.int32)
    return jnp.where(lengths == LONGEST, lengths // 4, drawn).astype(jnp.int32)


def strengthened(values, stream_key, source, target, blocks, factor):
    owner, partner = [(jnp.arange(values.shape[axis_at]) // (values.shape[axis_at] // blocks)).reshape([-1 if axis == axis_at else 1 for axis in range(values.ndim)]) for axis_at in (source, target)]
    chosen = jax.random.permutation(stream_key, blocks)[partner]
    strong = (owner == chosen) | (owner == (partner + blocks // 2) % blocks)
    return jnp.where(strong, factor * values, values)


def shard_levels(key, dims, pieces, least, high):
    factor_of = 1.0
    for dim, blocks in pieces:
        draws = jax.random.uniform(jax.random.fold_in(jax.random.fold_in(key, 6), dim), (blocks,), jnp.float32, least / len(pieces), high / len(pieces))
        factor_of = factor_of * jnp.repeat(jnp.exp(draws), dims[dim] // blocks).reshape((-1,) + (1,) * (len(dims) - 1 - dim))
    return factor_of


def scatter_about(key, extent, deviation, bound, pieces=(), kind=jnp.bfloat16):
    loudness = shard_levels(key, extent, pieces, -0.22, 0.18) if pieces else 1.0
    values = jax.random.normal(key, extent, jnp.float32) * deviation * loudness
    return jnp.minimum(jnp.maximum(values, -bound), bound).astype(kind)


def heavy_noise(own_key, dims, width, reach, cuts, heavy, kind=jnp.bfloat16):
    values = width * jax.random.normal(own_key, dims, jnp.float32)
    if cuts:
        values = values * shard_levels(own_key, dims, cuts, -0.22, 0.18)
    return jnp.clip(strengthened(values, jax.random.fold_in(own_key, 3), *heavy), -reach, reach).astype(kind)


def setup_inputs(seed: int = 0) -> dict:
    seeds = jax.random.split(jax.random.key(seed), 14)
    tokens = heavy_noise(seeds[0], (TOKENS, D), 1.0, 16.0, ((0, 64),), (0, 1, 64, 4.0))
    cotangent = heavy_noise(seeds[1], (TOKENS, D), 1.0, 16.0, ((0, 64),), (0, 1, 64, 4.0))
    next_kv_grad = scatter_about(seeds[2], (TOKENS, 2 * HD), 1.0, 6.0, ((0, 64),))
    seq_lengths = draw_seq_lengths(jax.random.fold_in(seeds[13], 71), 0)
    pad_counts = draw_pad_counts(jax.random.fold_in(seeds[13], 71), 0)
    norm_attn = jnp.clip(1.0 + 0.18 * jax.random.normal(seeds[5], (D,), jnp.float32), 0.1, 1.9)
    norm_ffn = jnp.clip(1.0 + 0.18 * jax.random.normal(seeds[6], (D,), jnp.float32), 0.1, 1.9)
    w_query = scatter_about(seeds[7], (D, HEADS * HD), D ** -0.5, 0.125, ((1, 2),))
    w_keyval = scatter_about(seeds[8], (D, 2 * HD), D ** -0.5, 0.125)
    w_out = scatter_about(seeds[9], (HEADS * HD, D), (HEADS * HD // 16) ** -0.5, 0.5, ((0, 2),))
    w_gate = scatter_about(seeds[10], (D, FF), D ** -0.5, 0.125, ((1, 2),))
    w_up = scatter_about(seeds[11], (D, FF), D ** -0.5, 0.125, ((1, 2),))
    w_down = scatter_about(seeds[12], (FF, D), FF ** -0.5, 0.078125, ((0, 2),))
    return dict(tokens=tokens, cotangent=cotangent, next_kv_grad=next_kv_grad, seq_lengths=seq_lengths, pad_counts=pad_counts, norm_attn=norm_attn, norm_ffn=norm_ffn, w_query=w_query, w_keyval=w_keyval, w_out=w_out, w_gate=w_gate, w_up=w_up, w_down=w_down)


EPSILON = 1e-05
THETA = 10000.0
MASKED = -1e+30

@jax.custom_vjp
def low(v):
    return lax.optimization_barrier(v.astype(jnp.bfloat16)).astype(jnp.float32)

@jax.custom_vjp
def low_back(v):
    return v

def low_keep(v):
    return (low(v), None)

def low_pass(kept, grad):
    return (grad,)

def back_keep(v):
    return (v, None)

def back_low(kept, grad):
    return (low(grad),)
low.defvjp(low_keep, low_pass)
low_back.defvjp(back_keep, back_low)

def token_facts(token_idx, seq_lengths, pad_counts):
    ends = jnp.cumsum(seq_lengths).astype(jnp.int32)
    which = lax.optimization_barrier(jnp.sum((token_idx[:, None] >= ends[None, :]).astype(jnp.int32), axis=1)).astype(jnp.int32)
    member = which[:, None] == jnp.arange(seq_lengths.shape[0], dtype=jnp.int32)[None, :]
    begin = lax.optimization_barrier(jnp.sum(jnp.where(member, (ends - seq_lengths)[None, :], 0), axis=1)).astype(jnp.int32)
    live = lax.optimization_barrier(jnp.sum(jnp.where(member, (seq_lengths - pad_counts)[None, :], 0), axis=1)).astype(jnp.int32)
    place = (token_idx - begin).astype(jnp.int32)
    return (jnp.where(token_idx >= 0, which, -1).astype(jnp.int32), place, place < live)

def rotation(place):
    half = HD // 2
    freqs = jnp.exp(-jnp.log(THETA) * jnp.arange(half, dtype=jnp.float32) * 2.0 / HD)
    angle = place.astype(jnp.float32)[:, None] * freqs[None, :]
    return (jnp.cos(angle), jnp.sin(angle))

def rotate(value, cos_table, sin_table):
    half = value.shape[-1] // 2
    lower_half = value[..., :half]
    upper_half = value[..., half:]
    return jnp.concatenate([lower_half * cos_table - upper_half * sin_table, upper_half * cos_table + lower_half * sin_table], axis=-1)

def matmul(left, right):
    return jnp.dot(left, right, precision=lax.Precision.HIGHEST)

def rms_norm(value, gain):
    return value * lax.rsqrt(lax.optimization_barrier(jnp.mean(value * value, axis=-1, keepdims=True)) + EPSILON) * gain

def attend_block(block_idx, query, padded_kv, seq_pad, real_pad):
    start = (block_idx * WINDOW).astype(jnp.int32)
    query_blk = lax.dynamic_slice_in_dim(query, start, WINDOW, 0)
    kv_blk = lax.dynamic_slice_in_dim(padded_kv, start, 2 * WINDOW, 0)
    seq_q = lax.dynamic_slice_in_dim(seq_pad, start + WINDOW, WINDOW, 0)
    seq_k = lax.dynamic_slice_in_dim(seq_pad, start, 2 * WINDOW, 0)
    real_k = lax.dynamic_slice_in_dim(real_pad, start, 2 * WINDOW, 0)
    tok_q = start + jnp.arange(WINDOW, dtype=jnp.int32)
    tok_k = start - WINDOW + jnp.arange(2 * WINDOW, dtype=jnp.int32)
    allowed = (seq_q[:, None] == seq_k[None, :]) & (tok_k[None, :] <= tok_q[:, None]) & (tok_q[:, None] - tok_k[None, :] < WINDOW) & (real_k[None, :] | (tok_k[None, :] == tok_q[:, None]))
    scores = jnp.einsum('qhd,kd->hqk', query_blk, kv_blk[:, :HD], precision=lax.Precision.HIGHEST) * HD ** (-0.5)
    scores = low_back(scores)
    scores = jnp.where(allowed[None], scores, MASKED)
    row_max = lax.optimization_barrier(jnp.max(scores, axis=-1, keepdims=True))
    exps = jnp.exp(scores - row_max)
    prob = low(exps / lax.optimization_barrier(jnp.sum(exps, axis=-1, keepdims=True)))
    attn = jnp.einsum('hqk,kd->qhd', prob, kv_blk[:, HD:], precision=lax.Precision.HIGHEST)
    return attn.reshape(WINDOW, HEADS * HD)

def reference(tokens, cotangent, next_kv_grad, seq_lengths, pad_counts, norm_attn, norm_ffn, w_query, w_keyval, w_out, w_gate, w_up, w_down):
    token_idx = jnp.arange(TOKENS, dtype=jnp.int32)
    seq_ids, place, real = token_facts(token_idx, seq_lengths, pad_counts)
    cos_table, sin_table = rotation(place)
    seq_pad = jnp.concatenate([jnp.full((WINDOW,), -1, jnp.int32), seq_ids])
    real_pad = jnp.concatenate([jnp.zeros((WINDOW,), bool), real])
    blocks = jnp.arange(TOKENS // WINDOW, dtype=jnp.int32)

    def forward(x_in, gain_a, gain_b, wq, wkv, wo, wg, wu, wd, zero_kv):
        hid_a = low(rms_norm(x_in, gain_a))
        query = low_back(matmul(hid_a, wq)).reshape(TOKENS, HEADS, HD)
        query = low(rotate(query, cos_table[:, None, :], sin_table[:, None, :]))
        keyval = low_back(matmul(hid_a, wkv))
        shared = low(jnp.concatenate([rotate(keyval[:, :HD], cos_table, sin_table), keyval[:, HD:]], axis=1)) + zero_kv
        padded_kv = jnp.concatenate([jnp.zeros((WINDOW, 2 * HD), jnp.float32), shared], axis=0)
        block_fn = jax.checkpoint(partial(attend_block, query=query, padded_kv=padded_kv, seq_pad=seq_pad, real_pad=real_pad))
        attn = lax.map(block_fn, blocks).reshape(TOKENS, HEADS * HD)
        attn = low(low_back(attn))
        mid = x_in + low_back(matmul(attn, wo))
        hid_b = low(rms_norm(mid, gain_b))
        gate = low_back(matmul(hid_b, wg))
        upval = low_back(matmul(hid_b, wu))
        act = low(low_back(jax.nn.silu(gate) * upval))
        mixed = mid + low_back(matmul(act, wd))
        return (mixed, shared)
    primals = (tokens.astype(jnp.float32), norm_attn, norm_ffn, w_query.astype(jnp.float32), w_keyval.astype(jnp.float32), w_out.astype(jnp.float32), w_gate.astype(jnp.float32), w_up.astype(jnp.float32), w_down.astype(jnp.float32), jnp.zeros((TOKENS, 2 * HD), jnp.float32))
    (mixed, shared), pullback = jax.vjp(forward, *primals)
    grads = pullback((cotangent.astype(jnp.float32), next_kv_grad.astype(jnp.float32)))
    d_x, g_gain_a, g_gain_b, g_query, g_keyval, g_out, g_gate, g_up, g_down, g_shared = grads
    return (mixed.astype(jnp.bfloat16), d_x.astype(jnp.bfloat16), shared.astype(jnp.bfloat16), g_shared, g_gain_a, g_gain_b, g_query, g_keyval, g_out, g_gate, g_up, g_down)
```

```python
import jax
import jax.numpy as jnp
from jax import lax
from jax.sharding import Mesh, PartitionSpec as P

HD = 128
WINDOW = 512
EPSILON = 1e-05
THETA = 10000.0
MASKED = -1e30
SEQ = ("xl", "y", "z", "c")
SIZES = {"xl": 2, "y": 4, "z": 4, "c": 2, "mp": 2}
BF = jnp.bfloat16
F32 = jnp.float32


def step_to(value, axis, steps):
    count = SIZES[axis]
    return lax.ppermute(value, axis, [(i, (i + steps) % count) for i in range(count)])


def shifted(value, steps):
    count = 64
    first, last = max(0, -steps), min(count, count - steps)
    return lax.ppermute(value, SEQ, [(i, i + steps) for i in range(first, last)])


def rounded(value):
    return lax.optimization_barrier(value.astype(BF)).astype(F32)


def mm(left, right):
    return jnp.dot(left, right, preferred_element_type=F32)


def contract_cols(left, right):
    return lax.dot_general(left, right, (((1,), (1,)), ((), ())), preferred_element_type=F32)


def pick(stack, index):
    return lax.dynamic_index_in_dim(stack, index, 0, keepdims=False)


def mp_sum(value):
    own = value.astype(BF)
    return own.astype(F32) + step_to(own, "mp", 1).astype(F32)


def token_facts(token_idx, seq_lengths, pad_counts):
    ends = jnp.cumsum(seq_lengths)
    which = jnp.sum((token_idx[:, None] >= ends[None, :]).astype(jnp.int32), axis=1)
    member = which[:, None] == jnp.arange(seq_lengths.shape[0], dtype=jnp.int32)[None, :]
    begin = jnp.sum(jnp.where(member, (ends - seq_lengths)[None, :], 0), axis=1)
    live = jnp.sum(jnp.where(member, (seq_lengths - pad_counts)[None, :], 0), axis=1)
    place = token_idx - begin
    return (jnp.where(token_idx >= 0, which, -1), place, place < live)


def rotation(place):
    half = HD // 2
    freqs = jnp.exp(-jnp.log(THETA) * jnp.arange(half, dtype=F32) * 2.0 / HD)
    angle = place.astype(F32)[:, None] * freqs[None, :]
    return (jnp.cos(angle), jnp.sin(angle))


def rotate(value, cos_table, sin_table):
    half = value.shape[-1] // 2
    low, high = value[..., :half], value[..., half:]
    return jnp.concatenate(
        [low * cos_table - high * sin_table, high * cos_table + low * sin_table], axis=-1
    )


def unrotate(value, cos_table, sin_table):
    return rotate(value, cos_table, -sin_table)


def norm_back(d_normed, normed, inverse):
    return inverse * (d_normed - normed * jnp.mean(d_normed * normed, axis=-1, keepdims=True))


def by_core(value, order):
    rows = value.T.reshape(2, 4, 4, 2, 32, value.shape[0])
    return rows.transpose((3,) + order + (4, 5)).reshape(2, 1024, value.shape[0])


def core_tokens(value, order):
    c = lax.axis_index("c")
    halves = by_core(value, order)
    return jnp.concatenate([pick(halves, c), step_to(pick(halves, 1 - c), "c", 1)], axis=1)


def ring_gather(value, axis):
    before, after = step_to(value, axis, 1), step_to(value, axis, -1)
    half = value.shape[0] // 2
    far_a, far_b = step_to(before[:half], axis, 1), step_to(after[half:], axis, -1)
    return [value, before, jnp.concatenate([far_a, far_b], axis=0), after]


def deal(value, axis):
    tokens, width = value.shape
    i = lax.axis_index(axis)
    parts = value.reshape(tokens, 4, width // 4).transpose(1, 0, 2)
    out = [pick(parts, i)]
    for k in (1, 2, 3):
        out.append(step_to(pick(parts, (i + k) % 4), axis, k))
    return [jnp.concatenate([p, step_to(p, "c", 1)], axis=0) for p in out]


def ring_sum(value, axis):
    i = lax.axis_index(axis)
    parts = value.reshape(4, value.shape[0] // 4, value.shape[1])
    half = parts.shape[1] // 2
    far = pick(parts, (i + 2) % 4).astype(BF)
    from_low, from_high = step_to(far[:half], axis, 1), step_to(far[half:], axis, -1)
    up, down = pick(parts, (i + 1) % 4), pick(parts, (i + 3) % 4)
    up = jnp.concatenate([up[:half] + from_low.astype(F32), up[half:]], axis=0).astype(BF)
    down = jnp.concatenate([down[:half], down[half:] + from_high.astype(F32)], axis=0).astype(BF)
    low, high = step_to(up, axis, 1), step_to(down, axis, -1)
    return pick(parts, i) + low.astype(F32) + high.astype(F32)


def pair_sum(value):
    xl = lax.axis_index("xl")
    own = lax.dynamic_index_in_dim(value, xl, 1, keepdims=False)
    other = lax.dynamic_index_in_dim(value, 1 - xl, 1, keepdims=False).astype(BF)
    return own + step_to(other, "xl", 1).astype(F32)


def undeal(value, axis):
    i = lax.axis_index(axis)
    value = value.astype(BF)
    got = [pick(value, i)]
    for k in (1, 2, 3):
        got.append(step_to(pick(value, (i + k) % 4), axis, k))
    stack = jnp.stack(got)
    return jnp.concatenate([pick(stack, (i - part) % 4) for part in range(4)], axis=1)


def shards(
    tokens,
    cotangent,
    next_kv_grad,
    seq_lengths,
    pad_counts,
    norm_attn,
    norm_ffn,
    w_query,
    w_keyval,
    w_out,
    w_gate,
    w_up,
    w_down,
):
    tok_rows = tokens.shape[0]
    rim_shards = (WINDOW + tok_rows - 1) // tok_rows
    rim_rows = rim_shards * tok_rows
    place_in_seq = lax.axis_index(SEQ)
    first_row = place_in_seq * tok_rows
    own_idx = first_row + jnp.arange(tok_rows, dtype=jnp.int32)
    key_idx = first_row - rim_rows + jnp.arange(rim_rows + tok_rows, dtype=jnp.int32)
    seq_q, place_q, real_q = token_facts(own_idx, seq_lengths, pad_counts)
    seq_k, place_k, real_k = token_facts(key_idx, seq_lengths, pad_counts)
    allowed = (
        (seq_q[:, None] == seq_k[None, :])
        & (key_idx[None, :] <= own_idx[:, None])
        & (own_idx[:, None] - key_idx[None, :] < WINDOW)
        & (real_k[None, :] | (key_idx[None, :] == own_idx[:, None]))
    )
    cos_table, sin_table = rotation(place_q)
    head_cnt = w_query.shape[1] // HD
    scale = HD ** (-0.5)
    yzx, zyx = (1, 2, 0), (2, 1, 0)

    cot_all = lax.all_gather(core_tokens(cotangent, zyx), "y")

    x_full = tokens.astype(F32)
    inv_a = lax.rsqrt(jnp.mean(x_full * x_full, axis=-1, keepdims=True) + EPSILON)
    normed_a = x_full * inv_a
    hid_a = (normed_a * norm_attn).astype(BF)
    query = mm(hid_a, w_query).reshape(tok_rows, head_cnt, HD)
    query = rotate(query, cos_table[:, None, :], sin_table[:, None, :]).astype(BF)
    keyval = mm(hid_a, w_keyval)
    shared = jnp.concatenate(
        [rotate(keyval[:, :HD], cos_table, sin_table), keyval[:, HD:]], axis=1
    ).astype(BF)
    rim_pieces = [shifted(shared, offset) for offset in range(rim_shards, 0, -1)]
    keys_all = jnp.concatenate(rim_pieces + [shared], axis=0)

    def scores_of(key_rows):
        scores = (
            jnp.einsum("qhd,kd->hqk", query, key_rows[:, :HD], preferred_element_type=F32) * scale
        )
        return jnp.where(allowed[None], scores, MASKED)

    scores = scores_of(keys_all)
    row_max = jnp.max(scores, axis=-1, keepdims=True)
    exps = jnp.exp(scores - row_max)
    row_total = jnp.sum(exps, axis=-1, keepdims=True)
    prob = (exps / row_total).astype(BF)
    log_total = row_max + jnp.log(row_total)
    attn = jnp.einsum("hqk,kd->qhd", prob, keys_all[:, HD:], preferred_element_type=F32)
    attn = attn.reshape(tok_rows, head_cnt * HD).astype(BF)
    middle = x_full + mp_sum(mm(attn, w_out))
    inv_b = lax.rsqrt(jnp.mean(middle * middle, axis=-1, keepdims=True) + EPSILON)
    normed_b = middle * inv_b
    hid_b = (normed_b * norm_ffn).astype(BF)
    hid_b_all = ring_gather(core_tokens(hid_b, yzx), "z")
    gate = mm(hid_b, w_gate)
    upval = mm(hid_b, w_up)
    sigm = jax.nn.sigmoid(gate)
    act = (gate * sigm * upval).astype(BF)
    d_act = rounded(contract_cols(cotangent, w_down))
    d_gate = (d_act * upval * sigm * (1.0 + gate * (1.0 - sigm))).astype(BF)
    d_up = (d_act * gate * sigm).astype(BF)
    d_hid_b = mp_sum(contract_cols(d_gate, w_gate) + contract_cols(d_up, w_up))

    d_gu_parts = deal(jnp.concatenate([d_gate, d_up], axis=1), "z")
    act_parts = deal(act, "y")
    y = lax.axis_index("y")

    mixed = (middle + mp_sum(mm(act, w_down))).astype(BF)

    g_gu = sum(mm(a, b) for a, b in zip(hid_b_all, d_gu_parts))
    g_down = sum(mm(pick(cot_all, (y - k) % 4), act_parts[k]) for k in range(4))

    d_out = cotangent.astype(F32)
    d_middle = d_out + norm_back(d_hid_b * norm_ffn, normed_b, inv_b)
    d_middle_b = d_middle.astype(BF)
    d_attn = contract_cols(d_middle_b, w_out).astype(BF).reshape(tok_rows, head_cnt, HD)
    attn_pair = jnp.concatenate([attn, step_to(attn, "c", 1)], axis=0)
    g_out = mm(core_tokens(d_middle_b, yzx), attn_pair)

    prob_full = jnp.exp(scores_of(keys_all) - log_total)
    prob_back = prob_full.astype(BF)
    d_prob = jnp.einsum("qhd,kd->hqk", d_attn, keys_all[:, HD:], preferred_element_type=F32)
    delta = jnp.sum(prob_full * d_prob, axis=-1, keepdims=True)
    d_score = (prob_full * (d_prob - delta)).astype(BF)
    d_query = (
        jnp.einsum("hqk,kd->qhd", d_score, keys_all[:, :HD], preferred_element_type=F32) * scale
    )
    d_key = jnp.einsum("hqk,qhd->kd", d_score, query, preferred_element_type=F32) * scale
    d_value = jnp.einsum("hqk,qhd->kd", prob_back, d_attn, preferred_element_type=F32)
    d_shared = jnp.concatenate([d_key, d_value], axis=1)
    local_grad = d_shared[rim_rows:]
    for offset in range(1, rim_shards + 1):
        piece = d_shared[(rim_shards - offset) * tok_rows : (rim_shards - offset + 1) * tok_rows]
        local_grad = local_grad + shifted(piece.astype(BF), -offset).astype(F32)
    d_query_b = (
        unrotate(d_query, cos_table[:, None, :], sin_table[:, None, :])
        .reshape(tok_rows, head_cnt * HD)
        .astype(BF)
    )
    hid_a_pair = core_tokens(hid_a, yzx)
    part_hid_a = mp_sum(contract_cols(d_query_b, w_query))
    summed_kv = mp_sum(local_grad)
    shared_grad = summed_kv + next_kv_grad.astype(F32)
    d_keyval = jnp.concatenate(
        [unrotate(shared_grad[:, :HD], cos_table, sin_table), shared_grad[:, HD:]], axis=1
    ).astype(BF)
    d_qkv = jnp.concatenate([d_query_b, d_keyval], axis=1)
    d_qkv = jnp.concatenate([d_qkv, step_to(d_qkv, "c", 1)], axis=0)
    g_qkv = mm(hid_a_pair, d_qkv)

    s_gu = ring_sum(g_gu, "y")
    s_gu = undeal(pair_sum(s_gu.reshape(4, 2, 32, -1)), "z").astype(F32)
    s_gate, s_up = jnp.split(s_gu, 2, axis=1)
    s_down = ring_sum(g_down, "z")
    s_down = undeal(pair_sum(s_down.reshape(4, 2, 32, -1)), "y").astype(F32).T
    s_out = ring_sum(ring_sum(g_out, "y"), "z")
    s_out = pair_sum(s_out.reshape(1, 2, 32, -1))[0].T
    s_qkv = ring_sum(ring_sum(g_qkv, "y"), "z")
    s_qkv = pair_sum(s_qkv.reshape(1, 2, 32, -1))[0]
    s_query, s_keyval = s_qkv[:, : head_cnt * HD], s_qkv[:, head_cnt * HD :]

    d_hid_a = part_hid_a + contract_cols(d_keyval, w_keyval)
    input_grad = (d_middle + norm_back(d_hid_a * norm_attn, normed_a, inv_a)).astype(BF)

    mine = place_in_seq * 32

    def rows(array):
        return lax.dynamic_slice_in_dim(array, mine, 32, 0).astype(F32)

    gain_b = jnp.sum(rows(w_gate) * s_gate, axis=1) + jnp.sum(rows(w_up) * s_up, axis=1)
    gain_a = jnp.sum(rows(w_query) * s_query, axis=1)
    gains = jnp.stack([gain_a, gain_b])
    gains = gains + step_to(gains, "mp", 1)
    gain_kv = jnp.sum(rows(w_keyval) * s_keyval, axis=1)
    s_gain_a = (gains[0] + gain_kv) / lax.dynamic_slice_in_dim(norm_attn, mine, 32, 0)
    s_gain_b = gains[1] / lax.dynamic_slice_in_dim(norm_ffn, mine, 32, 0)
    return (
        mixed,
        input_grad,
        shared,
        shared_grad,
        s_gain_a,
        s_gain_b,
        s_query,
        s_keyval,
        s_out,
        s_gate,
        s_up,
        s_down,
    )


def solution(mesh):
    fine = Mesh(mesh.devices.reshape(2, 4, 4, 2, 2), SEQ + ("mp",))
    rows = P(SEQ, None)
    placed = (
        rows,
        rows,
        rows,
        P(),
        P(),
        P(),
        P(),
        P(None, "mp"),
        P(),
        P("mp", None),
        P(None, "mp"),
        P(None, "mp"),
        P("mp", None),
    )
    return jax.shard_map(
        shards,
        mesh=fine,
        in_specs=placed,
        out_specs=(
            rows,
            rows,
            rows,
            rows,
            P(SEQ),
            P(SEQ),
            P(SEQ, "mp"),
            rows,
            P("mp", SEQ),
            P(SEQ, "mp"),
            P(SEQ, "mp"),
            P("mp", SEQ),
        ),
        check_vma=False,
    )
```

```python
import functools

import jax
import jax.numpy as jnp
from jax import lax
from jax.experimental import pallas as pl
from jax.experimental.pallas import tpu as pltpu
from jax.sharding import Mesh, PartitionSpec as P

HD = 128
WINDOW = 512
EPSILON = 1e-05
THETA = 10000.0
MASKED = -1e30
SEQ = ("xl", "y", "z", "c")
SIZES = {"xl": 2, "y": 4, "z": 4, "c": 2, "mp": 2}
BF = jnp.bfloat16
F32 = jnp.float32
TOK = 256
D = 2048
HEADS = 8
FF = 2816
SCALE = HD ** (-0.5)
LOG2E = 1.4426950408889634
VMEM = pl.BlockSpec(memory_space=pltpu.VMEM)
SMEM = pl.BlockSpec(memory_space=pltpu.SMEM)
HBM = pl.BlockSpec(memory_space=pl.ANY)
MIB = 2**20


def nn(left, right):
    return jnp.dot(left, right, preferred_element_type=F32)


def nt(left, right):
    return lax.dot_general(left, right, (((1,), (1,)), ((), ())), preferred_element_type=F32)


def tn(left, right):
    return lax.dot_general(left, right, (((0,), (0,)), ((), ())), preferred_element_type=F32)


def shape(*dims, dtype=BF):
    return jax.ShapeDtypeStruct(dims, dtype)


def kernel_call(body, outs, args, specs, scratch=(), vmem=56, after=(), carry=(), out_specs=None):
    single = not isinstance(outs, tuple)
    outs = (outs,) if single else outs
    if out_specs is None:
        out_specs = (VMEM,) * len(outs)
    given, extra, passed = len(args), len(after), len(carry)

    def run(*refs):
        rest = refs[given + extra + passed :]
        body(*refs[:given], *rest[: len(outs)], *rest[len(outs) + passed :])

    result = pl.pallas_call(
        run,
        out_shape=outs + tuple(shape(*c.shape, dtype=c.dtype) for c in carry),
        in_specs=list(specs) + [HBM] * (extra + passed),
        out_specs=tuple(out_specs) + (HBM,) * passed,
        scratch_shapes=list(scratch),
        input_output_aliases={given + extra + i: len(outs) + i for i in range(passed)},
        compiler_params=pltpu.CompilerParams(vmem_limit_bytes=vmem * MIB),
        cost_estimate=pl.CostEstimate(flops=1000, bytes_accessed=1000, transcendentals=0),
    )(*args, *after, *carry)
    main = result[0] if single else result[: len(outs)]
    return (main, result[len(outs) :]) if carry else main


def fetch(source, target, sems, pieces):
    copies = [
        pltpu.make_async_copy(source.at[piece], target.at[piece], sems.at[i])
        for i, piece in enumerate(pieces)
    ]
    for copy in copies:
        copy.start()
    return copies


def columns(count, width):
    return [(slice(None), pl.ds(i * width, width)) for i in range(count)]


def row_blocks(count, height):
    return [(pl.ds(i * height, height), slice(None)) for i in range(count)]


def turn(value, cos_table, sin_table):
    swapped = jnp.concatenate([value[:, HD // 2 :], value[:, : HD // 2]], axis=1)
    return value * cos_table + swapped * sin_table


def norm_kv_body(x_ref, gain_ref, w_ref, cos_ref, sin_ref, hid_ref, kv_ref):
    x = x_ref[...].astype(F32)
    inv = lax.rsqrt(jnp.mean(x * x, axis=1, keepdims=True) + EPSILON)
    hid = (x * inv * gain_ref[...]).astype(BF)
    hid_ref[...] = hid
    kv = nn(hid, w_ref[...])
    kv_ref[:, :HD] = turn(kv[:, :HD], cos_ref[...], sin_ref[...]).astype(BF)
    kv_ref[:, HD:] = kv[:, HD:].astype(BF)


def query_body(hid_ref, cos_ref, sin_ref, w_ref, q_ref, buf, sems):
    copies = fetch(w_ref, buf, sems, columns(4, 256))
    hid = hid_ref[...]
    for j in range(4):
        copies[j].wait()
        part = nn(hid, buf[:, j * 256 : j * 256 + 256])
        for h in range(2):
            q_ref[:, j * 256 + h * HD : j * 256 + h * HD + HD] = turn(
                part[:, h * HD : h * HD + HD], cos_ref[...], sin_ref[...]
            ).astype(BF)


def local_body(own_ref, near_ref, far_ref, out_ref):
    total = own_ref[...] + near_ref[...].astype(F32) + far_ref[...].astype(F32)
    out_ref[...] = total.astype(BF)


def copies_body(in_ref, out_ref, sems):
    copies = [pltpu.make_async_copy(in_ref, out_ref.at[k], sems.at[k]) for k in range(4)]
    for copy in copies:
        copy.start()
    for copy in copies:
        copy.wait()


def add_body(a_ref, b_ref, out_ref):
    for k in range(4):
        out_ref[k] = (a_ref[k].astype(F32) + b_ref[k].astype(F32)).astype(BF)


def fence_body(in_ref, out_ref):
    out_ref[...] = in_ref[...]


def sum_body(groups, *refs):
    out_ref, at = refs[-1], 0
    for count in groups:
        group, refs = refs[:count], refs[count:]
        stacked = count == 1 and len(group[0].shape) == 3
        pieces = [group[0].at[k] for k in range(4)] if stacked else group
        total = sum(p[...].astype(F32) for p in pieces)
        out_ref[:, at : at + total.shape[1]] = total.astype(BF)
        at += total.shape[1]


def fill_bias(first_ref, lengths_ref, pads_ref, bias):
    first = first_ref[0]
    count = lengths_ref.shape[0]
    starts, lives = [], []
    begin = jnp.int32(0)
    for s in range(count):
        starts.append(begin)
        lives.append(begin + lengths_ref[s] - pads_ref[s])
        begin = begin + lengths_ref[s]
    for b in range(2):
        row = lax.broadcasted_iota(jnp.int32, (128, 1), 0) + b * 128
        col = lax.broadcasted_iota(jnp.int32, (1, 640), 1) + b * 128
        query = row + first
        key = col + (first - WINDOW)
        low = jnp.zeros((128, 1), jnp.int32)
        real = jnp.zeros((1, 640), jnp.int32)
        for s in range(count):
            low = jnp.where(query >= starts[s], starts[s], low)
            real = jnp.where((key >= starts[s]) & (key < lives[s]), 1, real)
        low = jnp.maximum(low, query - (WINDOW - 1))
        here = lax.broadcasted_iota(jnp.int32, (128, 640), 1) + b * 128 + (first - WINDOW)
        when = lax.broadcasted_iota(jnp.int32, (128, 640), 0) + b * 128 + first
        seen = jnp.where(jnp.broadcast_to(real, (128, 640)) > 0, here, when + 1)
        ok = (here == when) | ((here >= low) & (seen <= when))
        bias[b] = jnp.where(ok, 0.0, MASKED)


def two_heads(ref, b, pair):
    rows = slice(b * 128, b * 128 + 128)
    return jnp.concatenate(
        [ref[rows, h * HD : h * HD + HD] for h in (2 * pair, 2 * pair + 1)], axis=0
    )


def attend_body(
    first_ref, lengths_ref, pads_ref, q_ref, far_ref, near_ref, kv_ref, w_ref,
    attn_ref, lse_ref, out_ref, bias, keys, buf, sem,
):
    copy = pltpu.make_async_copy(w_ref, buf, sem.at[0])
    copy.start()
    fill_bias(first_ref, lengths_ref, pads_ref, bias)
    keys[0:256] = far_ref[...]
    keys[256:512] = near_ref[...]
    keys[512:768] = kv_ref[...]
    for b in range(2):
        k = keys[b * 128 : b * 128 + 640, :HD]
        v = keys[b * 128 : b * 128 + 640, HD:]
        for pair in range(4):
            scores = nt(two_heads(q_ref, b, pair), k) * (SCALE * LOG2E)
            scores = scores + jnp.concatenate([bias[b], bias[b]], axis=0)
            top = jnp.max(scores, axis=1, keepdims=True)
            exps = jnp.exp2(scores - top)
            total = jnp.sum(exps, axis=1, keepdims=True)
            out = nn(exps.astype(BF), v) / total
            lse_ref[b * 4 + pair] = top + jnp.log2(total)
            for h in range(2):
                lanes = slice((2 * pair + h) * HD, (2 * pair + h) * HD + HD)
                attn_ref[b * 128 : b * 128 + 128, lanes] = out[h * 128 : h * 128 + 128].astype(BF)
    copy.wait()
    attn = attn_ref[...]
    for j in range(4):
        out_ref[:, j * 512 : j * 512 + 512] = nn(attn, buf[:, j * 512 : j * 512 + 512]).astype(BF)


def d_act_body(cot_ref, w_ref, out_ref, buf, sems):
    copies = fetch(w_ref, buf, sems, row_blocks(2, 1408))
    cot = cot_ref[...]
    for j in range(2):
        copies[j].wait()
        rows = slice(j * 1408, j * 1408 + 1408)
        out_ref[:, rows] = nt(cot, buf[rows]).astype(BF)


def middle_body(x_ref, a_ref, b_ref, gain_ref, mid_ref, hid_ref):
    mid = x_ref[...].astype(F32) + (a_ref[...].astype(F32) + b_ref[...].astype(F32))
    mid_ref[...] = mid
    inv = lax.rsqrt(jnp.mean(mid * mid, axis=1, keepdims=True) + EPSILON)
    hid = (mid * inv * gain_ref[...]).astype(BF)
    hid_ref[...] = hid


ACT_STARTS = (0, 6, 12, 17, 22)


def act_place(tile):
    part = max(i for i in range(4) if ACT_STARTS[i] <= tile)
    return part, (tile - ACT_STARTS[part]) * 128


FFN_STARTS = (0, 4, 12, 22)


def ffn_body(
    hid_ref, d_act_ref, wg_ref, wu_ref,
    d0, d1, d2, d3, act_out, out_ref,
    bufg, bufu, d_buf, act_buf, d_act_buf, semg, semu, sem_in, sem_out,
):
    pieces = [
        (slice(None), pl.ds(low * 128, (high - low) * 128))
        for low, high in zip(FFN_STARTS, FFN_STARTS[1:])
    ]
    gates = [pltpu.make_async_copy(wg_ref.at[p], bufg.at[p], semg.at[i]) for i, p in enumerate(pieces)]
    ups = [pltpu.make_async_copy(wu_ref.at[p], bufu.at[p], semu.at[i]) for i, p in enumerate(pieces)]
    d_act_in = pltpu.make_async_copy(d_act_ref, d_act_buf, sem_in.at[0])
    gates[0].start()
    ups[0].start()
    d_act_in.start()
    for g, u in zip(gates[1:], ups[1:]):
        g.start()
        u.start()
    hid = hid_ref[...]
    for j in range(3):
        low, high = FFN_STARTS[j], FFN_STARTS[j + 1]
        cols = slice(low * 128, high * 128)
        gates[j].wait()
        gate = nn(hid, bufg[:, cols])
        ups[j].wait()
        up = nn(hid, bufu[:, cols])
        if j == 0:
            d_act_in.wait()
        sigm = 1.0 / (1.0 + jnp.exp(-gate))
        silu = gate * sigm
        d_act = d_act_buf[:, cols].astype(F32)
        act = (silu * up).astype(BF)
        d_up = (d_act * silu).astype(BF)
        d_gate = (d_act * up * (sigm + silu * (1.0 - sigm))).astype(BF)
        for tile in range(low, high):
            lanes = slice((tile - low) * 128, (tile - low) * 128 + 128)
            part, at = act_place(tile)
            act_buf[part, :, at : at + 128] = act[:, lanes]
            quarter, at = tile // 11, (tile % 11) * 128
            d_buf[quarter, :, at : at + 128] = d_gate[:, lanes]
            d_buf[2 + quarter, :, at : at + 128] = d_up[:, lanes]
    for part in (2, 3):
        act_buf[part, :, 640:768] = jnp.zeros((TOK, 128), BF)
    z = lax.axis_index("z")
    sends = [pltpu.make_async_copy(act_buf, act_out, sem_out.at[4])]
    for k, d_out in enumerate((d0, d1, d2, d3)):
        sends.append(pltpu.make_async_copy(d_buf.at[(z + k) % 4], d_out, sem_out.at[k]))
    for send in sends:
        send.start()
    for i in range(2):
        rows = slice(i * 1024, i * 1024 + 1024)
        total = nt(d_buf[0], bufg[rows, :1408]) + nt(d_buf[1], bufg[rows, 1408:])
        total += nt(d_buf[2], bufu[rows, :1408]) + nt(d_buf[3], bufu[rows, 1408:])
        out_ref[:, rows] = total.astype(BF)
    for send in sends:
        send.wait()


def down_body(act_ref, w_ref, out_ref, buf, sems):
    copies = fetch(w_ref, buf, sems, columns(4, 512))
    for i in range(4):
        copies[i].wait()
        cols = slice(i * 512, i * 512 + 512)
        total = jnp.zeros((TOK, 512), F32)
        for part in range(4):
            low, high = ACT_STARTS[part] * 128, ACT_STARTS[part + 1] * 128
            total += nn(act_ref[part, :, : high - low], buf[low:high, cols])
        out_ref[:, cols] = total.astype(BF)


def back_body(
    cot_ref, a_ref, b_ref, mid_ref, gain_ref, w_ref,
    d_mid_ref, low_ref, d_attn_ref, buf, sem,
):
    copy = pltpu.make_async_copy(w_ref, buf, sem.at[0])
    copy.start()
    mid = mid_ref[...]
    inv = lax.rsqrt(jnp.mean(mid * mid, axis=1, keepdims=True) + EPSILON)
    normed = mid * inv
    e = (a_ref[...].astype(F32) + b_ref[...].astype(F32)) * gain_ref[...]
    d_mid = cot_ref[...].astype(F32) + inv * (
        e - normed * jnp.mean(e * normed, axis=1, keepdims=True)
    )
    d_mid_ref[...] = d_mid
    low = d_mid.astype(BF)
    low_ref[...] = low
    copy.wait()
    d_attn_ref[...] = nt(low, buf[...]).astype(BF)


def attend_back_body(
    first_ref, lengths_ref, pads_ref, q_ref, far_ref, near_ref, kv_ref, attn_ref, d_attn_ref, lse_ref,
    cos_ref, sin_ref, w_ref,
    dq_ref, d_far_ref, d_near_ref, d_own_ref, out_ref,
    bias, keys, stack_p, stack_d, stack_q, stack_o, total, buf, sem,
):
    copy = pltpu.make_async_copy(w_ref, buf, sem.at[0])
    copy.start()
    fill_bias(first_ref, lengths_ref, pads_ref, bias)
    keys[0:256] = far_ref[...]
    keys[256:512] = near_ref[...]
    keys[512:768] = kv_ref[...]
    total[...] = jnp.zeros_like(total)
    for b in range(2):
        window = slice(b * 128, b * 128 + 640)
        rows = slice(b * 128, b * 128 + 128)
        k = keys[window, :HD]
        v = keys[window, HD:]
        for pair in range(4):
            here = slice(pair * 256, pair * 256 + 256)
            q2 = two_heads(q_ref, b, pair)
            do2 = two_heads(d_attn_ref, b, pair)
            o2 = two_heads(attn_ref, b, pair)
            stack_q[here] = q2
            stack_o[here] = do2
            delta = jnp.sum(do2.astype(F32) * o2.astype(F32), axis=1, keepdims=True)
            scores = nt(q2, k) * (SCALE * LOG2E) + jnp.concatenate([bias[b], bias[b]], axis=0)
            prob = jnp.exp2(scores - lse_ref[b * 4 + pair])
            stack_p[here] = prob.astype(BF)
            d_score = (prob * (nt(do2, v) - delta)).astype(BF)
            stack_d[here] = d_score
            dq = nn(d_score, k) * SCALE
            for h in range(2):
                lanes = slice((2 * pair + h) * HD, (2 * pair + h) * HD + HD)
                dq_ref[rows, lanes] = turn(
                    dq[h * 128 : h * 128 + 128], cos_ref[rows], -sin_ref[rows]
                ).astype(BF)
        total[window, :HD] += tn(stack_d[...], stack_q[...]) * SCALE
        total[window, HD:] += tn(stack_p[...], stack_o[...])
    d_far_ref[...] = total[0:256].astype(BF)
    d_near_ref[...] = total[256:512].astype(BF)
    d_own_ref[...] = total[512:768]
    copy.wait()
    dq = dq_ref[...]
    for j in range(4):
        rows = slice(j * 512, j * 512 + 512)
        out_ref[:, rows] = nt(dq, buf[rows]).astype(BF)


def last_body(x_ref, d_mid_ref, a_ref, b_ref, d_kv_ref, w_ref, gain_ref, out_ref):
    x = x_ref[...].astype(F32)
    inv = lax.rsqrt(jnp.mean(x * x, axis=1, keepdims=True) + EPSILON)
    normed = x * inv
    d_hid = a_ref[...].astype(F32) + b_ref[...].astype(F32) + nt(d_kv_ref[...], w_ref[...])
    e = d_hid * gain_ref[...]
    out = d_mid_ref[...] + inv * (e - normed * jnp.mean(e * normed, axis=1, keepdims=True))
    out_ref[...] = out.astype(BF)


def pair_each(lefts, rights):
    return [list(zip(lefts, rights, strict=True))]


def pair_stacks(lefts, rights):
    return [[(lefts[0].at[k], rights[0].at[k]) for k in range(4)]]


def pair_two(lefts, rights):
    return [[(lefts[0], right)] for right in rights]


def grad_body(axis, pairing, lefts, rights, *refs):
    groups = pairing(refs[:lefts], refs[lefts : lefts + rights])
    outs, buf, sems = refs[lefts + rights : -2], refs[-2], refs[-1]
    me = lax.axis_index("c")
    for block in range(8):
        cols = slice(block * 256, block * 256 + 256)
        at = 0
        for group in groups:
            total = None
            for left, right in group:
                part = tn(left[:, cols], right[...])
                total = part if total is None else total + part
            total = total.astype(BF)
            lanes = slice(at, at + total.shape[1])
            at += total.shape[1]
            xl, y = block // 4, block % 4
            for z in range(4):
                chunk, row = (y, xl * 128 + z * 32) if axis == "y" else (z, xl * 128 + y * 32)
                for core in range(2):
                    rows = total[z * 64 + core * 32 : z * 64 + core * 32 + 32]
                    buf[(me + core) % 2, chunk, row : row + 32, lanes] = rows
    sends = [pltpu.make_async_copy(buf.at[k], out, sems.at[k]) for k, out in enumerate(outs)]
    for send in sends:
        send.start()
    for send in sends:
        send.wait()


def grad(axis, pairing, lefts, rights, n, after=(), carry=()):
    return kernel_call(
        functools.partial(grad_body, axis, pairing, len(lefts), len(rights)),
        (shape(4, 256, n),) * 2,
        (*lefts, *rights),
        [VMEM] * (len(lefts) + len(rights)),
        [pltpu.VMEM((2, 4, 256, n), BF), pltpu.SemaphoreType.DMA((2,))],
        after=after,
        carry=carry,
        out_specs=(HBM,) * 2,
    )


def step_to(value, axis, steps):
    count = SIZES[axis]
    return lax.ppermute(value, axis, [(i, (i + steps) % count) for i in range(count)])


def shifted(value, steps):
    count = 64
    first, last = max(0, -steps), min(count, count - steps)
    return lax.ppermute(value, SEQ, [(i, i + steps) for i in range(first, last)])


def pick(stack, index):
    return lax.dynamic_index_in_dim(stack, index, 0, keepdims=False)


def fence(after, carry=()):
    return kernel_call(
        fence_body, shape(8, 128, dtype=F32), (jnp.zeros((8, 128), F32),), [VMEM], after=after, carry=carry
    )


def from_others(value, axis):
    return [value] + [step_to(value, axis, k) for k in (1, 2, 3)]


def deal(parts, axis):
    return [parts[0]] + [step_to(parts[k], axis, k) for k in (1, 2, 3)]


def both_cores(own, other):
    return (own.astype(F32) + step_to(other, "c", 1).astype(F32)).astype(BF)


def deal_out(parts, axis):
    i = lax.axis_index(axis)
    return deal([pick(parts, (i + k) % 4) for k in range(4)], axis)


def swap(parts, axis):
    return lax.all_to_all(parts, axis, 0, 0, tiled=True)


def scatter(value, axes):
    return lax.all_to_all(value, axes, 0, 0, tiled=True)


def shards(
    tokens,
    cotangent,
    next_kv_grad,
    seq_lengths,
    pad_counts,
    norm_attn,
    norm_ffn,
    w_query,
    w_keyval,
    w_out,
    w_gate,
    w_up,
    w_down,
):
    place_in_seq = lax.axis_index(SEQ)
    first = (place_in_seq * TOK).astype(jnp.int32)
    index = first + jnp.arange(TOK, dtype=jnp.int32)
    begin, start = jnp.zeros((TOK,), jnp.int32), jnp.int32(0)
    for s in range(seq_lengths.shape[0]):
        begin = jnp.where(index >= start, start, begin)
        start = start + seq_lengths[s]
    half = HD // 2
    freqs = jnp.exp(-jnp.log(THETA) * jnp.arange(half, dtype=F32) * 2.0 / HD)
    angle = (index - begin).astype(F32)[:, None] * freqs[None, :]
    cos, sin = jnp.cos(angle), jnp.sin(angle)
    cos_table = jnp.concatenate([cos, cos], axis=1)
    sin_table = jnp.concatenate([-sin, sin], axis=1)
    first = first[None]

    gain_a, gain_b = norm_attn[None], norm_ffn[None]

    hid_a, shared = kernel_call(
        norm_kv_body,
        (shape(TOK, D), shape(TOK, 256)),
        (tokens, gain_a, w_keyval, cos_table, sin_table),
        [VMEM] * 5,
    )
    near, far = shifted(shared, 1), shifted(shared, 2)
    query = kernel_call(
        query_body,
        shape(TOK, 1024),
        (hid_a, cos_table, sin_table, w_query),
        [VMEM, VMEM, VMEM, HBM],
        [pltpu.VMEM((D, 1024), BF), pltpu.SemaphoreType.DMA((4,))],
    )
    keys_scratch = [pltpu.VMEM((2, 128, 640), F32), pltpu.VMEM((768, 256), BF)]
    attn, lse, branch = kernel_call(
        attend_body,
        (shape(TOK, 1024), shape(8, 256, 1, dtype=F32), shape(TOK, D)),
        (first, seq_lengths, pad_counts, query, far, near, shared, w_out),
        [SMEM] * 3 + [VMEM] * 4 + [HBM],
        keys_scratch + [pltpu.VMEM((1024, D), BF), pltpu.SemaphoreType.DMA((1,))],
    )
    branch_other = step_to(branch, "mp", 1)
    copies = kernel_call(
        copies_body,
        shape(4, TOK, D),
        (cotangent,),
        [VMEM],
        [pltpu.SemaphoreType.DMA((4,))],
        after=(branch,),
        out_specs=(HBM,),
    )
    cot_all = swap(copies, "y")
    d_act = kernel_call(
        d_act_body,
        shape(TOK, FF),
        (cotangent, w_down),
        [VMEM, HBM],
        [pltpu.VMEM((FF, D), BF), pltpu.SemaphoreType.DMA((2,))],
        after=(copies,),
    )
    middle, hid_b = kernel_call(
        middle_body,
        (shape(TOK, D, dtype=F32), shape(TOK, D)),
        (tokens, branch, branch_other, gain_b),
        [VMEM] * 4,
        after=(d_act,),
    )
    hid_b_all = from_others(hid_b, "z")
    *d_gu, act, d_hid_b = kernel_call(
        ffn_body,
        (shape(TOK, 1408),) * 4 + (shape(4, TOK, 768), shape(TOK, D)),
        (hid_b, d_act, w_gate, w_up),
        [VMEM, HBM, HBM, HBM],
        [
            pltpu.VMEM((D, FF), BF),
            pltpu.VMEM((D, FF), BF),
            pltpu.VMEM((4, TOK, 1408), BF),
            pltpu.VMEM((4, TOK, 768), BF),
            pltpu.VMEM((TOK, FF), BF),
            pltpu.SemaphoreType.DMA((3,)),
            pltpu.SemaphoreType.DMA((3,)),
            pltpu.SemaphoreType.DMA((1,)),
            pltpu.SemaphoreType.DMA((5,)),
        ],
        out_specs=(HBM,) * 5 + (VMEM,),
    )
    d_hid_b_other = step_to(d_hid_b, "mp", 1)
    act_all = swap(act, "y")
    ffn = kernel_call(
        down_body,
        shape(TOK, D),
        (act, w_down),
        [VMEM, HBM],
        [pltpu.VMEM((FF, D), BF), pltpu.SemaphoreType.DMA((4,))],
        after=(d_hid_b, cot_all),
    )
    flag, d_gu = fence((ffn, *hid_b_all[1:]), tuple(d_gu))
    d_gu = deal(d_gu, "z")
    d_middle, d_middle_b, d_attn = kernel_call(
        back_body,
        (shape(TOK, D, dtype=F32), shape(TOK, D), shape(TOK, 1024)),
        (cotangent, d_hid_b, d_hid_b_other, middle, gain_b, w_out),
        [VMEM] * 5 + [HBM],
        [pltpu.VMEM((1024, D), BF), pltpu.SemaphoreType.DMA((1,))],
        after=(flag,),
    )
    d_query, d_far, d_near, d_own, part_a = kernel_call(
        attend_back_body,
        (
            shape(TOK, 1024),
            shape(256, 256),
            shape(256, 256),
            shape(256, 256, dtype=F32),
            shape(TOK, D),
        ),
        (
            first, seq_lengths, pad_counts, query, far, near, shared, attn, d_attn, lse,
            cos_table, sin_table, w_query,
        ),
        [SMEM] * 3 + [VMEM] * 9 + [HBM],
        keys_scratch
        + [
            pltpu.VMEM((1024, 640), BF),
            pltpu.VMEM((1024, 640), BF),
            pltpu.VMEM((1024, HD), BF),
            pltpu.VMEM((1024, HD), BF),
            pltpu.VMEM((768, 256), F32),
            pltpu.VMEM((D, 1024), BF),
            pltpu.SemaphoreType.DMA((1,)),
        ],
    )
    g_out = grad("y", pair_each, [d_middle_b], [attn], 1024, after=(part_a,))
    local = kernel_call(
        local_body,
        shape(TOK, 256),
        (d_own, shifted(d_near, -1), shifted(d_far, -2)),
        [VMEM] * 3,
        after=(fence((g_out[0], act_all, *d_gu[1:])),),
    )
    g_gu, (part_a, ffn) = grad(
        "y", pair_each, hid_b_all, d_gu, 1408, after=(local,), carry=(part_a, ffn)
    )
    part_a_other = step_to(part_a, "mp", 1)
    shared_grad = local.astype(F32) + step_to(local, "mp", 1).astype(F32) + next_kv_grad.astype(F32)
    d_keyval = jnp.concatenate(
        [turn(shared_grad[:, :HD], cos_table, -sin_table), shared_grad[:, HD:]], axis=1
    ).astype(BF)
    g_qkv = grad("z", pair_two, [hid_a], [d_query, d_keyval], 1280, after=(g_gu[0],))
    g_gu = kernel_call(
        add_body, shape(4, 256, 1408), (g_gu[0], step_to(g_gu[1], "c", 1)), [VMEM] * 2, after=(g_qkv[0],)
    )
    gu_parts = swap(g_gu, "y")
    g_down, (ffn, *g_out) = grad(
        "z", pair_stacks, [cot_all], [act_all], 768, after=(g_gu,), carry=(ffn, *g_out)
    )
    mixed = (middle + (ffn.astype(F32) + step_to(ffn, "mp", 1).astype(F32))).astype(BF)
    input_grad = kernel_call(
        last_body,
        shape(TOK, D),
        (tokens, d_middle, part_a, part_a_other, d_keyval, w_keyval, gain_a),
        [VMEM] * 7,
    )

    def side_by_side(groups, after=()):
        n = sum(group[0].shape[-1] for group in groups)
        flat = [a for group in groups for a in group]
        return kernel_call(
            functools.partial(sum_body, [len(group) for group in groups]),
            shape(TOK, n),
            flat,
            [VMEM] * len(flat),
            after=after,
        )

    sum_qkv = side_by_side([deal_out(both_cores(*g_qkv), "z")])
    in_y = side_by_side([[gu_parts], deal_out(both_cores(*g_out), "y")], after=(sum_qkv,))
    from_xz = scatter(in_y, ("xl", "z"))
    in_z = side_by_side(
        [deal_out(both_cores(*g_down), "z"), [sum_qkv]], after=(from_xz,)
    )
    from_xz = jnp.sum(from_xz.reshape(2, 4, 32, -1).astype(F32), axis=0)
    from_xy = jnp.sum(scatter(in_z, ("xl", "y")).reshape(2, 4, 32, -1).astype(F32), axis=0)
    s_gate = jnp.concatenate([from_xz[0, :, :1408], from_xz[1, :, :1408]], axis=1)
    s_up = jnp.concatenate([from_xz[2, :, :1408], from_xz[3, :, :1408]], axis=1)
    widths = [(ACT_STARTS[i + 1] - ACT_STARTS[i]) * 128 for i in range(4)]
    s_down = jnp.concatenate([from_xy[i, :, :w] for i, w in enumerate(widths)], axis=1)
    s_down = lax.optimization_barrier(s_down).T
    rest = jnp.sum(from_xy[:, :, 768:], axis=0)
    s_out = lax.optimization_barrier(jnp.sum(from_xz[:, :, 1408:], axis=0)).T
    s_query, s_keyval = rest[:, :1024], rest[:, 1024:]

    mine = place_in_seq * 32

    def rows(array):
        return lax.dynamic_slice_in_dim(array, mine, 32, 0).astype(F32)

    sum_b = jnp.sum(rows(w_gate) * s_gate, axis=1) + jnp.sum(rows(w_up) * s_up, axis=1)
    sum_a = jnp.sum(rows(w_query) * s_query, axis=1)
    sums = jnp.stack([sum_a, sum_b])
    sums = sums + step_to(sums, "mp", 1)
    sum_kv = jnp.sum(rows(w_keyval) * s_keyval, axis=1)
    s_gain_a = (sums[0] + sum_kv) / lax.dynamic_slice_in_dim(norm_attn, mine, 32, 0)
    s_gain_b = sums[1] / lax.dynamic_slice_in_dim(norm_ffn, mine, 32, 0)
    return (
        mixed,
        input_grad,
        shared,
        shared_grad,
        s_gain_a,
        s_gain_b,
        s_query,
        s_keyval,
        s_out,
        s_gate,
        s_up,
        s_down,
    )


def solution(mesh):
    fine = Mesh(mesh.devices.reshape(2, 4, 4, 2, 2), SEQ + ("mp",))
    rows = P(SEQ, None)
    placed = (
        rows,
        rows,
        rows,
        P(),
        P(),
        P(),
        P(),
        P(None, "mp"),
        P(),
        P("mp", None),
        P(None, "mp"),
        P(None, "mp"),
        P("mp", None),
    )
    return jax.shard_map(
        shards,
        mesh=fine,
        in_specs=placed,
        out_specs=(
            rows,
            rows,
            rows,
            rows,
            P(SEQ),
            P(SEQ),
            P(SEQ, "mp"),
            rows,
            P("mp", SEQ),
            P(SEQ, "mp"),
            P(SEQ, "mp"),
            P("mp", SEQ),
        ),
        check_vma=False,
    )
```

```python
import functools

import jax
import jax.numpy as jnp
from jax import lax
from jax.experimental import pallas as pl
from jax.experimental.pallas import tpu as pltpu
from jax.sharding import Mesh, PartitionSpec as P

HD = 128
WINDOW = 512
EPSILON = 1e-05
THETA = 10000.0
MASKED = -1e30
SEQ = ("xl", "y", "z", "c")
SIZES = {"xl": 2, "y": 4, "z": 4, "c": 2, "mp": 2}
BF = jnp.bfloat16
F32 = jnp.float32
TOK = 256
D = 2048
HEADS = 8
FF = 2816
SCALE = HD ** (-0.5)
LOG2E = 1.4426950408889634
VMEM = pl.BlockSpec(memory_space=pltpu.VMEM)
SMEM = pl.BlockSpec(memory_space=pltpu.SMEM)
HBM = pl.BlockSpec(memory_space=pl.ANY)
MIB = 2**20


def nn(left, right):
    return jnp.dot(left, right, preferred_element_type=F32)


def nt(left, right):
    return lax.dot_general(left, right, (((1,), (1,)), ((), ())), preferred_element_type=F32)


def tn(left, right):
    return lax.dot_general(left, right, (((0,), (0,)), ((), ())), preferred_element_type=F32)


def shape(*dims, dtype=BF):
    return jax.ShapeDtypeStruct(dims, dtype)


def kernel_call(body, outs, args, specs, scratch=(), vmem=56, after=(), carry=(), out_specs=None, flops=1000):
    single = not isinstance(outs, tuple)
    outs = (outs,) if single else outs
    if out_specs is None:
        out_specs = (VMEM,) * len(outs)
    given, extra, passed = len(args), len(after), len(carry)

    def run(*refs):
        rest = refs[given + extra + passed :]
        body(*refs[:given], *rest[: len(outs)], *rest[len(outs) + passed :])

    result = pl.pallas_call(
        run,
        out_shape=outs + tuple(shape(*c.shape, dtype=c.dtype) for c in carry),
        in_specs=list(specs) + [HBM] * (extra + passed),
        out_specs=tuple(out_specs) + (HBM,) * passed,
        scratch_shapes=list(scratch),
        input_output_aliases={given + extra + i: len(outs) + i for i in range(passed)},
        compiler_params=pltpu.CompilerParams(vmem_limit_bytes=vmem * MIB),
        cost_estimate=pl.CostEstimate(flops=flops, bytes_accessed=1000, transcendentals=0),
    )(*args, *after, *carry)
    main = result[0] if single else result[: len(outs)]
    return (main, result[len(outs) :]) if carry else main


def fetch(source, target, sems, pieces):
    copies = [
        pltpu.make_async_copy(source.at[piece], target.at[piece], sems.at[i])
        for i, piece in enumerate(pieces)
    ]
    for copy in copies:
        copy.start()
    return copies


def columns(count, width):
    return [(slice(None), pl.ds(i * width, width)) for i in range(count)]


def row_blocks(count, height):
    return [(pl.ds(i * height, height), slice(None)) for i in range(count)]


def turn(value, cos_table, sin_table):
    swapped = jnp.concatenate([value[:, HD // 2 :], value[:, : HD // 2]], axis=1)
    return value * cos_table + swapped * sin_table


def norm_kv_body(x_ref, gain_ref, w_ref, cos_ref, sin_ref, hid_ref, kv_ref):
    x = x_ref[...].astype(F32)
    inv = lax.rsqrt(jnp.mean(x * x, axis=1, keepdims=True) + EPSILON)
    hid = (x * inv * gain_ref[...]).astype(BF)
    hid_ref[...] = hid
    kv = nn(hid, w_ref[...])
    kv_ref[:, :HD] = turn(kv[:, :HD], cos_ref[...], sin_ref[...]).astype(BF)
    kv_ref[:, HD:] = kv[:, HD:].astype(BF)


def query_body(hid_ref, cos_ref, sin_ref, w_ref, q_ref, buf, sems):
    copies = fetch(w_ref, buf, sems, columns(4, 256))
    hid = hid_ref[...]
    for j in range(4):
        copies[j].wait()
        part = nn(hid, buf[:, j * 256 : j * 256 + 256])
        for h in range(2):
            q_ref[:, j * 256 + h * HD : j * 256 + h * HD + HD] = turn(
                part[:, h * HD : h * HD + HD], cos_ref[...], sin_ref[...]
            ).astype(BF)


def local_body(own_ref, near_ref, far_ref, out_ref):
    total = own_ref[...] + near_ref[...].astype(F32) + far_ref[...].astype(F32)
    out_ref[...] = total.astype(BF)


def copies_body(in_ref, out_ref, sems):
    copies = [pltpu.make_async_copy(in_ref, out_ref.at[k], sems.at[k]) for k in range(4)]
    for copy in copies:
        copy.start()
    for copy in copies:
        copy.wait()


def add_body(a_ref, b_ref, out_ref):
    for k in range(4):
        out_ref[k] = (a_ref[k].astype(F32) + b_ref[k].astype(F32)).astype(BF)


def add_out_body(axis, pairs, *refs):
    pair_refs, outs, buf, sems = refs[: 2 * pairs], refs[2 * pairs : -2], refs[-2], refs[-1]
    i = lax.axis_index(axis)
    sends = [pltpu.make_async_copy(buf.at[k], out, sems.at[k]) for k, out in enumerate(outs)]
    for k, send in enumerate(sends):
        chunk, at = (i + k) % 4, 0
        for p in range(pairs):
            total = pair_refs[2 * p][chunk].astype(F32) + pair_refs[2 * p + 1][chunk].astype(F32)
            buf[k, :, at : at + total.shape[1]] = total.astype(BF)
            at += total.shape[1]
        send.start()
    for send in sends:
        send.wait()


def key_body(a_ref, b_ref, next_ref, cos_ref, sin_ref, grad_ref, d_ref):
    total = a_ref[...].astype(F32) + b_ref[...].astype(F32) + next_ref[...].astype(F32)
    grad_ref[...] = total
    d_ref[:, :HD] = turn(total[:, :HD], cos_ref[...], -sin_ref[...]).astype(BF)
    d_ref[:, HD:] = total[:, HD:].astype(BF)


def mixed_body(mid_ref, a_ref, b_ref, out_ref):
    out_ref[...] = (mid_ref[...] + (a_ref[...].astype(F32) + b_ref[...].astype(F32))).astype(BF)


def fence_body(in_ref, out_ref):
    out_ref[...] = in_ref[...]


def sum_body(groups, *refs):
    out_ref, at = refs[-1], 0
    for count in groups:
        group, refs = refs[:count], refs[count:]
        stacked = count == 1 and len(group[0].shape) == 3
        pieces = [group[0].at[k] for k in range(4)] if stacked else group
        total = sum(p[...].astype(F32) for p in pieces)
        out_ref[:, at : at + total.shape[1]] = total.astype(BF)
        at += total.shape[1]


def fill_bias(first_ref, lengths_ref, pads_ref, bias):
    first = first_ref[0]
    count = lengths_ref.shape[0]
    starts, lives = [], []
    begin = jnp.int32(0)
    for s in range(count):
        starts.append(begin)
        lives.append(begin + lengths_ref[s] - pads_ref[s])
        begin = begin + lengths_ref[s]
    for b in range(2):
        row = lax.broadcasted_iota(jnp.int32, (128, 1), 0) + b * 128
        col = lax.broadcasted_iota(jnp.int32, (1, 640), 1) + b * 128
        query = row + first
        key = col + (first - WINDOW)
        low = jnp.zeros((128, 1), jnp.int32)
        real = jnp.zeros((1, 640), jnp.int32)
        for s in range(count):
            low = jnp.where(query >= starts[s], starts[s], low)
            real = jnp.where((key >= starts[s]) & (key < lives[s]), 1, real)
        low = jnp.maximum(low, query - (WINDOW - 1))
        here = lax.broadcasted_iota(jnp.int32, (128, 640), 1) + b * 128 + (first - WINDOW)
        when = lax.broadcasted_iota(jnp.int32, (128, 640), 0) + b * 128 + first
        seen = jnp.where(jnp.broadcast_to(real, (128, 640)) > 0, here, when + 1)
        ok = (here == when) | ((here >= low) & (seen <= when))
        bias[b] = jnp.where(ok, 0.0, MASKED)


def two_heads(ref, b, pair):
    rows = slice(b * 128, b * 128 + 128)
    return jnp.concatenate(
        [ref[rows, h * HD : h * HD + HD] for h in (2 * pair, 2 * pair + 1)], axis=0
    )


def attend_body(
    first_ref, lengths_ref, pads_ref, q_ref, far_ref, near_ref, kv_ref, w_ref,
    attn_ref, lse_ref, out_ref, bias, keys, buf, sem,
):
    copy = pltpu.make_async_copy(w_ref, buf, sem.at[0])
    copy.start()
    fill_bias(first_ref, lengths_ref, pads_ref, bias)
    keys[0:256] = far_ref[...]
    keys[256:512] = near_ref[...]
    keys[512:768] = kv_ref[...]
    for b in range(2):
        k = keys[b * 128 : b * 128 + 640, :HD]
        v = keys[b * 128 : b * 128 + 640, HD:]
        for pair in range(4):
            scores = nt(two_heads(q_ref, b, pair), k) * (SCALE * LOG2E)
            scores = scores + jnp.concatenate([bias[b], bias[b]], axis=0)
            top = jnp.max(scores, axis=1, keepdims=True)
            exps = jnp.exp2(scores - top)
            total = jnp.sum(exps, axis=1, keepdims=True)
            out = nn(exps.astype(BF), v) / total
            lse_ref[b * 4 + pair] = top + jnp.log2(total)
            for h in range(2):
                lanes = slice((2 * pair + h) * HD, (2 * pair + h) * HD + HD)
                attn_ref[b * 128 : b * 128 + 128, lanes] = out[h * 128 : h * 128 + 128].astype(BF)
    copy.wait()
    attn = attn_ref[...]
    for j in range(4):
        out_ref[:, j * 512 : j * 512 + 512] = nn(attn, buf[:, j * 512 : j * 512 + 512]).astype(BF)


def d_act_body(cot_ref, w_ref, out_ref, buf, sems):
    copies = fetch(w_ref, buf, sems, row_blocks(2, 1408))
    cot = cot_ref[...]
    for j in range(2):
        copies[j].wait()
        rows = slice(j * 1408, j * 1408 + 1408)
        out_ref[:, rows] = nt(cot, buf[rows]).astype(BF)


def middle_body(x_ref, a_ref, b_ref, gain_ref, mid_ref, hid_ref):
    mid = x_ref[...].astype(F32) + (a_ref[...].astype(F32) + b_ref[...].astype(F32))
    mid_ref[...] = mid
    inv = lax.rsqrt(jnp.mean(mid * mid, axis=1, keepdims=True) + EPSILON)
    hid = (mid * inv * gain_ref[...]).astype(BF)
    hid_ref[...] = hid


ACT_STARTS = (0, 6, 12, 17, 22)


def act_place(tile):
    part = max(i for i in range(4) if ACT_STARTS[i] <= tile)
    return part, (tile - ACT_STARTS[part]) * 128


FFN_STARTS = (0, 4, 12, 22)


def ffn_body(
    hid_ref, d_act_ref, wg_ref, wu_ref,
    d0, d1, d2, d3, act_out, out_ref,
    bufg, bufu, d_buf, act_buf, d_act_buf, semg, semu, sem_in, sem_out,
):
    pieces = [
        (slice(None), pl.ds(low * 128, (high - low) * 128))
        for low, high in zip(FFN_STARTS, FFN_STARTS[1:])
    ]
    gates = [pltpu.make_async_copy(wg_ref.at[p], bufg.at[p], semg.at[i]) for i, p in enumerate(pieces)]
    ups = [pltpu.make_async_copy(wu_ref.at[p], bufu.at[p], semu.at[i]) for i, p in enumerate(pieces)]
    d_act_in = pltpu.make_async_copy(d_act_ref, d_act_buf, sem_in.at[0])
    gates[0].start()
    ups[0].start()
    d_act_in.start()
    for g, u in zip(gates[1:], ups[1:]):
        g.start()
        u.start()
    hid = hid_ref[...]
    for j in range(3):
        low, high = FFN_STARTS[j], FFN_STARTS[j + 1]
        cols = slice(low * 128, high * 128)
        gates[j].wait()
        gate = nn(hid, bufg[:, cols])
        ups[j].wait()
        up = nn(hid, bufu[:, cols])
        if j == 0:
            d_act_in.wait()
        sigm = 1.0 / (1.0 + jnp.exp(-gate))
        silu = gate * sigm
        d_act = d_act_buf[:, cols].astype(F32)
        act = (silu * up).astype(BF)
        d_up = (d_act * silu).astype(BF)
        d_gate = (d_act * up * (sigm + silu * (1.0 - sigm))).astype(BF)
        for tile in range(low, high):
            lanes = slice((tile - low) * 128, (tile - low) * 128 + 128)
            part, at = act_place(tile)
            act_buf[part, :, at : at + 128] = act[:, lanes]
            quarter, at = tile // 11, (tile % 11) * 128
            d_buf[quarter, :, at : at + 128] = d_gate[:, lanes]
            d_buf[2 + quarter, :, at : at + 128] = d_up[:, lanes]
    for part in (2, 3):
        act_buf[part, :, 640:768] = jnp.zeros((TOK, 128), BF)
    z = lax.axis_index("z")
    sends = [pltpu.make_async_copy(act_buf, act_out, sem_out.at[4])]
    for k, d_out in enumerate((d0, d1, d2, d3)):
        sends.append(pltpu.make_async_copy(d_buf.at[(z + k) % 4], d_out, sem_out.at[k]))
    for send in sends:
        send.start()
    for i in range(2):
        rows = slice(i * 1024, i * 1024 + 1024)
        total = nt(d_buf[0], bufg[rows, :1408]) + nt(d_buf[1], bufg[rows, 1408:])
        total += nt(d_buf[2], bufu[rows, :1408]) + nt(d_buf[3], bufu[rows, 1408:])
        out_ref[:, rows] = total.astype(BF)
    for send in sends:
        send.wait()


def down_body(act_ref, w_ref, out_ref, buf, sems):
    copies = fetch(w_ref, buf, sems, columns(4, 512))
    for i in range(4):
        copies[i].wait()
        cols = slice(i * 512, i * 512 + 512)
        total = jnp.zeros((TOK, 512), F32)
        for part in range(4):
            low, high = ACT_STARTS[part] * 128, ACT_STARTS[part + 1] * 128
            total += nn(act_ref[part, :, : high - low], buf[low:high, cols])
        out_ref[:, cols] = total.astype(BF)


def back_body(
    cot_ref, a_ref, b_ref, mid_ref, gain_ref, w_ref,
    d_mid_ref, low_ref, d_attn_ref, buf, sem,
):
    copy = pltpu.make_async_copy(w_ref, buf, sem.at[0])
    copy.start()
    mid = mid_ref[...]
    inv = lax.rsqrt(jnp.mean(mid * mid, axis=1, keepdims=True) + EPSILON)
    normed = mid * inv
    e = (a_ref[...].astype(F32) + b_ref[...].astype(F32)) * gain_ref[...]
    d_mid = cot_ref[...].astype(F32) + inv * (
        e - normed * jnp.mean(e * normed, axis=1, keepdims=True)
    )
    d_mid_ref[...] = d_mid
    low = d_mid.astype(BF)
    low_ref[...] = low
    copy.wait()
    d_attn_ref[...] = nt(low, buf[...]).astype(BF)


def attend_back_body(
    first_ref, lengths_ref, pads_ref, q_ref, far_ref, near_ref, kv_ref, attn_ref, d_attn_ref, lse_ref,
    cos_ref, sin_ref, w_ref,
    dq_ref, d_far_ref, d_near_ref, d_own_ref, out_ref,
    bias, keys, stack_p, stack_d, stack_q, stack_o, total, buf, sem,
):
    copy = pltpu.make_async_copy(w_ref, buf, sem.at[0])
    copy.start()
    fill_bias(first_ref, lengths_ref, pads_ref, bias)
    keys[0:256] = far_ref[...]
    keys[256:512] = near_ref[...]
    keys[512:768] = kv_ref[...]
    total[...] = jnp.zeros_like(total)
    for b in range(2):
        window = slice(b * 128, b * 128 + 640)
        rows = slice(b * 128, b * 128 + 128)
        k = keys[window, :HD]
        v = keys[window, HD:]
        for pair in range(4):
            here = slice(pair * 256, pair * 256 + 256)
            q2 = two_heads(q_ref, b, pair)
            do2 = two_heads(d_attn_ref, b, pair)
            o2 = two_heads(attn_ref, b, pair)
            stack_q[here] = q2
            stack_o[here] = do2
            delta = jnp.sum(do2.astype(F32) * o2.astype(F32), axis=1, keepdims=True)
            scores = nt(q2, k) * (SCALE * LOG2E) + jnp.concatenate([bias[b], bias[b]], axis=0)
            prob = jnp.exp2(scores - lse_ref[b * 4 + pair])
            stack_p[here] = prob.astype(BF)
            d_score = (prob * (nt(do2, v) - delta)).astype(BF)
            stack_d[here] = d_score
            dq = nn(d_score, k) * SCALE
            for h in range(2):
                lanes = slice((2 * pair + h) * HD, (2 * pair + h) * HD + HD)
                dq_ref[rows, lanes] = turn(
                    dq[h * 128 : h * 128 + 128], cos_ref[rows], -sin_ref[rows]
                ).astype(BF)
        total[window, :HD] += tn(stack_d[...], stack_q[...]) * SCALE
        total[window, HD:] += tn(stack_p[...], stack_o[...])
    d_far_ref[...] = total[0:256].astype(BF)
    d_near_ref[...] = total[256:512].astype(BF)
    d_own_ref[...] = total[512:768]
    copy.wait()
    dq = dq_ref[...]
    for j in range(4):
        rows = slice(j * 512, j * 512 + 512)
        out_ref[:, rows] = nt(dq, buf[rows]).astype(BF)


def last_body(x_ref, d_mid_ref, a_ref, b_ref, d_kv_ref, w_ref, gain_ref, out_ref):
    x = x_ref[...].astype(F32)
    inv = lax.rsqrt(jnp.mean(x * x, axis=1, keepdims=True) + EPSILON)
    normed = x * inv
    d_hid = a_ref[...].astype(F32) + b_ref[...].astype(F32) + nt(d_kv_ref[...], w_ref[...])
    e = d_hid * gain_ref[...]
    out = d_mid_ref[...] + inv * (e - normed * jnp.mean(e * normed, axis=1, keepdims=True))
    out_ref[...] = out.astype(BF)


def pair_each(lefts, rights):
    return [list(zip(lefts, rights, strict=True))]


def pair_stacks(lefts, rights):
    return [[(lefts[0].at[k], rights[0].at[k]) for k in range(4)]]


def pair_two(lefts, rights):
    return [[(lefts[0], right)] for right in rights]


def grad_body(axis, pairing, lefts, rights, *refs):
    groups = pairing(refs[:lefts], refs[lefts : lefts + rights])
    outs, buf, sems = refs[lefts + rights : -2], refs[-2], refs[-1]
    me = lax.axis_index("c")
    for block in range(8):
        cols = slice(block * 256, block * 256 + 256)
        at = 0
        for group in groups:
            total = None
            for left, right in group:
                part = tn(left[:, cols], right[...])
                total = part if total is None else total + part
            total = total.astype(BF)
            lanes = slice(at, at + total.shape[1])
            at += total.shape[1]
            xl, y = block // 4, block % 4
            for z in range(4):
                chunk, row = (y, xl * 128 + z * 32) if axis == "y" else (z, xl * 128 + y * 32)
                for core in range(2):
                    rows = total[z * 64 + core * 32 : z * 64 + core * 32 + 32]
                    buf[(me + core) % 2, chunk, row : row + 32, lanes] = rows
    sends = [pltpu.make_async_copy(buf.at[k], out, sems.at[k]) for k, out in enumerate(outs)]
    for send in sends:
        send.start()
    for send in sends:
        send.wait()


def grad(axis, pairing, lefts, rights, n, after=(), carry=()):
    return kernel_call(
        functools.partial(grad_body, axis, pairing, len(lefts), len(rights)),
        (shape(4, 256, n),) * 2,
        (*lefts, *rights),
        [VMEM] * (len(lefts) + len(rights)),
        [pltpu.VMEM((2, 4, 256, n), BF), pltpu.SemaphoreType.DMA((2,))],
        after=after,
        carry=carry,
        out_specs=(HBM,) * 2,
    )


def step_to(value, axis, steps):
    count = SIZES[axis]
    return lax.ppermute(value, axis, [(i, (i + steps) % count) for i in range(count)])


def shifted(value, steps):
    count = 64
    first, last = max(0, -steps), min(count, count - steps)
    return lax.ppermute(value, SEQ, [(i, i + steps) for i in range(first, last)])


def pick(stack, index):
    return lax.dynamic_index_in_dim(stack, index, 0, keepdims=False)


def fence(after, carry=()):
    result = kernel_call(
        fence_body, shape(8, 128, dtype=F32), (jnp.zeros((8, 128), F32),), [VMEM], after=after, carry=carry, flops=3 * 10**10
    )
    return result if carry else (result, ())


def from_others(value, axis):
    return [value] + [step_to(value, axis, k) for k in (1, 2, 3)]


def deal(parts, axis):
    return [parts[0]] + [step_to(parts[k], axis, k) for k in (1, 2, 3)]


def add_cores(pair, after=(), carry=()):
    own, other = pair
    return kernel_call(
        add_body, shape(*own.shape), (own, step_to(other, "c", 1)), [VMEM] * 2, after=after, carry=carry
    )


def deal_out(pairs, axis, after=(), carry=()):
    rows, n = pairs[0][0].shape[1], sum(own.shape[2] for own, _ in pairs)
    parts = kernel_call(
        functools.partial(add_out_body, axis, len(pairs)),
        (shape(rows, n),) * 4,
        tuple(a for pair in pairs for a in pair),
        [VMEM] * (2 * len(pairs)),
        [pltpu.VMEM((4, rows, n), BF), pltpu.SemaphoreType.DMA((4,))],
        after=after,
        carry=carry,
        out_specs=(HBM,) * 4,
    )
    parts, held = parts if carry else (parts, ())
    return deal(parts, axis), held


def swap(parts, axis):
    return lax.all_to_all(parts, axis, 0, 0, tiled=True)


def scatter(value, axes):
    return lax.all_to_all(value, axes, 0, 0, tiled=True)


def shards(
    tokens,
    cotangent,
    next_kv_grad,
    seq_lengths,
    pad_counts,
    norm_attn,
    norm_ffn,
    w_query,
    w_keyval,
    w_out,
    w_gate,
    w_up,
    w_down,
):
    place_in_seq = lax.axis_index(SEQ)
    first = (place_in_seq * TOK).astype(jnp.int32)
    index = first + jnp.arange(TOK, dtype=jnp.int32)
    begin, start = jnp.zeros((TOK,), jnp.int32), jnp.int32(0)
    for s in range(seq_lengths.shape[0]):
        begin = jnp.where(index >= start, start, begin)
        start = start + seq_lengths[s]
    half = HD // 2
    freqs = jnp.exp(-jnp.log(THETA) * jnp.arange(half, dtype=F32) * 2.0 / HD)
    angle = (index - begin).astype(F32)[:, None] * freqs[None, :]
    cos, sin = jnp.cos(angle), jnp.sin(angle)
    cos_table = jnp.concatenate([cos, cos], axis=1)
    sin_table = jnp.concatenate([-sin, sin], axis=1)
    first = first[None]

    gain_a, gain_b = norm_attn[None], norm_ffn[None]

    hid_a, shared = kernel_call(
        norm_kv_body,
        (shape(TOK, D), shape(TOK, 256)),
        (tokens, gain_a, w_keyval, cos_table, sin_table),
        [VMEM] * 5,
    )
    near, far = shifted(shared, 1), shifted(shared, 2)
    query = kernel_call(
        query_body,
        shape(TOK, 1024),
        (hid_a, cos_table, sin_table, w_query),
        [VMEM, VMEM, VMEM, HBM],
        [pltpu.VMEM((D, 1024), BF), pltpu.SemaphoreType.DMA((4,))],
    )
    keys_scratch = [pltpu.VMEM((2, 128, 640), F32), pltpu.VMEM((768, 256), BF)]
    attn, lse, branch = kernel_call(
        attend_body,
        (shape(TOK, 1024), shape(8, 256, 1, dtype=F32), shape(TOK, D)),
        (first, seq_lengths, pad_counts, query, far, near, shared, w_out),
        [SMEM] * 3 + [VMEM] * 4 + [HBM],
        keys_scratch + [pltpu.VMEM((1024, D), BF), pltpu.SemaphoreType.DMA((1,))],
    )
    branch_other = step_to(branch, "mp", 1)
    copies = kernel_call(
        copies_body,
        shape(4, TOK, D),
        (cotangent,),
        [VMEM],
        [pltpu.SemaphoreType.DMA((4,))],
        after=(branch,),
        out_specs=(HBM,),
    )
    cot_all = swap(copies, "y")
    d_act = kernel_call(
        d_act_body,
        shape(TOK, FF),
        (cotangent, w_down),
        [VMEM, HBM],
        [pltpu.VMEM((FF, D), BF), pltpu.SemaphoreType.DMA((2,))],
        after=(copies,),
    )
    middle, hid_b = kernel_call(
        middle_body,
        (shape(TOK, D, dtype=F32), shape(TOK, D)),
        (tokens, branch, branch_other, gain_b),
        [VMEM] * 4,
        after=(d_act,),
    )
    hid_b_all = from_others(hid_b, "z")
    *d_gu, act, d_hid_b = kernel_call(
        ffn_body,
        (shape(TOK, 1408),) * 4 + (shape(4, TOK, 768), shape(TOK, D)),
        (hid_b, d_act, w_gate, w_up),
        [VMEM, HBM, HBM, HBM],
        [
            pltpu.VMEM((D, FF), BF),
            pltpu.VMEM((D, FF), BF),
            pltpu.VMEM((4, TOK, 1408), BF),
            pltpu.VMEM((4, TOK, 768), BF),
            pltpu.VMEM((TOK, FF), BF),
            pltpu.SemaphoreType.DMA((3,)),
            pltpu.SemaphoreType.DMA((3,)),
            pltpu.SemaphoreType.DMA((1,)),
            pltpu.SemaphoreType.DMA((5,)),
        ],
        out_specs=(HBM,) * 5 + (VMEM,),
    )
    d_hid_b_other = step_to(d_hid_b, "mp", 1)
    act_all = swap(act, "y")
    ffn = kernel_call(
        down_body,
        shape(TOK, D),
        (act, w_down),
        [VMEM, HBM],
        [pltpu.VMEM((FF, D), BF), pltpu.SemaphoreType.DMA((4,))],
        after=(d_hid_b, cot_all),
    )
    flag, d_gu = fence((ffn, *hid_b_all[1:]), tuple(d_gu))
    d_gu = deal(d_gu, "z")
    (d_middle, d_middle_b, d_attn), (held_ffn,) = kernel_call(
        back_body,
        (shape(TOK, D, dtype=F32), shape(TOK, D), shape(TOK, 1024)),
        (cotangent, d_hid_b, d_hid_b_other, middle, gain_b, w_out),
        [VMEM] * 5 + [HBM],
        [pltpu.VMEM((1024, D), BF), pltpu.SemaphoreType.DMA((1,))],
        after=(flag,),
        carry=(ffn,),
    )
    d_query, d_far, d_near, d_own, part_a = kernel_call(
        attend_back_body,
        (
            shape(TOK, 1024),
            shape(256, 256),
            shape(256, 256),
            shape(256, 256, dtype=F32),
            shape(TOK, D),
        ),
        (
            first, seq_lengths, pad_counts, query, far, near, shared, attn, d_attn, lse,
            cos_table, sin_table, w_query,
        ),
        [SMEM] * 3 + [VMEM] * 9 + [HBM],
        keys_scratch
        + [
            pltpu.VMEM((1024, 640), BF),
            pltpu.VMEM((1024, 640), BF),
            pltpu.VMEM((1024, HD), BF),
            pltpu.VMEM((1024, HD), BF),
            pltpu.VMEM((768, 256), F32),
            pltpu.VMEM((D, 1024), BF),
            pltpu.SemaphoreType.DMA((1,)),
        ],
    )
    def side_by_side(groups, after=(), flops=1000):
        n = sum(group[0].shape[-1] for group in groups)
        flat = [a for group in groups for a in group]
        return kernel_call(
            functools.partial(sum_body, [len(group) for group in groups]),
            shape(TOK, n),
            flat,
            [VMEM] * len(flat),
            after=after,
            flops=flops,
        )

    g_out = grad("y", pair_each, [d_middle_b], [attn], 1024, after=(part_a,))
    out_got = step_to(g_out[1], "c", 1)
    g_down = grad("z", pair_stacks, [cot_all], [act_all], 768, after=(g_out[0],))
    down_got = step_to(g_down[1], "c", 1)
    ready, _ = fence((g_down[0], *d_gu[1:]))
    local, (held_ffn,) = kernel_call(
        local_body,
        shape(TOK, 256),
        (d_own, shifted(d_near, -1), shifted(d_far, -2)),
        [VMEM] * 3,
        after=(ready,),
        carry=(held_ffn,),
    )
    ffn_other = step_to(held_ffn, "mp", 1)
    out_parts, _ = deal_out([(g_out[0], out_got)], "y", after=(local, down_got))
    g_gu = grad("y", pair_each, hid_b_all, d_gu, 1408, after=(out_parts[0],))
    gu_got = step_to(g_gu[1], "c", 1)
    shared_grad, d_keyval = kernel_call(
        key_body,
        (shape(TOK, 256, dtype=F32), shape(TOK, 256)),
        (local, step_to(local, "mp", 1), next_kv_grad, cos_table, sin_table),
        [VMEM] * 5,
        after=(g_gu[0],),
    )
    g_qkv = grad("z", pair_two, [hid_a], [d_query, d_keyval], 1280, after=(g_gu[0],))
    qkv_got = step_to(g_qkv[1], "c", 1)
    sum_out = side_by_side([out_parts], after=(g_qkv[0], ffn_other), flops=5 * 10**10)
    gu_parts, _ = deal_out([(g_gu[0], gu_got)], "y", after=(sum_out,))
    z_parts, (part_a,) = deal_out(
        [(g_down[0], down_got), (g_qkv[0], qkv_got)], "z", after=(gu_parts[0],), carry=(part_a,)
    )
    mixed = kernel_call(
        mixed_body, shape(TOK, D), (middle, held_ffn, ffn_other), [VMEM] * 3, after=(z_parts[0],)
    )
    part_a_other = step_to(part_a, "mp", 1)
    in_y = side_by_side([gu_parts, [sum_out]], after=(mixed,))
    from_xz = scatter(in_y, ("xl", "z"))
    in_z = side_by_side([z_parts], after=(in_y,), flops=10**11)
    from_xy = scatter(in_z, ("xl", "y"))
    input_grad = kernel_call(
        last_body,
        shape(TOK, D),
        (tokens, d_middle, part_a, part_a_other, d_keyval, w_keyval, gain_a),
        [VMEM] * 7,
        after=(in_z,),
    )
    from_xz = jnp.sum(from_xz.reshape(2, 4, 32, -1).astype(F32), axis=0)
    from_xy = jnp.sum(from_xy.reshape(2, 4, 32, -1).astype(F32), axis=0)
    s_gate = jnp.concatenate([from_xz[0, :, :1408], from_xz[1, :, :1408]], axis=1)
    s_up = jnp.concatenate([from_xz[2, :, :1408], from_xz[3, :, :1408]], axis=1)
    widths = [(ACT_STARTS[i + 1] - ACT_STARTS[i]) * 128 for i in range(4)]
    s_down = jnp.concatenate([from_xy[i, :, :w] for i, w in enumerate(widths)], axis=1)
    s_down = lax.optimization_barrier(s_down).T
    rest = jnp.sum(from_xy[:, :, 768:], axis=0)
    s_out = lax.optimization_barrier(jnp.sum(from_xz[:, :, 1408:], axis=0)).T
    s_query, s_keyval = rest[:, :1024], rest[:, 1024:]

    mine = place_in_seq * 32

    def rows(array):
        return lax.dynamic_slice_in_dim(array, mine, 32, 0).astype(F32)

    sum_b = jnp.sum(rows(w_gate) * s_gate, axis=1) + jnp.sum(rows(w_up) * s_up, axis=1)
    sum_a = jnp.sum(rows(w_query) * s_query, axis=1)
    sums = jnp.stack([sum_a, sum_b])
    sums = sums + step_to(sums, "mp", 1)
    sum_kv = jnp.sum(rows(w_keyval) * s_keyval, axis=1)
    s_gain_a = (sums[0] + sum_kv) / lax.dynamic_slice_in_dim(norm_attn, mine, 32, 0)
    s_gain_b = sums[1] / lax.dynamic_slice_in_dim(norm_ffn, mine, 32, 0)
    return (
        mixed,
        input_grad,
        shared,
        shared_grad,
        s_gain_a,
        s_gain_b,
        s_query,
        s_keyval,
        s_out,
        s_gate,
        s_up,
        s_down,
    )


def solution(mesh):
    fine = Mesh(mesh.devices.reshape(2, 4, 4, 2, 2), SEQ + ("mp",))
    rows = P(SEQ, None)
    placed = (
        rows,
        rows,
        rows,
        P(),
        P(),
        P(),
        P(),
        P(None, "mp"),
        P(),
        P("mp", None),
        P(None, "mp"),
        P(None, "mp"),
        P("mp", None),
    )
    return jax.shard_map(
        shards,
        mesh=fine,
        in_specs=placed,
        out_specs=(
            rows,
            rows,
            rows,
            rows,
            P(SEQ),
            P(SEQ),
            P(SEQ, "mp"),
            rows,
            P("mp", SEQ),
            P(SEQ, "mp"),
            P(SEQ, "mp"),
            P("mp", SEQ),
        ),
        check_vma=False,
    )
```

```python
import functools

import jax
import jax.numpy as jnp
from jax import lax
from jax.experimental import pallas as pl
from jax.experimental.pallas import tpu as pltpu
from jax.sharding import Mesh, PartitionSpec as P

HD = 128
WINDOW = 512
EPSILON = 1e-05
THETA = 10000.0
MASKED = -1e30
SEQ = ("xl", "y", "z", "c")
SIZES = {"xl": 2, "y": 4, "z": 4, "c": 2, "mp": 2}
BF = jnp.bfloat16
F32 = jnp.float32
TOK = 256
D = 2048
HEADS = 8
FF = 2816
SCALE = HD ** (-0.5)
LOG2E = 1.4426950408889634
VMEM = pl.BlockSpec(memory_space=pltpu.VMEM)
SMEM = pl.BlockSpec(memory_space=pltpu.SMEM)
HBM = pl.BlockSpec(memory_space=pl.ANY)
MIB = 2**20


def nn(left, right):
    return jnp.dot(left, right, preferred_element_type=F32)


def nt(left, right):
    return lax.dot_general(left, right, (((1,), (1,)), ((), ())), preferred_element_type=F32)


def tn(left, right):
    return lax.dot_general(left, right, (((0,), (0,)), ((), ())), preferred_element_type=F32)


def shape(*dims, dtype=BF):
    return jax.ShapeDtypeStruct(dims, dtype)


def kernel_call(body, outs, args, specs, scratch=(), vmem=56, after=(), carry=(), out_specs=None, flops=1000):
    single = not isinstance(outs, tuple)
    outs = (outs,) if single else outs
    if out_specs is None:
        out_specs = (VMEM,) * len(outs)
    given, extra, passed = len(args), len(after), len(carry)

    def run(*refs):
        rest = refs[given + extra + passed :]
        body(*refs[:given], *rest[: len(outs)], *rest[len(outs) + passed :])

    result = pl.pallas_call(
        run,
        out_shape=outs + tuple(shape(*c.shape, dtype=c.dtype) for c in carry),
        in_specs=list(specs) + [HBM] * (extra + passed),
        out_specs=tuple(out_specs) + (HBM,) * passed,
        scratch_shapes=list(scratch),
        input_output_aliases={given + extra + i: len(outs) + i for i in range(passed)},
        compiler_params=pltpu.CompilerParams(vmem_limit_bytes=vmem * MIB),
        cost_estimate=pl.CostEstimate(flops=flops, bytes_accessed=1000, transcendentals=0),
    )(*args, *after, *carry)
    main = result[0] if single else result[: len(outs)]
    return (main, result[len(outs) :]) if carry else main


def in_vmem(value):
    return pltpu.with_memory_space_constraint(value, pltpu.VMEM)


def fetch(source, target, sems, pieces):
    copies = [
        pltpu.make_async_copy(source.at[piece], target.at[piece], sems.at[i])
        for i, piece in enumerate(pieces)
    ]
    for copy in copies:
        copy.start()
    return copies


def columns(count, width):
    return [(slice(None), pl.ds(i * width, width)) for i in range(count)]


def row_blocks(count, height):
    return [(pl.ds(i * height, height), slice(None)) for i in range(count)]


def turn(value, cos_table, sin_table):
    swapped = jnp.concatenate([value[:, HD // 2 :], value[:, : HD // 2]], axis=1)
    return value * cos_table + swapped * sin_table


def norm_kv_body(
    first_ref, lengths_ref, x_ref, gain_ref, w_ref, freq_ref, hid_ref, kv_ref, cos_ref, sin_ref
):
    index = lax.broadcasted_iota(jnp.int32, (TOK, 1), 0) + first_ref[0]
    place, start = index, jnp.int32(0)
    for s in range(lengths_ref.shape[0]):
        place = jnp.where(index >= start, index - start, place)
        start = start + lengths_ref[s]
    angle = place.astype(F32) * freq_ref[...]
    cos_ref[...] = jnp.cos(angle)
    sin = jnp.sin(angle)
    sin_ref[...] = jnp.where(lax.broadcasted_iota(jnp.int32, (TOK, HD), 1) < HD // 2, -sin, sin)
    x = x_ref[...].astype(F32)
    inv = lax.rsqrt(jnp.mean(x * x, axis=1, keepdims=True) + EPSILON)
    hid = (x * inv * gain_ref[...]).astype(BF)
    hid_ref[...] = hid
    kv = nn(hid, w_ref[...])
    kv_ref[:, :HD] = turn(kv[:, :HD], cos_ref[...], sin_ref[...]).astype(BF)
    kv_ref[:, HD:] = kv[:, HD:].astype(BF)


def query_body(hid_ref, cos_ref, sin_ref, w_ref, q_ref, buf, sems):
    copies = fetch(w_ref, buf, sems, columns(4, 256))
    hid = hid_ref[...]
    for j in range(4):
        copies[j].wait()
        part = nn(hid, buf[:, j * 256 : j * 256 + 256])
        for h in range(2):
            q_ref[:, j * 256 + h * HD : j * 256 + h * HD + HD] = turn(
                part[:, h * HD : h * HD + HD], cos_ref[...], sin_ref[...]
            ).astype(BF)


def local_body(own_ref, near_ref, far_ref, out_ref):
    total = own_ref[...] + near_ref[...].astype(F32) + far_ref[...].astype(F32)
    out_ref[...] = total.astype(BF)


def copies_body(in_ref, out_ref, sems):
    copies = [pltpu.make_async_copy(in_ref, out_ref.at[k], sems.at[k]) for k in range(4)]
    for copy in copies:
        copy.start()
    for copy in copies:
        copy.wait()


def add_body(pairs, places, *refs):
    sources = refs[: 2 * pairs]
    outs = refs[2 * pairs : 2 * pairs + (1 if places is None else 4)]
    buf, out_sems, in_sems, *held = refs[2 * pairs + len(outs) :]
    i = 0 if places is None else lax.axis_index(places)
    loads, sends = [], []
    for k in range(4):
        chunk = k if places is None else (i + k) % 4
        loads.append(
            [
                pltpu.make_async_copy(a.at[chunk], b.at[k], in_sems.at[4 * p + k])
                for p, (a, b) in enumerate(zip(sources, held))
            ]
        )
        out = outs[0].at[k] if places is None else outs[k]
        sends.append(pltpu.make_async_copy(buf.at[k], out, out_sems.at[k]))
    for chunk_loads in loads:
        for load in chunk_loads:
            load.start()
    for k in range(4):
        for load in loads[k]:
            load.wait()
        at = 0
        for p in range(pairs):
            total = held[2 * p][k].astype(F32) + held[2 * p + 1][k].astype(F32)
            buf[k, :, at : at + total.shape[1]] = total.astype(BF)
            at += total.shape[1]
        sends[k].start()
    for send in sends:
        send.wait()


def key_body(a_ref, b_ref, next_ref, cos_ref, sin_ref, grad_ref, d_ref):
    total = a_ref[...].astype(F32) + b_ref[...].astype(F32) + next_ref[...].astype(F32)
    grad_ref[...] = total
    d_ref[:, :HD] = turn(total[:, :HD], cos_ref[...], -sin_ref[...]).astype(BF)
    d_ref[:, HD:] = total[:, HD:].astype(BF)


def mixed_body(mid_ref, a_ref, b_ref, out_ref):
    out_ref[...] = (mid_ref[...] + (a_ref[...].astype(F32) + b_ref[...].astype(F32))).astype(BF)


def fence_body(in_ref, out_ref):
    out_ref[...] = in_ref[...]


def sum_body(groups, *refs):
    out_ref, at = refs[-1], 0
    for count in groups:
        group, refs = refs[:count], refs[count:]
        stacked = count == 1 and len(group[0].shape) == 3
        pieces = [group[0].at[k] for k in range(4)] if stacked else group
        total = sum(p[...].astype(F32) for p in pieces)
        out_ref[:, at : at + total.shape[1]] = total.astype(BF)
        at += total.shape[1]


def spread_body(a_ref, b_ref, c_ref, d_ref, *refs):
    outs, buf, sems = refs[:8], refs[8], refs[9]
    total = a_ref[...].astype(F32) + b_ref[...].astype(F32)
    total = (total + c_ref[...].astype(F32) + d_ref[...].astype(F32)).astype(BF)
    for k in range(8):
        buf[k] = total[k * 32 : k * 32 + 32]
    xl, y = lax.axis_index("xl"), lax.axis_index("y")
    sends = []
    for k, out in enumerate(outs):
        place = (xl + k // 4) % 2 * 4 + (y + k % 4) % 4
        sends.append(pltpu.make_async_copy(buf.at[place], out, sems.at[k]))
    for send in sends:
        send.start()
    for send in sends:
        send.wait()


def finish_body(*refs):
    pieces, (down_ref, query_ref, key_ref, parts) = refs[:8], refs[8:]
    rest = sum(p[:, 768:].astype(F32) for p in pieces)
    query_ref[...] = rest[:, :1024]
    key_ref[...] = rest[:, 1024:]
    y = lax.axis_index("y")
    for dy in range(4):
        part = pieces[dy][:, :768].astype(F32) + pieces[4 + dy][:, :768].astype(F32)
        parts[(y + 4 - dy) % 4] = part
    for i in range(4):
        low, high = ACT_STARTS[i] * 128, ACT_STARTS[i + 1] * 128
        down_ref[:, low:high] = parts[i][:, : high - low]


def fill_bias(first_ref, lengths_ref, pads_ref, bias):
    first = first_ref[0]
    count = lengths_ref.shape[0]
    starts, lives = [], []
    begin = jnp.int32(0)
    for s in range(count):
        starts.append(begin)
        lives.append(begin + lengths_ref[s] - pads_ref[s])
        begin = begin + lengths_ref[s]
    for b in range(2):
        row = lax.broadcasted_iota(jnp.int32, (128, 1), 0) + b * 128
        col = lax.broadcasted_iota(jnp.int32, (1, 640), 1) + b * 128
        query = row + first
        key = col + (first - WINDOW)
        low = jnp.zeros((128, 1), jnp.int32)
        real = jnp.zeros((1, 640), jnp.int32)
        for s in range(count):
            low = jnp.where(query >= starts[s], starts[s], low)
            real = jnp.where((key >= starts[s]) & (key < lives[s]), 1, real)
        low = jnp.maximum(low, query - (WINDOW - 1))
        here = lax.broadcasted_iota(jnp.int32, (128, 640), 1) + b * 128 + (first - WINDOW)
        when = lax.broadcasted_iota(jnp.int32, (128, 640), 0) + b * 128 + first
        seen = jnp.where(jnp.broadcast_to(real, (128, 640)) > 0, here, when + 1)
        ok = (here == when) | ((here >= low) & (seen <= when))
        bias[b] = jnp.where(ok, 0.0, MASKED)


def two_heads(ref, b, pair):
    rows = slice(b * 128, b * 128 + 128)
    return jnp.concatenate(
        [ref[rows, h * HD : h * HD + HD] for h in (2 * pair, 2 * pair + 1)], axis=0
    )


def attend_body(
    first_ref, lengths_ref, pads_ref, q_ref, far_ref, near_ref, kv_ref, w_ref,
    attn_ref, lse_ref, out_ref, bias, keys, buf, sem,
):
    copy = pltpu.make_async_copy(w_ref, buf, sem.at[0])
    copy.start()
    fill_bias(first_ref, lengths_ref, pads_ref, bias)
    keys[0:256] = far_ref[...]
    keys[256:512] = near_ref[...]
    keys[512:768] = kv_ref[...]
    for b in range(2):
        k = keys[b * 128 : b * 128 + 640, :HD]
        v = keys[b * 128 : b * 128 + 640, HD:]
        for pair in range(4):
            scores = nt(two_heads(q_ref, b, pair), k) * (SCALE * LOG2E)
            scores = scores + jnp.concatenate([bias[b], bias[b]], axis=0)
            top = jnp.max(scores, axis=1, keepdims=True)
            exps = jnp.exp2(scores - top)
            total = jnp.sum(exps, axis=1, keepdims=True)
            out = nn(exps.astype(BF), v) / total
            lse_ref[b * 4 + pair] = top + jnp.log2(total)
            for h in range(2):
                lanes = slice((2 * pair + h) * HD, (2 * pair + h) * HD + HD)
                attn_ref[b * 128 : b * 128 + 128, lanes] = out[h * 128 : h * 128 + 128].astype(BF)
    copy.wait()
    attn = attn_ref[...]
    for j in range(4):
        out_ref[:, j * 512 : j * 512 + 512] = nn(attn, buf[:, j * 512 : j * 512 + 512]).astype(BF)


def d_act_body(cot_ref, w_ref, out_ref, buf, sems):
    copies = fetch(w_ref, buf, sems, row_blocks(2, 1408))
    cot = cot_ref[...]
    for j in range(2):
        copies[j].wait()
        rows = slice(j * 1408, j * 1408 + 1408)
        out_ref[:, rows] = nt(cot, buf[rows]).astype(BF)


def middle_body(x_ref, a_ref, b_ref, gain_ref, mid_ref, hid_ref):
    mid = x_ref[...].astype(F32) + (a_ref[...].astype(F32) + b_ref[...].astype(F32))
    mid_ref[...] = mid
    inv = lax.rsqrt(jnp.mean(mid * mid, axis=1, keepdims=True) + EPSILON)
    hid = (mid * inv * gain_ref[...]).astype(BF)
    hid_ref[...] = hid


ACT_STARTS = (0, 6, 12, 17, 22)


def act_place(tile):
    part = max(i for i in range(4) if ACT_STARTS[i] <= tile)
    return part, (tile - ACT_STARTS[part]) * 128


FFN_STARTS = (0, 4, 12, 22)


def ffn_body(
    hid_ref, d_act_ref, wg_ref, wu_ref,
    d0, d1, d2, d3, act_out, out_ref,
    bufg, bufu, d_buf, act_buf, d_act_buf, semg, semu, sem_in, sem_out,
):
    pieces = [
        (slice(None), pl.ds(low * 128, (high - low) * 128))
        for low, high in zip(FFN_STARTS, FFN_STARTS[1:])
    ]
    gates = [pltpu.make_async_copy(wg_ref.at[p], bufg.at[p], semg.at[i]) for i, p in enumerate(pieces)]
    ups = [pltpu.make_async_copy(wu_ref.at[p], bufu.at[p], semu.at[i]) for i, p in enumerate(pieces)]
    d_act_in = pltpu.make_async_copy(d_act_ref, d_act_buf, sem_in.at[0])
    gates[0].start()
    ups[0].start()
    d_act_in.start()
    for g, u in zip(gates[1:], ups[1:]):
        g.start()
        u.start()
    hid = hid_ref[...]
    for j in range(3):
        low, high = FFN_STARTS[j], FFN_STARTS[j + 1]
        cols = slice(low * 128, high * 128)
        gates[j].wait()
        gate = nn(hid, bufg[:, cols])
        ups[j].wait()
        up = nn(hid, bufu[:, cols])
        if j == 0:
            d_act_in.wait()
        sigm = 1.0 / (1.0 + jnp.exp(-gate))
        silu = gate * sigm
        d_act = d_act_buf[:, cols].astype(F32)
        act = (silu * up).astype(BF)
        d_up = (d_act * silu).astype(BF)
        d_gate = (d_act * up * (sigm + silu * (1.0 - sigm))).astype(BF)
        for tile in range(low, high):
            lanes = slice((tile - low) * 128, (tile - low) * 128 + 128)
            part, at = act_place(tile)
            act_buf[part, :, at : at + 128] = act[:, lanes]
            quarter, at = tile // 11, (tile % 11) * 128
            d_buf[quarter, :, at : at + 128] = d_gate[:, lanes]
            d_buf[2 + quarter, :, at : at + 128] = d_up[:, lanes]
    for part in (2, 3):
        act_buf[part, :, 640:768] = jnp.zeros((TOK, 128), BF)
    z = lax.axis_index("z")
    sends = [pltpu.make_async_copy(act_buf, act_out, sem_out.at[4])]
    for k, d_out in enumerate((d0, d1, d2, d3)):
        sends.append(pltpu.make_async_copy(d_buf.at[(z + k) % 4], d_out, sem_out.at[k]))
    for send in sends:
        send.start()
    for i in range(2):
        rows = slice(i * 1024, i * 1024 + 1024)
        total = nt(d_buf[0], bufg[rows, :1408]) + nt(d_buf[1], bufg[rows, 1408:])
        total += nt(d_buf[2], bufu[rows, :1408]) + nt(d_buf[3], bufu[rows, 1408:])
        out_ref[:, rows] = total.astype(BF)
    for send in sends:
        send.wait()


def down_body(act_ref, w_ref, out_ref, buf, sems):
    copies = fetch(w_ref, buf, sems, columns(4, 512))
    for i in range(4):
        copies[i].wait()
        cols = slice(i * 512, i * 512 + 512)
        total = jnp.zeros((TOK, 512), F32)
        for part in range(4):
            low, high = ACT_STARTS[part] * 128, ACT_STARTS[part + 1] * 128
            total += nn(act_ref[part, :, : high - low], buf[low:high, cols])
        out_ref[:, cols] = total.astype(BF)


def back_body(
    cot_ref, a_ref, b_ref, mid_ref, gain_ref, w_ref,
    d_mid_ref, low_ref, d_attn_ref, buf, sem,
):
    copy = pltpu.make_async_copy(w_ref, buf, sem.at[0])
    copy.start()
    mid = mid_ref[...]
    inv = lax.rsqrt(jnp.mean(mid * mid, axis=1, keepdims=True) + EPSILON)
    normed = mid * inv
    e = (a_ref[...].astype(F32) + b_ref[...].astype(F32)) * gain_ref[...]
    d_mid = cot_ref[...].astype(F32) + inv * (
        e - normed * jnp.mean(e * normed, axis=1, keepdims=True)
    )
    d_mid_ref[...] = d_mid
    low = d_mid.astype(BF)
    low_ref[...] = low
    copy.wait()
    d_attn_ref[...] = nt(low, buf[...]).astype(BF)


def attend_back_body(
    first_ref, lengths_ref, pads_ref, q_ref, far_ref, near_ref, kv_ref, attn_ref, d_attn_ref, lse_ref,
    cos_ref, sin_ref, w_ref,
    dq_ref, d_far_ref, d_near_ref, d_own_ref, out_ref,
    bias, keys, stack_p, stack_d, stack_q, stack_o, total, buf, sem,
):
    copy = pltpu.make_async_copy(w_ref, buf, sem.at[0])
    copy.start()
    fill_bias(first_ref, lengths_ref, pads_ref, bias)
    keys[0:256] = far_ref[...]
    keys[256:512] = near_ref[...]
    keys[512:768] = kv_ref[...]
    total[...] = jnp.zeros_like(total)
    for b in range(2):
        window = slice(b * 128, b * 128 + 640)
        rows = slice(b * 128, b * 128 + 128)
        k = keys[window, :HD]
        v = keys[window, HD:]
        for pair in range(4):
            here = slice(pair * 256, pair * 256 + 256)
            q2 = two_heads(q_ref, b, pair)
            do2 = two_heads(d_attn_ref, b, pair)
            o2 = two_heads(attn_ref, b, pair)
            stack_q[here] = q2
            stack_o[here] = do2
            delta = jnp.sum(do2.astype(F32) * o2.astype(F32), axis=1, keepdims=True)
            scores = nt(q2, k) * (SCALE * LOG2E) + jnp.concatenate([bias[b], bias[b]], axis=0)
            prob = jnp.exp2(scores - lse_ref[b * 4 + pair])
            stack_p[here] = prob.astype(BF)
            d_score = (prob * (nt(do2, v) - delta)).astype(BF)
            stack_d[here] = d_score
            dq = nn(d_score, k) * SCALE
            for h in range(2):
                lanes = slice((2 * pair + h) * HD, (2 * pair + h) * HD + HD)
                dq_ref[rows, lanes] = turn(
                    dq[h * 128 : h * 128 + 128], cos_ref[rows], -sin_ref[rows]
                ).astype(BF)
        total[window, :HD] += tn(stack_d[...], stack_q[...]) * SCALE
        total[window, HD:] += tn(stack_p[...], stack_o[...])
    d_far_ref[...] = total[0:256].astype(BF)
    d_near_ref[...] = total[256:512].astype(BF)
    d_own_ref[...] = total[512:768]
    copy.wait()
    dq = dq_ref[...]
    for j in range(4):
        rows = slice(j * 512, j * 512 + 512)
        out_ref[:, rows] = nt(dq, buf[rows]).astype(BF)


def last_body(x_ref, d_mid_ref, a_ref, b_ref, d_kv_ref, w_ref, gain_ref, out_ref):
    x = x_ref[...].astype(F32)
    inv = lax.rsqrt(jnp.mean(x * x, axis=1, keepdims=True) + EPSILON)
    normed = x * inv
    d_hid = a_ref[...].astype(F32) + b_ref[...].astype(F32) + nt(d_kv_ref[...], w_ref[...])
    e = d_hid * gain_ref[...]
    out = d_mid_ref[...] + inv * (e - normed * jnp.mean(e * normed, axis=1, keepdims=True))
    out_ref[...] = out.astype(BF)


def pair_each(lefts, rights):
    return [list(zip(lefts, rights, strict=True))]


def pair_stacks(lefts, rights):
    return [[(lefts[0].at[k], rights[0].at[k]) for k in range(4)]]


def pair_two(lefts, rights):
    return [[(lefts[0], right)] for right in rights]


def grad_body(axis, pairing, lefts, rights, *refs):
    sources, outs = refs[: lefts + rights], refs[lefts + rights : lefts + rights + 2]
    buf, out_sems, in_sems, *held = refs[lefts + rights + 2 :]
    loads = [pltpu.make_async_copy(a, b, in_sems.at[i]) for i, (a, b) in enumerate(zip(sources, held))]
    for load in loads:
        load.start()
    for load in loads:
        load.wait()
    groups = pairing(held[:lefts], held[lefts:])
    me = lax.axis_index("c")
    sends = []
    for step in range(8):
        xl, y = step % 2, step // 2
        block = xl * 4 + y
        cols = slice(block * 256, block * 256 + 256)
        at = 0
        for group in groups:
            total = None
            for left, right in group:
                part = tn(left[:, cols], right[...])
                total = part if total is None else total + part
            total = total.astype(BF)
            lanes = slice(at, at + total.shape[1])
            at += total.shape[1]
            for z in range(4):
                chunk, row = (y, xl * 128 + z * 32) if axis == "y" else (z, xl * 128 + y * 32)
                for core in range(2):
                    rows = total[z * 64 + core * 32 : z * 64 + core * 32 + 32]
                    buf[(me + core) % 2, chunk, row : row + 32, lanes] = rows
        if axis == "y" and xl == 1:
            sends += [
                pltpu.make_async_copy(buf.at[k, y], out.at[y], out_sems.at[4 * k + y])
                for k, out in enumerate(outs)
            ]
            for send in sends[-2:]:
                send.start()
    if axis == "z":
        sends = [pltpu.make_async_copy(buf.at[k], out, out_sems.at[k]) for k, out in enumerate(outs)]
        for send in sends:
            send.start()
    for send in sends:
        send.wait()


def grad(axis, pairing, lefts, rights, n, after=(), carry=(), flops=1000):
    args = (*lefts, *rights)
    return kernel_call(
        functools.partial(grad_body, axis, pairing, len(lefts), len(rights)),
        (shape(4, 256, n),) * 2,
        args,
        [HBM] * len(args),
        [
            pltpu.VMEM((2, 4, 256, n), BF),
            pltpu.SemaphoreType.DMA((8,)),
            pltpu.SemaphoreType.DMA((len(args),)),
            *[pltpu.VMEM(a.shape, BF) for a in args],
        ],
        flops=flops,
        after=after,
        carry=carry,
        out_specs=(HBM,) * 2,
    )


def step_to(value, axis, steps):
    count = SIZES[axis]
    return lax.ppermute(value, axis, [(i, (i + steps) % count) for i in range(count)])


def shifted(value, steps):
    count = 64
    first, last = max(0, -steps), min(count, count - steps)
    return lax.ppermute(value, SEQ, [(i, i + steps) for i in range(first, last)])


def pick(stack, index):
    return lax.dynamic_index_in_dim(stack, index, 0, keepdims=False)


def fence(after, carry=()):
    result = kernel_call(
        fence_body, shape(8, 128, dtype=F32), (jnp.zeros((8, 128), F32),), [VMEM], after=after, carry=carry, flops=3 * 10**10
    )
    return result if carry else (result, ())


def from_others(value, axis):
    return [value] + [step_to(value, axis, k) for k in (1, 2, 3)]


def deal(parts, axis):
    return [parts[0]] + [step_to(parts[k], axis, k) for k in (1, 2, 3)]


def add_cores(pairs, axis=None, after=(), carry=(), flops=1000):
    rows, n = pairs[0][0].shape[1], sum(own.shape[2] for own, _ in pairs)
    args = tuple(a for pair in pairs for a in pair)
    outs = shape(4, rows, n) if axis is None else (shape(rows, n),) * 4
    return kernel_call(
        functools.partial(add_body, len(pairs), axis),
        outs,
        args,
        [HBM] * len(args),
        [
            pltpu.VMEM((4, rows, n), BF),
            pltpu.SemaphoreType.DMA((4,)),
            pltpu.SemaphoreType.DMA((4 * len(args),)),
            *[pltpu.VMEM(a.shape, BF) for a in args],
        ],
        after=after,
        carry=carry,
        out_specs=(HBM,) if axis is None else (HBM,) * 4,
        flops=flops,
    )


def swap(parts, axis):
    return lax.all_to_all(parts, axis, 0, 0, tiled=True)


def around(value, dx, dy):
    moves = [(a * 4 + b, (a + dx) % 2 * 4 + (b + dy) % 4) for a in range(2) for b in range(4)]
    return lax.ppermute(value, ("xl", "y"), moves)


def scatter(value, axes):
    return lax.all_to_all(value, axes, 0, 0, tiled=True)


def shards(
    tokens,
    cotangent,
    next_kv_grad,
    seq_lengths,
    pad_counts,
    norm_attn,
    norm_ffn,
    w_query,
    w_keyval,
    w_out,
    w_gate,
    w_up,
    w_down,
):
    place_in_seq = lax.axis_index(SEQ)
    first = (place_in_seq * TOK).astype(jnp.int32)
    half = HD // 2
    freqs = jnp.exp(-jnp.log(THETA) * jnp.arange(half, dtype=F32) * 2.0 / HD)
    freqs = jnp.concatenate([freqs, freqs])[None]
    first = first[None]

    gain_a, gain_b = norm_attn[None], norm_ffn[None]

    hid_a, shared, cos_table, sin_table = kernel_call(
        norm_kv_body,
        (shape(TOK, D), shape(TOK, 256), shape(TOK, HD, dtype=F32), shape(TOK, HD, dtype=F32)),
        (first, seq_lengths, tokens, gain_a, w_keyval, freqs),
        [SMEM] * 2 + [VMEM] * 4,
    )
    near, far = shifted(shared, 1), shifted(shared, 2)
    query = kernel_call(
        query_body,
        shape(TOK, 1024),
        (hid_a, cos_table, sin_table, w_query),
        [VMEM, VMEM, VMEM, HBM],
        [pltpu.VMEM((D, 1024), BF), pltpu.SemaphoreType.DMA((4,))],
    )
    keys_scratch = [pltpu.VMEM((2, 128, 640), F32), pltpu.VMEM((768, 256), BF)]
    attn, lse, branch = kernel_call(
        attend_body,
        (shape(TOK, 1024), shape(8, 256, 1, dtype=F32), shape(TOK, D)),
        (first, seq_lengths, pad_counts, query, far, near, shared, w_out),
        [SMEM] * 3 + [VMEM] * 4 + [HBM],
        keys_scratch + [pltpu.VMEM((1024, D), BF), pltpu.SemaphoreType.DMA((1,))],
    )
    branch_other = step_to(branch, "mp", 1)
    copies = kernel_call(
        copies_body,
        shape(4, TOK, D),
        (cotangent,),
        [VMEM],
        [pltpu.SemaphoreType.DMA((4,))],
        after=(branch,),
        out_specs=(HBM,),
    )
    cot_all = swap(copies, "y")
    d_act = kernel_call(
        d_act_body,
        shape(TOK, FF),
        (cotangent, w_down),
        [VMEM, HBM],
        [pltpu.VMEM((FF, D), BF), pltpu.SemaphoreType.DMA((2,))],
        after=(copies,),
    )
    middle, hid_b = kernel_call(
        middle_body,
        (shape(TOK, D, dtype=F32), shape(TOK, D)),
        (tokens, branch, in_vmem(branch_other), gain_b),
        [VMEM] * 4,
        vmem=32,
        after=(d_act,),
    )
    hid_b_all = from_others(hid_b, "z")
    *d_gu, act, d_hid_b = kernel_call(
        ffn_body,
        (shape(TOK, 1408),) * 4 + (shape(4, TOK, 768), shape(TOK, D)),
        (hid_b, d_act, w_gate, w_up),
        [VMEM, HBM, HBM, HBM],
        [
            pltpu.VMEM((D, FF), BF),
            pltpu.VMEM((D, FF), BF),
            pltpu.VMEM((4, TOK, 1408), BF),
            pltpu.VMEM((4, TOK, 768), BF),
            pltpu.VMEM((TOK, FF), BF),
            pltpu.SemaphoreType.DMA((3,)),
            pltpu.SemaphoreType.DMA((3,)),
            pltpu.SemaphoreType.DMA((1,)),
            pltpu.SemaphoreType.DMA((5,)),
        ],
        out_specs=(HBM,) * 5 + (VMEM,),
        flops=3 * 10**10 + 2,
    )
    d_hid_b_other = step_to(d_hid_b, "mp", 1)
    act_all = swap(act, "y")
    ffn = kernel_call(
        down_body,
        shape(TOK, D),
        (act, w_down),
        [VMEM, HBM],
        [pltpu.VMEM((FF, D), BF), pltpu.SemaphoreType.DMA((4,))],
        after=(d_hid_b, cot_all),
    )
    flag, d_gu = fence((ffn, *hid_b_all[1:]), tuple(d_gu))
    d_gu = deal(d_gu, "z")
    (d_middle, d_middle_b, d_attn), (held_ffn,) = kernel_call(
        back_body,
        (shape(TOK, D, dtype=F32), shape(TOK, D), shape(TOK, 1024)),
        (cotangent, d_hid_b, d_hid_b_other, middle, gain_b, w_out),
        [VMEM] * 5 + [HBM],
        [pltpu.VMEM((1024, D), BF), pltpu.SemaphoreType.DMA((1,))],
        after=(flag,),
        carry=(ffn,),
    )
    d_query, d_far, d_near, d_own, part_a = kernel_call(
        attend_back_body,
        (
            shape(TOK, 1024),
            shape(256, 256),
            shape(256, 256),
            shape(256, 256, dtype=F32),
            shape(TOK, D),
        ),
        (
            first, seq_lengths, pad_counts, query, far, near, shared, attn, d_attn, lse,
            cos_table, sin_table, w_query,
        ),
        [SMEM] * 3 + [VMEM] * 9 + [HBM],
        keys_scratch
        + [
            pltpu.VMEM((1024, 640), BF),
            pltpu.VMEM((1024, 640), BF),
            pltpu.VMEM((1024, HD), BF),
            pltpu.VMEM((1024, HD), BF),
            pltpu.VMEM((768, 256), F32),
            pltpu.VMEM((D, 1024), BF),
            pltpu.SemaphoreType.DMA((1,)),
        ],
    )
    def side_by_side(groups, after=(), flops=1000):
        n = sum(group[0].shape[-1] for group in groups)
        flat = [a for group in groups for a in group]
        return kernel_call(
            functools.partial(sum_body, [len(group) for group in groups]),
            shape(TOK, n),
            flat,
            [VMEM] * len(flat),
            after=after,
            flops=flops,
        )

    g_out = grad("y", pair_each, [d_middle_b], [attn], 1024, after=(part_a,))
    out_got = step_to(g_out[1], "c", 1)
    g_down = grad("z", pair_stacks, [cot_all], [act_all], 768, after=(g_out[0],))
    down_got = step_to(g_down[1], "c", 1)
    ready, _ = fence((g_down[0], *d_gu[1:]))
    local = kernel_call(
        local_body,
        shape(TOK, 256),
        (d_own, shifted(d_near, -1), shifted(d_far, -2)),
        [VMEM] * 3,
        after=(ready,),
    )
    g_gu = grad("y", pair_each, hid_b_all, d_gu, 1408, after=(local, out_got, down_got))
    gu_got = step_to(g_gu[1], "c", 1)
    shared_grad, d_keyval = kernel_call(
        key_body,
        (shape(TOK, 256, dtype=F32), shape(TOK, 256)),
        (local, step_to(local, "mp", 1), next_kv_grad, cos_table, sin_table),
        [VMEM] * 5,
        after=(g_gu[0],),
    )
    g_qkv = grad("z", pair_two, [hid_a], [d_query, d_keyval], 1280, after=(g_gu[0],), flops=3 * 10**10 + 1)
    qkv_got = step_to(g_qkv[1], "c", 1)
    y_sums, (part_a, held_ffn) = add_cores(
        [(g_gu[0], gu_got), (g_out[0], out_got)], after=(g_qkv[0],), carry=(part_a, held_ffn)
    )
    y_parts = swap(y_sums, "y")
    part_a_other = step_to(part_a, "mp", 1)
    ffn_other = step_to(held_ffn, "mp", 1)
    z_parts = deal(
        add_cores(
            [(g_down[0], down_got), (g_qkv[0], qkv_got)], "z", after=(y_sums,), flops=10**11 + 1
        ),
        "z",
    )
    mixed = kernel_call(
        mixed_body, shape(TOK, D), (middle, held_ffn, ffn_other), [VMEM] * 3, after=(z_parts[0],)
    )
    input_grad = kernel_call(
        last_body,
        shape(TOK, D),
        (tokens, d_middle, part_a, part_a_other, d_keyval, w_keyval, gain_a),
        [VMEM] * 7,
        after=(mixed,),
    )
    in_y = side_by_side([[y_parts]], after=(input_grad,))
    from_xz = scatter(in_y, ("xl", "z"))
    z_spread = kernel_call(
        spread_body,
        (shape(32, 2048),) * 8,
        z_parts,
        [VMEM] * 4,
        [pltpu.VMEM((8, 32, 2048), BF), pltpu.SemaphoreType.DMA((8,))],
        after=(in_y,),
        out_specs=(HBM,) * 8,
        flops=10**11,
    )
    from_xy = [z_spread[0]] + [around(z_spread[k], k // 4, k % 4) for k in range(1, 8)]
    s_down, s_query, s_keyval = kernel_call(
        finish_body,
        (shape(32, FF, dtype=F32), shape(32, 1024, dtype=F32), shape(32, 256, dtype=F32)),
        from_xy,
        [VMEM] * 8,
        [pltpu.VMEM((4, 32, 768), F32)],
    )
    from_xz = jnp.sum(from_xz.reshape(2, 4, 32, -1).astype(F32), axis=0)
    s_gate = jnp.concatenate([from_xz[0, :, :1408], from_xz[1, :, :1408]], axis=1)
    s_up = jnp.concatenate([from_xz[2, :, :1408], from_xz[3, :, :1408]], axis=1)
    s_down = lax.optimization_barrier(s_down).T
    s_out = lax.optimization_barrier(jnp.sum(from_xz[:, :, 1408:], axis=0)).T

    mine = place_in_seq * 32

    def rows(array):
        return lax.dynamic_slice_in_dim(array, mine, 32, 0).astype(F32)

    sum_b = jnp.sum(rows(w_gate) * s_gate, axis=1) + jnp.sum(rows(w_up) * s_up, axis=1)
    sum_a = jnp.sum(rows(w_query) * s_query, axis=1)
    sums = jnp.stack([sum_a, sum_b])
    sums = sums + step_to(sums, "mp", 1)
    sum_kv = jnp.sum(rows(w_keyval) * s_keyval, axis=1)
    s_gain_a = (sums[0] + sum_kv) / lax.dynamic_slice_in_dim(norm_attn, mine, 32, 0)
    s_gain_b = sums[1] / lax.dynamic_slice_in_dim(norm_ffn, mine, 32, 0)
    return (
        mixed,
        input_grad,
        shared,
        shared_grad,
        s_gain_a,
        s_gain_b,
        s_query,
        s_keyval,
        s_out,
        s_gate,
        s_up,
        s_down,
    )


def solution(mesh):
    fine = Mesh(mesh.devices.reshape(2, 4, 4, 2, 2), SEQ + ("mp",))
    rows = P(SEQ, None)
    placed = (
        rows,
        rows,
        rows,
        P(),
        P(),
        P(),
        P(),
        P(None, "mp"),
        P(),
        P("mp", None),
        P(None, "mp"),
        P(None, "mp"),
        P("mp", None),
    )
    return jax.shard_map(
        shards,
        mesh=fine,
        in_specs=placed,
        out_specs=(
            rows,
            rows,
            rows,
            rows,
            P(SEQ),
            P(SEQ),
            P(SEQ, "mp"),
            rows,
            P("mp", SEQ),
            P(SEQ, "mp"),
            P(SEQ, "mp"),
            P("mp", SEQ),
        ),
        check_vma=False,
    )
```

```python
import functools

import jax
import jax.numpy as jnp
from jax import lax
from jax.experimental import pallas as pl
from jax.experimental.pallas import tpu as pltpu
from jax.sharding import Mesh, PartitionSpec as P

HD = 128
WINDOW = 512
EPSILON = 1e-05
THETA = 10000.0
MASKED = -1e30
SEQ = ("xl", "y", "z", "c")
SIZES = {"xl": 2, "y": 4, "z": 4, "c": 2, "mp": 2}
BF = jnp.bfloat16
F32 = jnp.float32
TOK = 256
D = 2048
HEADS = 8
FF = 2816
SCALE = HD ** (-0.5)
LOG2E = 1.4426950408889634
VMEM = pl.BlockSpec(memory_space=pltpu.VMEM)
SMEM = pl.BlockSpec(memory_space=pltpu.SMEM)
HBM = pl.BlockSpec(memory_space=pl.ANY)
MIB = 2**20


def nn(left, right):
    return jnp.dot(left, right, preferred_element_type=F32)


def nt(left, right):
    return lax.dot_general(left, right, (((1,), (1,)), ((), ())), preferred_element_type=F32)


def tn(left, right):
    return lax.dot_general(left, right, (((0,), (0,)), ((), ())), preferred_element_type=F32)


def shape(*dims, dtype=BF):
    return jax.ShapeDtypeStruct(dims, dtype)


def kernel_call(body, outs, args, specs, scratch=(), vmem=56, after=(), carry=(), out_specs=None, flops=1000):
    single = not isinstance(outs, tuple)
    outs = (outs,) if single else outs
    if out_specs is None:
        out_specs = (VMEM,) * len(outs)
    given, extra, passed = len(args), len(after), len(carry)

    def run(*refs):
        rest = refs[given + extra + passed :]
        body(*refs[:given], *rest[: len(outs)], *rest[len(outs) + passed :])

    result = pl.pallas_call(
        run,
        out_shape=outs + tuple(shape(*c.shape, dtype=c.dtype) for c in carry),
        in_specs=list(specs) + [HBM] * (extra + passed),
        out_specs=tuple(out_specs) + (HBM,) * passed,
        scratch_shapes=list(scratch),
        input_output_aliases={given + extra + i: len(outs) + i for i in range(passed)},
        compiler_params=pltpu.CompilerParams(vmem_limit_bytes=vmem * MIB),
        cost_estimate=pl.CostEstimate(flops=flops, bytes_accessed=1000, transcendentals=0),
    )(*args, *map(in_hbm, after), *map(in_hbm, carry))
    main = result[0] if single else result[: len(outs)]
    return (main, result[len(outs) :]) if carry else main


def in_vmem(value):
    return pltpu.with_memory_space_constraint(value, pltpu.VMEM)


def in_hbm(value):
    return pltpu.with_memory_space_constraint(value, pltpu.HBM)


def fetch(source, target, sems, pieces):
    copies = [
        pltpu.make_async_copy(source.at[piece], target.at[piece], sems.at[i])
        for i, piece in enumerate(pieces)
    ]
    for copy in copies:
        copy.start()
    return copies


def columns(count, width):
    return [(slice(None), pl.ds(i * width, width)) for i in range(count)]


def row_blocks(count, height):
    return [(pl.ds(i * height, height), slice(None)) for i in range(count)]


def turn(value, cos_table, sin_table):
    swapped = jnp.concatenate([value[:, HD // 2 :], value[:, : HD // 2]], axis=1)
    return value * cos_table + swapped * sin_table


def norm_kv_body(
    first_ref, lengths_ref, x_ref, gain_ref, w_ref, freq_ref, hid_ref, kv_ref, cos_ref, sin_ref
):
    index = lax.broadcasted_iota(jnp.int32, (TOK, 1), 0) + first_ref[0]
    place, start = index, jnp.int32(0)
    for s in range(lengths_ref.shape[0]):
        place = jnp.where(index >= start, index - start, place)
        start = start + lengths_ref[s]
    angle = place.astype(F32) * freq_ref[...]
    cos_ref[...] = jnp.cos(angle)
    sin = jnp.sin(angle)
    sin_ref[...] = jnp.where(lax.broadcasted_iota(jnp.int32, (TOK, HD), 1) < HD // 2, -sin, sin)
    x = x_ref[...].astype(F32)
    inv = lax.rsqrt(jnp.mean(x * x, axis=1, keepdims=True) + EPSILON)
    hid = (x * inv * gain_ref[...]).astype(BF)
    hid_ref[...] = hid
    kv = nn(hid, w_ref[...])
    kv_ref[:, :HD] = turn(kv[:, :HD], cos_ref[...], sin_ref[...]).astype(BF)
    kv_ref[:, HD:] = kv[:, HD:].astype(BF)


def query_body(hid_ref, cos_ref, sin_ref, w_ref, q_ref, buf, sems):
    copies = fetch(w_ref, buf, sems, columns(4, 256))
    hid = hid_ref[...]
    for j in range(4):
        copies[j].wait()
        part = nn(hid, buf[:, j * 256 : j * 256 + 256])
        for h in range(2):
            q_ref[:, j * 256 + h * HD : j * 256 + h * HD + HD] = turn(
                part[:, h * HD : h * HD + HD], cos_ref[...], sin_ref[...]
            ).astype(BF)


def local_body(own_ref, near_ref, far_ref, out_ref):
    total = own_ref[...] + near_ref[...].astype(F32) + far_ref[...].astype(F32)
    out_ref[...] = total.astype(BF)


def copies_body(in_ref, out_ref, sems):
    copies = [pltpu.make_async_copy(in_ref, out_ref.at[k], sems.at[k]) for k in range(4)]
    for copy in copies:
        copy.start()
    for copy in copies:
        copy.wait()


def add_body(pairs, places, *refs):
    sources = refs[: 2 * pairs]
    outs = refs[2 * pairs : 2 * pairs + (1 if places is None else 4)]
    buf, out_sems, in_sems, *held = refs[2 * pairs + len(outs) :]
    i = 0 if places is None else lax.axis_index(places)
    loads, sends = [], []
    for k in range(4):
        chunk = k if places is None else (i + k) % 4
        loads.append(
            [
                pltpu.make_async_copy(a.at[chunk], b.at[k], in_sems.at[4 * p + k])
                for p, (a, b) in enumerate(zip(sources, held))
            ]
        )
        out = outs[0].at[k] if places is None else outs[k]
        sends.append(pltpu.make_async_copy(buf.at[k], out, out_sems.at[k]))
    for chunk_loads in loads:
        for load in chunk_loads:
            load.start()
    for k in range(4):
        for load in loads[k]:
            load.wait()
        at = 0
        for p in range(pairs):
            total = held[2 * p][k].astype(F32) + held[2 * p + 1][k].astype(F32)
            buf[k, :, at : at + total.shape[1]] = total.astype(BF)
            at += total.shape[1]
        sends[k].start()
    for send in sends:
        send.wait()


def key_body(a_ref, b_ref, next_ref, cos_ref, sin_ref, grad_ref, d_ref, half_ref):
    total = a_ref[...].astype(F32) + b_ref[...].astype(F32) + next_ref[...].astype(F32)
    grad_ref[...] = total
    d_key = turn(total[:, :HD], cos_ref[...], -sin_ref[...]).astype(BF)
    d_value = total[:, HD:].astype(BF)
    d_ref[:, :HD] = d_key
    d_ref[:, HD:] = d_value
    first = lax.axis_index("mp") == 0
    half_ref[...] = jnp.where(first, d_key.astype(F32), d_value.astype(F32)).astype(BF)


def mixed_body(mid_ref, a_ref, b_ref, out_ref):
    out_ref[...] = (mid_ref[...] + (a_ref[...].astype(F32) + b_ref[...].astype(F32))).astype(BF)


def fence_body(out_ref):
    pass


def sum_body(groups, *refs):
    out_ref, at = refs[-1], 0
    for count in groups:
        group, refs = refs[:count], refs[count:]
        stacked = count == 1 and len(group[0].shape) == 3
        pieces = [group[0].at[k] for k in range(4)] if stacked else group
        total = sum(p[...].astype(F32) for p in pieces)
        out_ref[:, at : at + total.shape[1]] = total.astype(BF)
        at += total.shape[1]


def spread_body(a_ref, b_ref, c_ref, d_ref, *refs):
    outs, buf, sems = refs[:8], refs[8], refs[9]
    total = a_ref[...].astype(F32) + b_ref[...].astype(F32)
    total = (total + c_ref[...].astype(F32) + d_ref[...].astype(F32)).astype(BF)
    for k in range(8):
        buf[k] = total[k * 32 : k * 32 + 32]
    xl, y = lax.axis_index("xl"), lax.axis_index("y")
    sends = []
    for k, out in enumerate(outs):
        place = (xl + k // 4) % 2 * 4 + (y + k % 4) % 4
        sends.append(pltpu.make_async_copy(buf.at[place], out, sems.at[k]))
    for send in sends:
        send.start()
    for send in sends:
        send.wait()


def my_rows(copies, arrays, bufs, sems):
    place = 0
    for axis in SEQ:
        place = place * SIZES[axis] + lax.axis_index(axis)
    rows = pl.ds(pl.multiple_of(place * 32, 32), 32)
    for i, (array, buf) in enumerate(zip(arrays, bufs)):
        copies.append(pltpu.make_async_copy(array.at[rows], buf, sems.at[i]))
        copies[-1].start()
    return copies


def row_sums(weights, grads):
    return jnp.sum(weights[...].astype(F32) * grads, axis=1, keepdims=True)


def finish_y_body(got_ref, wg_ref, wu_ref, gate_ref, up_ref, out_ref, sum_ref, wg, wu, sems):
    copies = my_rows([], (wg_ref, wu_ref), (wg, wu), sems)
    both = got_ref[0:128].astype(F32) + got_ref[128:256].astype(F32)
    part = [both[z * 32 : z * 32 + 32] for z in range(4)]
    out_ref[...] = part[0][:, 1408:] + part[1][:, 1408:] + part[2][:, 1408:] + part[3][:, 1408:]
    for copy in copies:
        copy.wait()
    total = jnp.zeros((32, 1), F32)
    for ref, weights, z in ((gate_ref, wg, 0), (up_ref, wu, 2)):
        for half in range(2):
            grads = part[z + half][:, :1408]
            lanes = slice(half * 1408, half * 1408 + 1408)
            ref[:, lanes] = grads
            total += row_sums(weights[:, lanes], grads)
    sum_ref[...] = jnp.broadcast_to(total, (32, 128))


def finish_body(*refs):
    pieces, (sum_b_ref, wq_ref, wk_ref, down_ref, query_ref, sum_ref, parts, wq, wk, sems) = (
        refs[:8],
        refs[8:],
    )
    copies = my_rows([], (wq_ref, wk_ref), (wq, wk), sems)
    rest = sum(p[:, 768:].astype(F32) for p in pieces)
    query_ref[...] = rest[:, :1024]
    y = lax.axis_index("y")
    for dy in range(4):
        part = pieces[dy][:, :768].astype(F32) + pieces[4 + dy][:, :768].astype(F32)
        parts[(y + 4 - dy) % 4] = part
    for i in range(4):
        low, high = ACT_STARTS[i] * 128, ACT_STARTS[i + 1] * 128
        down_ref[:, low:high] = parts[i][:, : high - low]
    for copy in copies:
        copy.wait()
    lane = lax.broadcasted_iota(jnp.int32, (32, 128), 1)
    keys = rest[:, 1024:]
    key_weights = wk[:, pl.ds(pl.multiple_of(lax.axis_index("mp") * HD, HD), HD)]
    sum_a = row_sums(wq, rest[:, :1024]) + row_sums(key_weights, keys)
    sum_ref[:, :128] = jnp.where(lane == 1, sum_b_ref[...], sum_a)
    sum_ref[:, 128:] = keys


def fill_bias(first_ref, lengths_ref, pads_ref, bias):
    first = first_ref[0]
    count = lengths_ref.shape[0]
    starts, lives = [], []
    begin = jnp.int32(0)
    for s in range(count):
        starts.append(begin)
        lives.append(begin + lengths_ref[s] - pads_ref[s])
        begin = begin + lengths_ref[s]
    for b in range(2):
        row = lax.broadcasted_iota(jnp.int32, (128, 1), 0) + b * 128
        col = lax.broadcasted_iota(jnp.int32, (1, 640), 1) + b * 128
        query = row + first
        key = col + (first - WINDOW)
        low = jnp.zeros((128, 1), jnp.int32)
        real = jnp.zeros((1, 640), jnp.int32)
        for s in range(count):
            low = jnp.where(query >= starts[s], starts[s], low)
            real = jnp.where((key >= starts[s]) & (key < lives[s]), 1, real)
        low = jnp.maximum(low, query - (WINDOW - 1))
        here = lax.broadcasted_iota(jnp.int32, (128, 640), 1) + b * 128 + (first - WINDOW)
        when = lax.broadcasted_iota(jnp.int32, (128, 640), 0) + b * 128 + first
        seen = jnp.where(jnp.broadcast_to(real, (128, 640)) > 0, here, when + 1)
        ok = (here == when) | ((here >= low) & (seen <= when))
        bias[b] = jnp.where(ok, 0.0, MASKED)


def two_heads(ref, b, pair):
    rows = slice(b * 128, b * 128 + 128)
    return jnp.concatenate(
        [ref[rows, h * HD : h * HD + HD] for h in (2 * pair, 2 * pair + 1)], axis=0
    )


def attend_body(
    first_ref, lengths_ref, pads_ref, q_ref, far_ref, near_ref, kv_ref, w_ref,
    attn_ref, lse_ref, out_ref, bias, keys, buf, sem,
):
    copy = pltpu.make_async_copy(w_ref, buf, sem.at[0])
    copy.start()
    fill_bias(first_ref, lengths_ref, pads_ref, bias)
    keys[0:256] = far_ref[...]
    keys[256:512] = near_ref[...]
    keys[512:768] = kv_ref[...]
    for b in range(2):
        k = keys[b * 128 : b * 128 + 640, :HD]
        v = keys[b * 128 : b * 128 + 640, HD:]
        for pair in range(4):
            scores = nt(two_heads(q_ref, b, pair), k) * (SCALE * LOG2E)
            scores = scores + jnp.concatenate([bias[b], bias[b]], axis=0)
            top = jnp.max(scores, axis=1, keepdims=True)
            exps = jnp.exp2(scores - top)
            total = jnp.sum(exps, axis=1, keepdims=True)
            out = nn(exps.astype(BF), v) / total
            lse_ref[b * 4 + pair] = top + jnp.log2(total)
            for h in range(2):
                lanes = slice((2 * pair + h) * HD, (2 * pair + h) * HD + HD)
                attn_ref[b * 128 : b * 128 + 128, lanes] = out[h * 128 : h * 128 + 128].astype(BF)
    copy.wait()
    attn = attn_ref[...]
    for j in range(4):
        out_ref[:, j * 512 : j * 512 + 512] = nn(attn, buf[:, j * 512 : j * 512 + 512]).astype(BF)


def d_act_body(cot_ref, w_ref, out_ref, flag_ref, buf, sems):
    copies = fetch(w_ref, buf, sems, row_blocks(2, 1408))
    cot = cot_ref[...]
    for j in range(2):
        copies[j].wait()
        rows = slice(j * 1408, j * 1408 + 1408)
        out_ref[:, rows] = nt(cot, buf[rows]).astype(BF)
    flag_ref[...] = cot[0:16, 0:128]


def middle_body(x_ref, a_ref, b_ref, gain_ref, mid_ref, hid_ref):
    mid = x_ref[...].astype(F32) + (a_ref[...].astype(F32) + b_ref[...].astype(F32))
    mid_ref[...] = mid
    inv = lax.rsqrt(jnp.mean(mid * mid, axis=1, keepdims=True) + EPSILON)
    hid = (mid * inv * gain_ref[...]).astype(BF)
    hid_ref[...] = hid


ACT_STARTS = (0, 6, 12, 17, 22)


def act_place(tile):
    part = max(i for i in range(4) if ACT_STARTS[i] <= tile)
    return part, (tile - ACT_STARTS[part]) * 128


FFN_STARTS = (0, 4, 12, 22)


def ffn_body(
    hid_ref, d_act_ref, wg_ref, wu_ref,
    d0, d1, d2, d3, act_out, out_ref,
    bufg, bufu, d_buf, act_buf, d_act_buf, semg, semu, sem_in, sem_out,
):
    pieces = [
        (slice(None), pl.ds(low * 128, (high - low) * 128))
        for low, high in zip(FFN_STARTS, FFN_STARTS[1:])
    ]
    gates = [pltpu.make_async_copy(wg_ref.at[p], bufg.at[p], semg.at[i]) for i, p in enumerate(pieces)]
    ups = [pltpu.make_async_copy(wu_ref.at[p], bufu.at[p], semu.at[i]) for i, p in enumerate(pieces)]
    d_act_in = pltpu.make_async_copy(d_act_ref, d_act_buf, sem_in.at[0])
    gates[0].start()
    ups[0].start()
    d_act_in.start()
    for g, u in zip(gates[1:], ups[1:]):
        g.start()
        u.start()
    hid = hid_ref[...]
    for j in range(3):
        low, high = FFN_STARTS[j], FFN_STARTS[j + 1]
        cols = slice(low * 128, high * 128)
        gates[j].wait()
        gate = nn(hid, bufg[:, cols])
        ups[j].wait()
        up = nn(hid, bufu[:, cols])
        if j == 0:
            d_act_in.wait()
        sigm = 1.0 / (1.0 + jnp.exp(-gate))
        silu = gate * sigm
        d_act = d_act_buf[:, cols].astype(F32)
        act = (silu * up).astype(BF)
        d_up = (d_act * silu).astype(BF)
        d_gate = (d_act * up * (sigm + silu * (1.0 - sigm))).astype(BF)
        for tile in range(low, high):
            lanes = slice((tile - low) * 128, (tile - low) * 128 + 128)
            part, at = act_place(tile)
            act_buf[part, :, at : at + 128] = act[:, lanes]
            quarter, at = tile // 11, (tile % 11) * 128
            d_buf[quarter, :, at : at + 128] = d_gate[:, lanes]
            d_buf[2 + quarter, :, at : at + 128] = d_up[:, lanes]
    for part in (2, 3):
        act_buf[part, :, 640:768] = jnp.zeros((TOK, 128), BF)
    z = lax.axis_index("z")
    sends = [pltpu.make_async_copy(act_buf, act_out, sem_out.at[4])]
    for k, d_out in enumerate((d0, d1, d2, d3)):
        sends.append(pltpu.make_async_copy(d_buf.at[(z + k) % 4], d_out, sem_out.at[k]))
    for send in sends:
        send.start()
    for i in range(2):
        rows = slice(i * 1024, i * 1024 + 1024)
        total = nt(d_buf[0], bufg[rows, :1408]) + nt(d_buf[1], bufg[rows, 1408:])
        total += nt(d_buf[2], bufu[rows, :1408]) + nt(d_buf[3], bufu[rows, 1408:])
        out_ref[:, rows] = total.astype(BF)
    for send in sends:
        send.wait()


def down_body(act_ref, w_ref, out_ref, buf, sems):
    copies = fetch(w_ref, buf, sems, columns(4, 512))
    for i in range(4):
        copies[i].wait()
        cols = slice(i * 512, i * 512 + 512)
        total = jnp.zeros((TOK, 512), F32)
        for part in range(4):
            low, high = ACT_STARTS[part] * 128, ACT_STARTS[part + 1] * 128
            total += nn(act_ref[part, :, : high - low], buf[low:high, cols])
        out_ref[:, cols] = total.astype(BF)


def back_body(
    cot_ref, a_ref, b_ref, mid_ref, gain_ref, w_ref,
    d_mid_ref, low_ref, d_attn_ref, buf, d_mid_buf, low_buf, sem,
):
    copy = pltpu.make_async_copy(w_ref, buf, sem.at[0])
    copy.start()
    mid = mid_ref[...]
    inv = lax.rsqrt(jnp.mean(mid * mid, axis=1, keepdims=True) + EPSILON)
    normed = mid * inv
    e = (a_ref[...].astype(F32) + b_ref[...].astype(F32)) * gain_ref[...]
    d_mid = cot_ref[...].astype(F32) + inv * (
        e - normed * jnp.mean(e * normed, axis=1, keepdims=True)
    )
    d_mid_buf[...] = d_mid
    low = d_mid.astype(BF)
    low_buf[...] = low
    sends = [
        pltpu.make_async_copy(d_mid_buf, d_mid_ref, sem.at[1]),
        pltpu.make_async_copy(low_buf, low_ref, sem.at[2]),
    ]
    for send in sends:
        send.start()
    copy.wait()
    d_attn_ref[...] = nt(low, buf[...]).astype(BF)
    for send in sends:
        send.wait()


def attend_back_body(
    first_ref, lengths_ref, pads_ref, q_ref, far_ref, near_ref, kv_ref, attn_ref, d_attn_ref, lse_ref,
    cos_ref, sin_ref, w_ref,
    dq_ref, d_far_ref, d_near_ref, d_own_ref, out_ref,
    bias, keys, stack_p, stack_d, stack_q, stack_o, total, buf, sem,
):
    copy = pltpu.make_async_copy(w_ref, buf, sem.at[0])
    copy.start()
    fill_bias(first_ref, lengths_ref, pads_ref, bias)
    keys[0:256] = far_ref[...]
    keys[256:512] = near_ref[...]
    keys[512:768] = kv_ref[...]
    total[...] = jnp.zeros_like(total)
    for b in range(2):
        window = slice(b * 128, b * 128 + 640)
        rows = slice(b * 128, b * 128 + 128)
        k = keys[window, :HD]
        v = keys[window, HD:]
        for pair in range(4):
            here = slice(pair * 256, pair * 256 + 256)
            q2 = two_heads(q_ref, b, pair)
            do2 = two_heads(d_attn_ref, b, pair)
            o2 = two_heads(attn_ref, b, pair)
            stack_q[here] = q2
            stack_o[here] = do2
            delta = jnp.sum(do2.astype(F32) * o2.astype(F32), axis=1, keepdims=True)
            scores = nt(q2, k) * (SCALE * LOG2E) + jnp.concatenate([bias[b], bias[b]], axis=0)
            prob = jnp.exp2(scores - lse_ref[b * 4 + pair])
            stack_p[here] = prob.astype(BF)
            d_score = (prob * (nt(do2, v) - delta)).astype(BF)
            stack_d[here] = d_score
            dq = nn(d_score, k) * SCALE
            for h in range(2):
                lanes = slice((2 * pair + h) * HD, (2 * pair + h) * HD + HD)
                dq_ref[rows, lanes] = turn(
                    dq[h * 128 : h * 128 + 128], cos_ref[rows], -sin_ref[rows]
                ).astype(BF)
        total[window, :HD] += tn(stack_d[...], stack_q[...]) * SCALE
        total[window, HD:] += tn(stack_p[...], stack_o[...])
    d_far_ref[...] = total[0:256].astype(BF)
    d_near_ref[...] = total[256:512].astype(BF)
    d_own_ref[...] = total[512:768]
    copy.wait()
    dq = dq_ref[...]
    for j in range(4):
        rows = slice(j * 512, j * 512 + 512)
        out_ref[:, rows] = nt(dq, buf[rows]).astype(BF)


def last_body(x_ref, d_mid_ref, a_ref, b_ref, d_kv_ref, w_ref, gain_ref, out_ref):
    x = x_ref[...].astype(F32)
    inv = lax.rsqrt(jnp.mean(x * x, axis=1, keepdims=True) + EPSILON)
    normed = x * inv
    d_hid = a_ref[...].astype(F32) + b_ref[...].astype(F32) + nt(d_kv_ref[...], w_ref[...])
    e = d_hid * gain_ref[...]
    out = d_mid_ref[...] + inv * (e - normed * jnp.mean(e * normed, axis=1, keepdims=True))
    out_ref[...] = out.astype(BF)


def pair_each(lefts, rights):
    return [list(zip(lefts, rights, strict=True))]


def pair_stacks(lefts, rights):
    return [[(lefts[0].at[k], rights[0].at[k]) for k in range(4)]]


def pair_two(lefts, rights):
    return [[(lefts[0], right)] for right in rights]


def grad_body(axis, pairing, lefts, rights, *refs):
    sources, outs = refs[: lefts + rights], refs[lefts + rights : lefts + rights + 2]
    buf, out_sems, in_sems, *held = refs[lefts + rights + 2 :]
    stacked = len(sources[0].shape) == 3
    pieces = [(a, b) for a, b in zip(sources, held)]
    if stacked:
        pieces = [(a.at[k], b.at[k]) for a, b in pieces for k in range(4)]
    count = 4 if stacked else lefts
    loads = [pltpu.make_async_copy(a, b, in_sems.at[i]) for i, (a, b) in enumerate(pieces)]
    for i in range(max(count, len(loads) - count)):
        for load in loads[:count][i : i + 1] + loads[count:][i : i + 1]:
            load.start()
    groups = pairing(held[:lefts], held[lefts:])
    if count == 1:
        for load in loads:
            load.wait()
    me = lax.axis_index("c")
    sends = []
    for step in range(8):
        xl, y = step % 2, step // 2
        block = xl * 4 + y
        cols = slice(block * 256, block * 256 + 256)
        at = 0
        for group in groups:
            total = None
            for i, (left, right) in enumerate(group):
                if step == 0 and count > 1:
                    loads[i].wait()
                    loads[count + i].wait()
                part = tn(left[:, cols], right[...])
                total = part if total is None else total + part
            total = total.astype(BF)
            lanes = slice(at, at + total.shape[1])
            at += total.shape[1]
            for z in range(4):
                chunk, row = (y, xl * 128 + z * 32) if axis == "y" else (z, xl * 128 + y * 32)
                for core in range(2):
                    rows = total[z * 64 + core * 32 : z * 64 + core * 32 + 32]
                    buf[(me + core) % 2, chunk, row : row + 32, lanes] = rows
        if axis == "y" and xl == 1:
            sends += [
                pltpu.make_async_copy(buf.at[k, y], out.at[y], out_sems.at[4 * k + y])
                for k, out in enumerate(outs)
            ]
            for send in sends[-2:]:
                send.start()
        if axis == "z":
            rows = pl.ds(xl * 128 + y * 32, 32)
            sends += [
                pltpu.make_async_copy(buf.at[k, :, rows], out.at[:, rows], out_sems.at[8 * k + step])
                for k, out in enumerate(outs)
            ]
            for send in sends[-2:]:
                send.start()
    for send in sends:
        send.wait()


def grad(axis, pairing, lefts, rights, n, after=(), carry=(), flops=1000):
    args = tuple(map(in_hbm, (*lefts, *rights)))
    return kernel_call(
        functools.partial(grad_body, axis, pairing, len(lefts), len(rights)),
        (shape(4, 256, n),) * 2,
        args,
        [HBM] * len(args),
        [
            pltpu.VMEM((2, 4, 256, n), BF),
            pltpu.SemaphoreType.DMA((16,)),
            pltpu.SemaphoreType.DMA((8 if args[0].ndim == 3 else len(args),)),
            *[pltpu.VMEM(a.shape, BF) for a in args],
        ],
        flops=flops,
        after=after,
        carry=carry,
        out_specs=(HBM,) * 2,
    )


def step_to(value, axis, steps):
    count = SIZES[axis]
    return lax.ppermute(value, axis, [(i, (i + steps) % count) for i in range(count)])


def shifted(value, steps):
    count = 64
    first, last = max(0, -steps), min(count, count - steps)
    return lax.ppermute(value, SEQ, [(i, i + steps) for i in range(first, last)])


def pick(stack, index):
    return lax.dynamic_index_in_dim(stack, index, 0, keepdims=False)


def fence(after, carry=()):
    result = kernel_call(
        fence_body, shape(8, 128, dtype=F32), (), [], after=after, carry=carry, flops=3 * 10**10, out_specs=(HBM,)
    )
    return result if carry else (result, ())


def from_others(value, axis):
    return [value] + [step_to(value, axis, k) for k in (1, 2, 3)]


def deal(parts, axis):
    return [parts[0]] + [step_to(parts[k], axis, k) for k in (1, 2, 3)]


def add_cores(pairs, axis=None, after=(), carry=(), flops=1000, near=False):
    rows, n = pairs[0][0].shape[1], sum(own.shape[2] for own, _ in pairs)
    args = tuple(a for pair in pairs for a in (in_hbm(pair[0]), (in_vmem if near else in_hbm)(pair[1])))
    outs = shape(4, rows, n) if axis is None else (shape(rows, n),) * 4
    return kernel_call(
        functools.partial(add_body, len(pairs), axis),
        outs,
        args,
        [HBM] * len(args),
        [
            pltpu.VMEM((4, rows, n), BF),
            pltpu.SemaphoreType.DMA((4,)),
            pltpu.SemaphoreType.DMA((4 * len(args),)),
            *[pltpu.VMEM(a.shape, BF) for a in args],
        ],
        after=after,
        carry=carry,
        out_specs=(HBM,) if axis is None else (HBM,) * 4,
        flops=flops,
    )


def swap(parts, axis):
    return lax.all_to_all(parts, axis, 0, 0, tiled=True)


def around(value, dx, dy):
    moves = [(a * 4 + b, (a + dx) % 2 * 4 + (b + dy) % 4) for a in range(2) for b in range(4)]
    return lax.ppermute(value, ("xl", "y"), moves)


def scatter(value, axes):
    return lax.all_to_all(value, axes, 0, 0, tiled=True)


def shards(
    tokens,
    cotangent,
    next_kv_grad,
    seq_lengths,
    pad_counts,
    norm_attn,
    norm_ffn,
    w_query,
    w_keyval,
    w_out,
    w_gate,
    w_up,
    w_down,
):
    place_in_seq = lax.axis_index(SEQ)
    first = (place_in_seq * TOK).astype(jnp.int32)
    half = HD // 2
    freqs = jnp.exp(-jnp.log(THETA) * jnp.arange(half, dtype=F32) * 2.0 / HD)
    freqs = jnp.concatenate([freqs, freqs])[None]
    first = first[None]

    gain_a, gain_b = norm_attn[None], norm_ffn[None]

    hid_a, shared, cos_table, sin_table = kernel_call(
        norm_kv_body,
        (shape(TOK, D), shape(TOK, 256), shape(TOK, HD, dtype=F32), shape(TOK, HD, dtype=F32)),
        (first, seq_lengths, tokens, gain_a, w_keyval, freqs),
        [SMEM] * 2 + [VMEM] * 4,
    )
    near, far = shifted(shared, 1), shifted(shared, 2)
    query = kernel_call(
        query_body,
        shape(TOK, 1024),
        (hid_a, cos_table, sin_table, w_query),
        [VMEM, VMEM, VMEM, HBM],
        [pltpu.VMEM((D, 1024), BF), pltpu.SemaphoreType.DMA((4,))],
    )
    keys_scratch = [pltpu.VMEM((2, 128, 640), F32), pltpu.VMEM((768, 256), BF)]
    attn, lse, branch = kernel_call(
        attend_body,
        (shape(TOK, 1024), shape(8, 256, 1, dtype=F32), shape(TOK, D)),
        (first, seq_lengths, pad_counts, query, far, near, shared, w_out),
        [SMEM] * 3 + [VMEM] * 4 + [HBM],
        keys_scratch + [pltpu.VMEM((1024, D), BF), pltpu.SemaphoreType.DMA((1,))],
    )
    branch_other = step_to(branch, "mp", 1)
    copies = kernel_call(
        copies_body,
        shape(4, TOK, D),
        (cotangent,),
        [VMEM],
        [pltpu.SemaphoreType.DMA((4,))],
        after=(branch,),
        out_specs=(HBM,),
    )
    cot_all = swap(copies, "y")
    d_act, d_act_flag = kernel_call(
        d_act_body,
        (shape(TOK, FF), shape(16, 128)),
        (cotangent, w_down),
        [VMEM, HBM],
        [pltpu.VMEM((FF, D), BF), pltpu.SemaphoreType.DMA((2,))],
        after=(copies,),
    )
    middle, hid_b = kernel_call(
        middle_body,
        (shape(TOK, D, dtype=F32), shape(TOK, D)),
        (tokens, branch, in_vmem(branch_other), gain_b),
        [VMEM] * 4,
        vmem=32,
        after=(d_act_flag,),
    )
    hid_b_all = from_others(hid_b, "z")
    *d_gu, act, d_hid_b = kernel_call(
        ffn_body,
        (shape(TOK, 1408),) * 4 + (shape(4, TOK, 768), shape(TOK, D)),
        (hid_b, d_act, w_gate, w_up),
        [VMEM, HBM, HBM, HBM],
        [
            pltpu.VMEM((D, FF), BF),
            pltpu.VMEM((D, FF), BF),
            pltpu.VMEM((4, TOK, 1408), BF),
            pltpu.VMEM((4, TOK, 768), BF),
            pltpu.VMEM((TOK, FF), BF),
            pltpu.SemaphoreType.DMA((3,)),
            pltpu.SemaphoreType.DMA((3,)),
            pltpu.SemaphoreType.DMA((1,)),
            pltpu.SemaphoreType.DMA((5,)),
        ],
        out_specs=(HBM,) * 5 + (VMEM,),
        flops=3 * 10**10 + 2,
    )
    d_hid_b_other = step_to(d_hid_b, "mp", 1)
    act_all = swap(act, "y")
    ffn = kernel_call(
        down_body,
        shape(TOK, D),
        (act, w_down),
        [VMEM, HBM],
        [pltpu.VMEM((FF, D), BF), pltpu.SemaphoreType.DMA((4,))],
        after=(d_hid_b, cot_all),
    )
    flag, d_gu[2:] = fence((ffn, *hid_b_all[1:]), tuple(d_gu[2:]))
    d_gu = deal(d_gu, "z")
    (d_middle, d_middle_b, d_attn), (held_ffn,) = kernel_call(
        back_body,
        (shape(TOK, D, dtype=F32), shape(TOK, D), shape(TOK, 1024)),
        (cotangent, d_hid_b, d_hid_b_other, middle, gain_b, w_out),
        [VMEM] * 5 + [HBM],
        [
            pltpu.VMEM((1024, D), BF),
            pltpu.VMEM((TOK, D), F32),
            pltpu.VMEM((TOK, D), BF),
            pltpu.SemaphoreType.DMA((3,)),
        ],
        after=(flag,),
        carry=(ffn,),
        out_specs=(HBM, HBM, VMEM),
    )
    d_query, d_far, d_near, d_own, part_a = kernel_call(
        attend_back_body,
        (
            shape(TOK, 1024),
            shape(256, 256),
            shape(256, 256),
            shape(256, 256, dtype=F32),
            shape(TOK, D),
        ),
        (
            first, seq_lengths, pad_counts, query, far, near, shared, attn, d_attn, lse,
            cos_table, sin_table, w_query,
        ),
        [SMEM] * 3 + [VMEM] * 9 + [HBM],
        keys_scratch
        + [
            pltpu.VMEM((1024, 640), BF),
            pltpu.VMEM((1024, 640), BF),
            pltpu.VMEM((1024, HD), BF),
            pltpu.VMEM((1024, HD), BF),
            pltpu.VMEM((768, 256), F32),
            pltpu.VMEM((D, 1024), BF),
            pltpu.SemaphoreType.DMA((1,)),
        ],
    )
    def side_by_side(groups, after=(), flops=1000):
        n = sum(group[0].shape[-1] for group in groups)
        flat = [a for group in groups for a in group]
        return kernel_call(
            functools.partial(sum_body, [len(group) for group in groups]),
            shape(TOK, n),
            flat,
            [VMEM] * len(flat),
            after=after,
            flops=flops,
        )

    g_out = grad("y", pair_each, [d_middle_b], [attn], 1024, after=(part_a,))
    out_got = step_to(g_out[1], "c", 1)
    g_down = grad("z", pair_stacks, [cot_all], [act_all], 768, after=(g_out[0],))
    down_got = step_to(g_down[1], "c", 1)
    ready, _ = fence((g_down[0], *d_gu[1:]))
    local = kernel_call(
        local_body,
        shape(TOK, 256),
        (d_own, shifted(d_near, -1), shifted(d_far, -2)),
        [VMEM] * 3,
        after=(ready,),
    )
    g_gu = grad("y", pair_each, hid_b_all, d_gu, 1408, after=(local, out_got, down_got))
    gu_got = step_to(g_gu[1], "c", 1)
    shared_grad, d_keyval, d_half = kernel_call(
        key_body,
        (shape(TOK, 256, dtype=F32), shape(TOK, 256), shape(TOK, HD)),
        (local, step_to(local, "mp", 1), next_kv_grad, cos_table, sin_table),
        [VMEM] * 5,
        after=(g_gu[0],),
    )
    g_qkv = grad("z", pair_two, [hid_a], [d_query, d_half], 1152, after=(g_gu[0],), flops=3 * 10**10 + 1)
    qkv_got = step_to(g_qkv[1], "c", 1)
    y_sums, (part_a, held_ffn) = add_cores(
        [(g_gu[0], gu_got), (g_out[0], out_got)], after=(g_qkv[0],), carry=(part_a, held_ffn)
    )
    y_parts = swap(y_sums, "y")
    z_sums = add_cores(
        [(g_down[0], down_got), (g_qkv[0], qkv_got)], "z", after=(y_sums,), flops=10**11 + 1
    )
    z_parts = deal(z_sums, "z")
    part_a_other = step_to(part_a, "mp", 1)
    ffn_other = step_to(held_ffn, "mp", 1)
    mixed = kernel_call(
        mixed_body, shape(TOK, D), (middle, held_ffn, ffn_other), [VMEM] * 3, after=(z_parts[0],)
    )
    input_grad = kernel_call(
        last_body,
        shape(TOK, D),
        (tokens, d_middle, part_a, part_a_other, d_keyval, w_keyval, gain_a),
        [VMEM] * 7,
        after=(mixed,),
    )
    in_y = side_by_side([[y_parts]], after=(input_grad,))
    from_xz = scatter(in_y, ("xl", "z"))
    z_spread = kernel_call(
        spread_body,
        (shape(32, 1920),) * 8,
        z_parts,
        [VMEM] * 4,
        [pltpu.VMEM((8, 32, 1920), BF), pltpu.SemaphoreType.DMA((8,))],
        after=(in_y,),
        out_specs=(HBM,) * 8,
        flops=10**11,
    )
    s_gate, s_up, s_out, sum_b = kernel_call(
        finish_y_body,
        (
            shape(32, FF, dtype=F32),
            shape(32, FF, dtype=F32),
            shape(32, 1024, dtype=F32),
            shape(32, 128, dtype=F32),
        ),
        (from_xz, w_gate, w_up),
        [VMEM, HBM, HBM],
        [pltpu.VMEM((32, FF), BF), pltpu.VMEM((32, FF), BF), pltpu.SemaphoreType.DMA((2,))],
    )
    from_xy = [z_spread[0]] + [around(z_spread[k], k // 4, k % 4) for k in range(1, 8)]
    s_down, s_query, sums = kernel_call(
        finish_body,
        (
            shape(32, FF, dtype=F32),
            shape(32, 1024, dtype=F32),
            shape(32, 256, dtype=F32),
        ),
        (*from_xy, sum_b, w_query, w_keyval),
        [VMEM] * 9 + [HBM] * 2,
        [
            pltpu.VMEM((4, 32, 768), F32),
            pltpu.VMEM((32, 1024), BF),
            pltpu.VMEM((32, 256), BF),
            pltpu.SemaphoreType.DMA((2,)),
        ],
    )
    s_down = lax.optimization_barrier(s_down).T
    s_out = lax.optimization_barrier(s_out).T

    mine = place_in_seq * 32
    others = step_to(sums, "mp", 1)
    both = sums[:, :128] + others[:, :128]
    first = lax.axis_index("mp") == 0
    keys, values = jnp.where(first, sums, others), jnp.where(first, others, sums)
    s_keyval = jnp.concatenate([keys[:, 128:], values[:, 128:]], axis=1)
    s_gain_a = both[:, 0] / lax.dynamic_slice_in_dim(norm_attn, mine, 32, 0)
    s_gain_b = both[:, 1] / lax.dynamic_slice_in_dim(norm_ffn, mine, 32, 0)
    return (
        mixed,
        input_grad,
        shared,
        shared_grad,
        s_gain_a,
        s_gain_b,
        s_query,
        s_keyval,
        s_out,
        s_gate,
        s_up,
        s_down,
    )


def solution(mesh):
    fine = Mesh(mesh.devices.reshape(2, 4, 4, 2, 2), SEQ + ("mp",))
    rows = P(SEQ, None)
    placed = (
        rows,
        rows,
        rows,
        P(),
        P(),
        P(),
        P(),
        P(None, "mp"),
        P(),
        P("mp", None),
        P(None, "mp"),
        P(None, "mp"),
        P("mp", None),
    )
    return jax.shard_map(
        shards,
        mesh=fine,
        in_specs=placed,
        out_specs=(
            rows,
            rows,
            rows,
            rows,
            P(SEQ),
            P(SEQ),
            P(SEQ, "mp"),
            rows,
            P("mp", SEQ),
            P(SEQ, "mp"),
            P(SEQ, "mp"),
            P("mp", SEQ),
        ),
        check_vma=False,
    )
```

```python
import functools

import jax
import jax.numpy as jnp
from jax import lax
from jax.experimental import pallas as pl
from jax.experimental.pallas import tpu as pltpu
from jax.sharding import Mesh, PartitionSpec as P

HD = 128
WINDOW = 512
EPSILON = 1e-05
THETA = 10000.0
MASKED = -1e30
SEQ = ("xl", "y", "z", "c")
SIZES = {"xl": 2, "y": 4, "z": 4, "c": 2, "mp": 2}
BF = jnp.bfloat16
F32 = jnp.float32
TOK = 256
D = 2048
HEADS = 8
FF = 2816
SCALE = HD ** (-0.5)
LOG2E = 1.4426950408889634
VMEM = pl.BlockSpec(memory_space=pltpu.VMEM)
SMEM = pl.BlockSpec(memory_space=pltpu.SMEM)
HBM = pl.BlockSpec(memory_space=pl.ANY)
MIB = 2**20


def nn(left, right):
    return jnp.dot(left, right, preferred_element_type=F32)


def nt(left, right):
    return lax.dot_general(left, right, (((1,), (1,)), ((), ())), preferred_element_type=F32)


def tn(left, right):
    return lax.dot_general(left, right, (((0,), (0,)), ((), ())), preferred_element_type=F32)


def shape(*dims, dtype=BF):
    return jax.ShapeDtypeStruct(dims, dtype)


def kernel_call(body, outs, args, specs, scratch=(), vmem=56, after=(), carry=(), out_specs=None, flops=1000):
    single = not isinstance(outs, tuple)
    outs = (outs,) if single else outs
    if out_specs is None:
        out_specs = (VMEM,) * len(outs)
    given, extra, passed = len(args), len(after), len(carry)

    def run(*refs):
        rest = refs[given + extra + passed :]
        body(*refs[:given], *rest[: len(outs)], *rest[len(outs) + passed :])

    result = pl.pallas_call(
        run,
        out_shape=outs + tuple(shape(*c.shape, dtype=c.dtype) for c in carry),
        in_specs=list(specs) + [HBM] * (extra + passed),
        out_specs=tuple(out_specs) + (HBM,) * passed,
        scratch_shapes=list(scratch),
        input_output_aliases={given + extra + i: len(outs) + i for i in range(passed)},
        compiler_params=pltpu.CompilerParams(vmem_limit_bytes=vmem * MIB),
        cost_estimate=pl.CostEstimate(flops=flops, bytes_accessed=1000, transcendentals=0),
    )(*args, *map(in_hbm, after), *map(in_hbm, carry))
    main = result[0] if single else result[: len(outs)]
    return (main, result[len(outs) :]) if carry else main


def in_vmem(value):
    return pltpu.with_memory_space_constraint(value, pltpu.VMEM)


def in_hbm(value):
    return pltpu.with_memory_space_constraint(value, pltpu.HBM)


def fetch(source, target, sems, pieces):
    copies = [
        pltpu.make_async_copy(source.at[piece], target.at[piece], sems.at[i])
        for i, piece in enumerate(pieces)
    ]
    for copy in copies:
        copy.start()
    return copies


def columns(count, width):
    return [(slice(None), pl.ds(i * width, width)) for i in range(count)]


def row_blocks(count, height):
    return [(pl.ds(i * height, height), slice(None)) for i in range(count)]


def turn(value, cos_table, sin_table):
    swapped = jnp.concatenate([value[:, HD // 2 :], value[:, : HD // 2]], axis=1)
    return value * cos_table + swapped * sin_table


def norm_kv_body(
    first_ref, lengths_ref, x_ref, gain_ref, w_ref, freq_ref, hid_ref, kv_ref, cos_ref, sin_ref
):
    index = lax.broadcasted_iota(jnp.int32, (TOK, 1), 0) + first_ref[0]
    place, start = index, jnp.int32(0)
    for s in range(lengths_ref.shape[0]):
        place = jnp.where(index >= start, index - start, place)
        start = start + lengths_ref[s]
    angle = place.astype(F32) * freq_ref[...]
    cos_ref[...] = jnp.cos(angle)
    sin = jnp.sin(angle)
    sin_ref[...] = jnp.where(lax.broadcasted_iota(jnp.int32, (TOK, HD), 1) < HD // 2, -sin, sin)
    x = x_ref[...].astype(F32)
    inv = lax.rsqrt(jnp.mean(x * x, axis=1, keepdims=True) + EPSILON)
    hid = (x * inv * gain_ref[...]).astype(BF)
    hid_ref[...] = hid
    kv = nn(hid, w_ref[...])
    kv_ref[:, :HD] = turn(kv[:, :HD], cos_ref[...], sin_ref[...]).astype(BF)
    kv_ref[:, HD:] = kv[:, HD:].astype(BF)


def query_body(hid_ref, cos_ref, sin_ref, w_ref, q_ref, buf, hid_buf, cos_buf, sin_buf, sems):
    pieces = columns(2, 512)
    weights = [pltpu.make_async_copy(w_ref.at[p], buf.at[p], sems.at[i]) for i, p in enumerate(pieces)]
    pairs = ((hid_ref, hid_buf), (cos_ref, cos_buf), (sin_ref, sin_buf))
    others = [pltpu.make_async_copy(a, b, sems.at[2 + i]) for i, (a, b) in enumerate(pairs)]
    for copy in (others[0], weights[0], others[1], others[2], weights[1]):
        copy.start()
    for copy in others:
        copy.wait()
    hid, cos_table, sin_table = hid_buf[...], cos_buf[...], sin_buf[...]
    for j in range(2):
        weights[j].wait()
        part = nn(hid, buf[:, j * 512 : j * 512 + 512])
        for h in range(4):
            q_ref[:, j * 512 + h * HD : j * 512 + h * HD + HD] = turn(
                part[:, h * HD : h * HD + HD], cos_table, sin_table
            ).astype(BF)


def local_body(own_ref, near_ref, far_ref, out_ref):
    total = own_ref[...] + near_ref[...].astype(F32) + far_ref[...].astype(F32)
    out_ref[...] = total.astype(BF)


def copies_body(in_ref, out_ref, sems):
    copies = [pltpu.make_async_copy(in_ref, out_ref.at[k], sems.at[k]) for k in range(4)]
    for copy in copies:
        copy.start()
    for copy in copies:
        copy.wait()


def add_body(pairs, places, *refs):
    sources = refs[: 2 * pairs]
    outs = refs[2 * pairs : 2 * pairs + (1 if places is None else 4)]
    buf, out_sems, in_sems, *held = refs[2 * pairs + len(outs) :]
    i = 0 if places is None else lax.axis_index(places)
    loads, sends = [], []
    for k in range(4):
        chunk = k if places is None else (i + k) % 4
        loads.append(
            [
                pltpu.make_async_copy(a.at[chunk], b.at[k], in_sems.at[4 * p + k])
                for p, (a, b) in enumerate(zip(sources, held))
            ]
        )
        out = outs[0].at[k] if places is None else outs[k]
        sends.append(pltpu.make_async_copy(buf.at[k], out, out_sems.at[k]))
    for chunk_loads in loads:
        for load in chunk_loads:
            load.start()
    for k in range(4):
        for load in loads[k]:
            load.wait()
        at = 0
        for p in range(pairs):
            total = held[2 * p][k].astype(F32) + held[2 * p + 1][k].astype(F32)
            buf[k, :, at : at + total.shape[1]] = total.astype(BF)
            at += total.shape[1]
        sends[k].start()
    for send in sends:
        send.wait()


def key_body(a_ref, b_ref, next_ref, cos_ref, sin_ref, grad_ref, d_ref, half_ref):
    total = a_ref[...].astype(F32) + b_ref[...].astype(F32) + next_ref[...].astype(F32)
    grad_ref[...] = total
    d_key = turn(total[:, :HD], cos_ref[...], -sin_ref[...]).astype(BF)
    d_value = total[:, HD:].astype(BF)
    d_ref[:, :HD] = d_key
    d_ref[:, HD:] = d_value
    first = lax.axis_index("mp") == 0
    half_ref[...] = jnp.where(first, d_key.astype(F32), d_value.astype(F32)).astype(BF)


def mixed_body(mid_ref, a_ref, b_ref, out_ref):
    out_ref[...] = (mid_ref[...] + (a_ref[...].astype(F32) + b_ref[...].astype(F32))).astype(BF)


def fence_body(out_ref):
    pass


def sum_body(groups, *refs):
    out_ref, at = refs[-1], 0
    for count in groups:
        group, refs = refs[:count], refs[count:]
        stacked = count == 1 and len(group[0].shape) == 3
        pieces = [group[0].at[k] for k in range(4)] if stacked else group
        total = sum(p[...].astype(F32) for p in pieces)
        out_ref[:, at : at + total.shape[1]] = total.astype(BF)
        at += total.shape[1]


def spread_body(a_ref, b_ref, c_ref, d_ref, *refs):
    outs, buf, sems = refs[:8], refs[8], refs[9]
    total = a_ref[...].astype(F32) + b_ref[...].astype(F32)
    total = (total + c_ref[...].astype(F32) + d_ref[...].astype(F32)).astype(BF)
    for k in range(8):
        buf[k] = total[k * 32 : k * 32 + 32]
    xl, y = lax.axis_index("xl"), lax.axis_index("y")
    sends = []
    for k, out in enumerate(outs):
        place = (xl + k // 4) % 2 * 4 + (y + k % 4) % 4
        sends.append(pltpu.make_async_copy(buf.at[place], out, sems.at[k]))
    for send in sends:
        send.start()
    for send in sends:
        send.wait()


def my_rows(copies, arrays, bufs, sems):
    place = 0
    for axis in SEQ:
        place = place * SIZES[axis] + lax.axis_index(axis)
    rows = pl.ds(pl.multiple_of(place * 32, 32), 32)
    for i, (array, buf) in enumerate(zip(arrays, bufs)):
        copies.append(pltpu.make_async_copy(array.at[rows], buf, sems.at[i]))
        copies[-1].start()
    return copies


def row_sums(weights, grads):
    return jnp.sum(weights[...].astype(F32) * grads, axis=1, keepdims=True)


def finish_y_body(got_ref, wg_ref, wu_ref, gate_ref, up_ref, out_ref, sum_ref, wg, wu, sems):
    copies = my_rows([], (wg_ref, wu_ref), (wg, wu), sems)
    both = got_ref[0:128].astype(F32) + got_ref[128:256].astype(F32)
    part = [both[z * 32 : z * 32 + 32] for z in range(4)]
    out_ref[...] = part[0][:, 1408:] + part[1][:, 1408:] + part[2][:, 1408:] + part[3][:, 1408:]
    for copy in copies:
        copy.wait()
    total = jnp.zeros((32, 1), F32)
    for ref, weights, z in ((gate_ref, wg, 0), (up_ref, wu, 2)):
        for half in range(2):
            grads = part[z + half][:, :1408]
            lanes = slice(half * 1408, half * 1408 + 1408)
            ref[:, lanes] = grads
            total += row_sums(weights[:, lanes], grads)
    sum_ref[...] = jnp.broadcast_to(total, (32, 128))


def finish_body(*refs):
    pieces, (sum_b_ref, wq_ref, wk_ref, down_ref, query_ref, sum_ref, parts, wq, wk, sems) = (
        refs[:8],
        refs[8:],
    )
    copies = my_rows([], (wq_ref, wk_ref), (wq, wk), sems)
    rest = sum(p[:, 768:].astype(F32) for p in pieces)
    query_ref[...] = rest[:, :1024]
    y = lax.axis_index("y")
    for dy in range(4):
        part = pieces[dy][:, :768].astype(F32) + pieces[4 + dy][:, :768].astype(F32)
        parts[(y + 4 - dy) % 4] = part
    for i in range(4):
        low, high = ACT_STARTS[i] * 128, ACT_STARTS[i + 1] * 128
        down_ref[:, low:high] = parts[i][:, : high - low]
    for copy in copies:
        copy.wait()
    lane = lax.broadcasted_iota(jnp.int32, (32, 128), 1)
    keys = rest[:, 1024:]
    key_weights = wk[:, pl.ds(pl.multiple_of(lax.axis_index("mp") * HD, HD), HD)]
    sum_a = row_sums(wq, rest[:, :1024]) + row_sums(key_weights, keys)
    sum_ref[:, :128] = jnp.where(lane == 1, sum_b_ref[...], sum_a)
    sum_ref[:, 128:] = keys


def fill_bias(first_ref, lengths_ref, pads_ref, bias):
    first = first_ref[0]
    count = lengths_ref.shape[0]
    starts, lives = [], []
    begin = jnp.int32(0)
    for s in range(count):
        starts.append(begin)
        lives.append(begin + lengths_ref[s] - pads_ref[s])
        begin = begin + lengths_ref[s]
    for b in range(2):
        row = lax.broadcasted_iota(jnp.int32, (128, 1), 0) + b * 128
        col = lax.broadcasted_iota(jnp.int32, (1, 640), 1) + b * 128
        query = row + first
        key = col + (first - WINDOW)
        low = jnp.zeros((128, 1), jnp.int32)
        real = jnp.zeros((1, 640), jnp.int32)
        for s in range(count):
            low = jnp.where(query >= starts[s], starts[s], low)
            real = jnp.where((key >= starts[s]) & (key < lives[s]), 1, real)
        low = jnp.maximum(low, query - (WINDOW - 1))
        here = lax.broadcasted_iota(jnp.int32, (128, 640), 1) + b * 128 + (first - WINDOW)
        when = lax.broadcasted_iota(jnp.int32, (128, 640), 0) + b * 128 + first
        seen = jnp.where(jnp.broadcast_to(real, (128, 640)) > 0, here, when + 1)
        ok = (here == when) | ((here >= low) & (seen <= when))
        bias[b] = jnp.where(ok, 0.0, MASKED)


def two_heads(ref, b, pair):
    rows = slice(b * 128, b * 128 + 128)
    return jnp.concatenate(
        [ref[rows, h * HD : h * HD + HD] for h in (2 * pair, 2 * pair + 1)], axis=0
    )


def attend_body(
    first_ref, lengths_ref, pads_ref, q_ref, far_ref, near_ref, kv_ref, w_ref,
    attn_ref, lse_ref, out_ref, bias, keys, buf, sem,
):
    copy = pltpu.make_async_copy(w_ref, buf, sem.at[0])
    copy.start()
    fill_bias(first_ref, lengths_ref, pads_ref, bias)
    keys[0:256] = far_ref[...]
    keys[256:512] = near_ref[...]
    keys[512:768] = kv_ref[...]
    for b in range(2):
        k = keys[b * 128 : b * 128 + 640, :HD]
        v = keys[b * 128 : b * 128 + 640, HD:]
        for pair in range(4):
            scores = nt(two_heads(q_ref, b, pair), k) * (SCALE * LOG2E)
            scores = scores + jnp.concatenate([bias[b], bias[b]], axis=0)
            top = jnp.max(scores, axis=1, keepdims=True)
            exps = jnp.exp2(scores - top)
            total = jnp.sum(exps, axis=1, keepdims=True)
            out = nn(exps.astype(BF), v) / total
            lse_ref[b * 4 + pair] = top + jnp.log2(total)
            for h in range(2):
                lanes = slice((2 * pair + h) * HD, (2 * pair + h) * HD + HD)
                attn_ref[b * 128 : b * 128 + 128, lanes] = out[h * 128 : h * 128 + 128].astype(BF)
    copy.wait()
    attn = attn_ref[...]
    for j in range(4):
        out_ref[:, j * 512 : j * 512 + 512] = nn(attn, buf[:, j * 512 : j * 512 + 512]).astype(BF)


def d_act_body(cot_ref, w_ref, out_ref, flag_ref, buf, sems):
    copies = fetch(w_ref, buf, sems, row_blocks(2, 1408))
    cot = cot_ref[...]
    for j in range(2):
        copies[j].wait()
        rows = slice(j * 1408, j * 1408 + 1408)
        out_ref[:, rows] = nt(cot, buf[rows]).astype(BF)
    flag_ref[...] = cot[0:16, 0:128]


def middle_body(x_ref, a_ref, b_ref, gain_ref, mid_ref, hid_ref):
    mid = x_ref[...].astype(F32) + (a_ref[...].astype(F32) + b_ref[...].astype(F32))
    mid_ref[...] = mid
    inv = lax.rsqrt(jnp.mean(mid * mid, axis=1, keepdims=True) + EPSILON)
    hid = (mid * inv * gain_ref[...]).astype(BF)
    hid_ref[...] = hid


ACT_STARTS = (0, 6, 12, 17, 22)


def act_place(tile):
    part = max(i for i in range(4) if ACT_STARTS[i] <= tile)
    return part, (tile - ACT_STARTS[part]) * 128


FFN_STARTS = (0, 4, 12, 22)


def ffn_body(
    hid_ref, d_act_ref, wg_ref, wu_ref,
    d0, d1, d2, d3, act_out, out_ref,
    bufg, bufu, d_buf, act_buf, d_act_buf, semg, semu, sem_in, sem_out,
):
    pieces = [
        (slice(None), pl.ds(low * 128, (high - low) * 128))
        for low, high in zip(FFN_STARTS, FFN_STARTS[1:])
    ]
    gates = [pltpu.make_async_copy(wg_ref.at[p], bufg.at[p], semg.at[i]) for i, p in enumerate(pieces)]
    ups = [pltpu.make_async_copy(wu_ref.at[p], bufu.at[p], semu.at[i]) for i, p in enumerate(pieces)]
    d_act_in = pltpu.make_async_copy(d_act_ref, d_act_buf, sem_in.at[0])
    gates[0].start()
    ups[0].start()
    d_act_in.start()
    for g, u in zip(gates[1:], ups[1:]):
        g.start()
        u.start()
    hid = hid_ref[...]
    for j in range(3):
        low, high = FFN_STARTS[j], FFN_STARTS[j + 1]
        cols = slice(low * 128, high * 128)
        gates[j].wait()
        gate = nn(hid, bufg[:, cols])
        ups[j].wait()
        up = nn(hid, bufu[:, cols])
        if j == 0:
            d_act_in.wait()
        sigm = 1.0 / (1.0 + jnp.exp(-gate))
        silu = gate * sigm
        d_act = d_act_buf[:, cols].astype(F32)
        act = (silu * up).astype(BF)
        d_up = (d_act * silu).astype(BF)
        d_gate = (d_act * up * (sigm + silu * (1.0 - sigm))).astype(BF)
        for tile in range(low, high):
            lanes = slice((tile - low) * 128, (tile - low) * 128 + 128)
            part, at = act_place(tile)
            act_buf[part, :, at : at + 128] = act[:, lanes]
            quarter, at = tile // 11, (tile % 11) * 128
            d_buf[quarter, :, at : at + 128] = d_gate[:, lanes]
            d_buf[2 + quarter, :, at : at + 128] = d_up[:, lanes]
    for part in (2, 3):
        act_buf[part, :, 640:768] = jnp.zeros((TOK, 128), BF)
    z = lax.axis_index("z")
    sends = [pltpu.make_async_copy(act_buf, act_out, sem_out.at[4])]
    for k, d_out in enumerate((d0, d1, d2, d3)):
        sends.append(pltpu.make_async_copy(d_buf.at[(z + k) % 4], d_out, sem_out.at[k]))
    for send in sends:
        send.start()
    for i in range(2):
        rows = slice(i * 1024, i * 1024 + 1024)
        total = nt(d_buf[0], bufg[rows, :1408]) + nt(d_buf[1], bufg[rows, 1408:])
        total += nt(d_buf[2], bufu[rows, :1408]) + nt(d_buf[3], bufu[rows, 1408:])
        out_ref[:, rows] = total.astype(BF)
    for send in sends:
        send.wait()


def down_body(act_ref, w_ref, out_ref, buf, sems):
    copies = fetch(w_ref, buf, sems, columns(4, 512))
    for i in range(4):
        copies[i].wait()
        cols = slice(i * 512, i * 512 + 512)
        total = jnp.zeros((TOK, 512), F32)
        for part in range(4):
            low, high = ACT_STARTS[part] * 128, ACT_STARTS[part + 1] * 128
            total += nn(act_ref[part, :, : high - low], buf[low:high, cols])
        out_ref[:, cols] = total.astype(BF)


def back_body(
    cot_ref, a_ref, b_ref, mid_ref, gain_ref, w_ref,
    d_mid_ref, low_ref, d_attn_ref, buf, d_mid_buf, low_buf, sem,
):
    copy = pltpu.make_async_copy(w_ref, buf, sem.at[0])
    copy.start()
    mid = mid_ref[...]
    inv = lax.rsqrt(jnp.mean(mid * mid, axis=1, keepdims=True) + EPSILON)
    normed = mid * inv
    e = (a_ref[...].astype(F32) + b_ref[...].astype(F32)) * gain_ref[...]
    d_mid = cot_ref[...].astype(F32) + inv * (
        e - normed * jnp.mean(e * normed, axis=1, keepdims=True)
    )
    d_mid_buf[...] = d_mid
    low = d_mid.astype(BF)
    low_buf[...] = low
    sends = [
        pltpu.make_async_copy(d_mid_buf, d_mid_ref, sem.at[1]),
        pltpu.make_async_copy(low_buf, low_ref, sem.at[2]),
    ]
    for send in sends:
        send.start()
    copy.wait()
    d_attn_ref[...] = nt(low, buf[...]).astype(BF)
    for send in sends:
        send.wait()


def attend_back_body(
    first_ref, lengths_ref, pads_ref, q_ref, far_ref, near_ref, kv_ref, attn_ref, d_attn_ref, lse_ref,
    cos_ref, sin_ref, w_ref,
    dq_ref, d_far_ref, d_near_ref, d_own_ref, out_ref,
    bias, keys, stack_p, stack_d, stack_q, stack_o, total, buf, sem,
):
    copy = pltpu.make_async_copy(w_ref, buf, sem.at[0])
    copy.start()
    fill_bias(first_ref, lengths_ref, pads_ref, bias)
    keys[0:256] = far_ref[...]
    keys[256:512] = near_ref[...]
    keys[512:768] = kv_ref[...]
    total[...] = jnp.zeros_like(total)
    for b in range(2):
        window = slice(b * 128, b * 128 + 640)
        rows = slice(b * 128, b * 128 + 128)
        k = keys[window, :HD]
        v = keys[window, HD:]
        for pair in range(4):
            here = slice(pair * 256, pair * 256 + 256)
            q2 = two_heads(q_ref, b, pair)
            do2 = two_heads(d_attn_ref, b, pair)
            o2 = two_heads(attn_ref, b, pair)
            stack_q[here] = q2
            stack_o[here] = do2
            delta = jnp.sum(do2.astype(F32) * o2.astype(F32), axis=1, keepdims=True)
            scores = nt(q2, k) * (SCALE * LOG2E) + jnp.concatenate([bias[b], bias[b]], axis=0)
            prob = jnp.exp2(scores - lse_ref[b * 4 + pair])
            stack_p[here] = prob.astype(BF)
            d_score = (prob * (nt(do2, v) - delta)).astype(BF)
            stack_d[here] = d_score
            dq = nn(d_score, k) * SCALE
            for h in range(2):
                lanes = slice((2 * pair + h) * HD, (2 * pair + h) * HD + HD)
                dq_ref[rows, lanes] = turn(
                    dq[h * 128 : h * 128 + 128], cos_ref[rows], -sin_ref[rows]
                ).astype(BF)
        total[window, :HD] += tn(stack_d[...], stack_q[...]) * SCALE
        total[window, HD:] += tn(stack_p[...], stack_o[...])
    d_far_ref[...] = total[0:256].astype(BF)
    d_near_ref[...] = total[256:512].astype(BF)
    d_own_ref[...] = total[512:768]
    copy.wait()
    dq = dq_ref[...]
    for j in range(4):
        rows = slice(j * 512, j * 512 + 512)
        out_ref[:, rows] = nt(dq, buf[rows]).astype(BF)


def last_body(x_ref, d_mid_ref, a_ref, b_ref, d_kv_ref, w_ref, gain_ref, out_ref):
    x = x_ref[...].astype(F32)
    inv = lax.rsqrt(jnp.mean(x * x, axis=1, keepdims=True) + EPSILON)
    normed = x * inv
    d_hid = a_ref[...].astype(F32) + b_ref[...].astype(F32) + nt(d_kv_ref[...], w_ref[...])
    e = d_hid * gain_ref[...]
    out = d_mid_ref[...] + inv * (e - normed * jnp.mean(e * normed, axis=1, keepdims=True))
    out_ref[...] = out.astype(BF)


def pair_each(lefts, rights):
    return [list(zip(lefts, rights, strict=True))]


def pair_stacks(lefts, rights):
    return [[(lefts[0].at[k], rights[0].at[k]) for k in range(4)]]


def pair_two(lefts, rights):
    return [[(lefts[0], right)] for right in rights]


def grad_body(axis, pairing, lefts, rights, *refs):
    sources, outs = refs[: lefts + rights], refs[lefts + rights : lefts + rights + 2]
    buf, out_sems, in_sems, *held = refs[lefts + rights + 2 :]
    stacked = len(sources[0].shape) == 3
    pieces = [(a, b) for a, b in zip(sources, held)]
    if stacked:
        pieces = [(a.at[k], b.at[k]) for a, b in pieces for k in range(4)]
    count = 4 if stacked else lefts
    loads = [pltpu.make_async_copy(a, b, in_sems.at[i]) for i, (a, b) in enumerate(pieces)]
    for i in range(max(count, len(loads) - count)):
        for load in loads[:count][i : i + 1] + loads[count:][i : i + 1]:
            load.start()
    groups = pairing(held[:lefts], held[lefts:])
    if count == 1:
        for load in loads:
            load.wait()
    me = lax.axis_index("c")
    sends = []
    for step in range(8):
        xl, y = step % 2, step // 2
        block = xl * 4 + y
        cols = slice(block * 256, block * 256 + 256)
        at = 0
        for group in groups:
            total = None
            for i, (left, right) in enumerate(group):
                if step == 0 and count > 1:
                    loads[i].wait()
                    loads[count + i].wait()
                part = tn(left[:, cols], right[...])
                total = part if total is None else total + part
            total = total.astype(BF)
            lanes = slice(at, at + total.shape[1])
            at += total.shape[1]
            for z in range(4):
                chunk, row = (y, xl * 128 + z * 32) if axis == "y" else (z, xl * 128 + y * 32)
                for core in range(2):
                    rows = total[z * 64 + core * 32 : z * 64 + core * 32 + 32]
                    buf[(me + core) % 2, chunk, row : row + 32, lanes] = rows
        if axis == "y" and xl == 1:
            sends += [
                pltpu.make_async_copy(buf.at[k, y], out.at[y], out_sems.at[4 * k + y])
                for k, out in enumerate(outs)
            ]
            for send in sends[-2:]:
                send.start()
        if axis == "z":
            rows = pl.ds(xl * 128 + y * 32, 32)
            sends += [
                pltpu.make_async_copy(buf.at[k, :, rows], out.at[:, rows], out_sems.at[8 * k + step])
                for k, out in enumerate(outs)
            ]
            for send in sends[-2:]:
                send.start()
    for send in sends:
        send.wait()


def grad(axis, pairing, lefts, rights, n, after=(), carry=(), flops=1000):
    args = tuple(map(in_hbm, (*lefts, *rights)))
    return kernel_call(
        functools.partial(grad_body, axis, pairing, len(lefts), len(rights)),
        (shape(4, 256, n),) * 2,
        args,
        [HBM] * len(args),
        [
            pltpu.VMEM((2, 4, 256, n), BF),
            pltpu.SemaphoreType.DMA((16,)),
            pltpu.SemaphoreType.DMA((8 if args[0].ndim == 3 else len(args),)),
            *[pltpu.VMEM(a.shape, BF) for a in args],
        ],
        flops=flops,
        after=after,
        carry=carry,
        out_specs=(HBM,) * 2,
    )


def step_to(value, axis, steps):
    count = SIZES[axis]
    return lax.ppermute(value, axis, [(i, (i + steps) % count) for i in range(count)])


def shifted(value, steps):
    count = 64
    first, last = max(0, -steps), min(count, count - steps)
    return lax.ppermute(value, SEQ, [(i, i + steps) for i in range(first, last)])


def pick(stack, index):
    return lax.dynamic_index_in_dim(stack, index, 0, keepdims=False)


def fence(after, carry=()):
    result = kernel_call(
        fence_body, shape(8, 128, dtype=F32), (), [], after=after, carry=carry, flops=3 * 10**10, out_specs=(HBM,)
    )
    return result if carry else (result, ())


def from_others(value, axis):
    return [value] + [step_to(value, axis, k) for k in (1, 2, 3)]


def deal(parts, axis):
    return [parts[0]] + [step_to(parts[k], axis, k) for k in (1, 2, 3)]


def add_cores(pairs, axis=None, after=(), carry=(), flops=1000, near=False):
    rows, n = pairs[0][0].shape[1], sum(own.shape[2] for own, _ in pairs)
    args = tuple(a for pair in pairs for a in (in_hbm(pair[0]), (in_vmem if near else in_hbm)(pair[1])))
    outs = shape(4, rows, n) if axis is None else (shape(rows, n),) * 4
    return kernel_call(
        functools.partial(add_body, len(pairs), axis),
        outs,
        args,
        [HBM] * len(args),
        [
            pltpu.VMEM((4, rows, n), BF),
            pltpu.SemaphoreType.DMA((4,)),
            pltpu.SemaphoreType.DMA((4 * len(args),)),
            *[pltpu.VMEM(a.shape, BF) for a in args],
        ],
        after=after,
        carry=carry,
        out_specs=(HBM,) if axis is None else (HBM,) * 4,
        flops=flops,
    )


def swap(parts, axis):
    return lax.all_to_all(parts, axis, 0, 0, tiled=True)


def around(value, dx, dy):
    moves = [(a * 4 + b, (a + dx) % 2 * 4 + (b + dy) % 4) for a in range(2) for b in range(4)]
    return lax.ppermute(value, ("xl", "y"), moves)


def scatter(value, axes):
    return lax.all_to_all(value, axes, 0, 0, tiled=True)


def shards(
    tokens,
    cotangent,
    next_kv_grad,
    seq_lengths,
    pad_counts,
    norm_attn,
    norm_ffn,
    w_query,
    w_keyval,
    w_out,
    w_gate,
    w_up,
    w_down,
):
    place_in_seq = lax.axis_index(SEQ)
    first = (place_in_seq * TOK).astype(jnp.int32)
    half = HD // 2
    freqs = jnp.exp(-jnp.log(THETA) * jnp.arange(half, dtype=F32) * 2.0 / HD)
    freqs = jnp.concatenate([freqs, freqs])[None]
    first = first[None]

    gain_a, gain_b = norm_attn[None], norm_ffn[None]

    hid_a, shared, cos_table, sin_table = kernel_call(
        norm_kv_body,
        (shape(TOK, D), shape(TOK, 256), shape(TOK, HD, dtype=F32), shape(TOK, HD, dtype=F32)),
        (first, seq_lengths, tokens, gain_a, w_keyval, freqs),
        [SMEM] * 2 + [VMEM] * 4,
    )
    near, far = shifted(shared, 1), shifted(shared, 2)
    query = kernel_call(
        query_body,
        shape(TOK, 1024),
        (hid_a, cos_table, sin_table, w_query),
        [HBM] * 4,
        [
            pltpu.VMEM((D, 1024), BF),
            pltpu.VMEM((TOK, D), BF),
            pltpu.VMEM((TOK, HD), F32),
            pltpu.VMEM((TOK, HD), F32),
            pltpu.SemaphoreType.DMA((5,)),
        ],
    )
    keys_scratch = [pltpu.VMEM((2, 128, 640), F32), pltpu.VMEM((768, 256), BF)]
    attn, lse, branch = kernel_call(
        attend_body,
        (shape(TOK, 1024), shape(8, 256, 1, dtype=F32), shape(TOK, D)),
        (first, seq_lengths, pad_counts, query, far, near, shared, w_out),
        [SMEM] * 3 + [VMEM] * 4 + [HBM],
        keys_scratch + [pltpu.VMEM((1024, D), BF), pltpu.SemaphoreType.DMA((1,))],
    )
    branch_other = step_to(branch, "mp", 1)
    copies = kernel_call(
        copies_body,
        shape(4, TOK, D),
        (cotangent,),
        [VMEM],
        [pltpu.SemaphoreType.DMA((4,))],
        after=(branch,),
        out_specs=(HBM,),
    )
    cot_all = swap(copies, "y")
    d_act, d_act_flag = kernel_call(
        d_act_body,
        (shape(TOK, FF), shape(16, 128)),
        (cotangent, w_down),
        [VMEM, HBM],
        [pltpu.VMEM((FF, D), BF), pltpu.SemaphoreType.DMA((2,))],
        after=(copies,),
    )
    middle, hid_b = kernel_call(
        middle_body,
        (shape(TOK, D, dtype=F32), shape(TOK, D)),
        (tokens, branch, in_vmem(branch_other), gain_b),
        [VMEM] * 4,
        vmem=32,
        after=(d_act_flag,),
    )
    hid_b_all = from_others(hid_b, "z")
    *d_gu, act, d_hid_b = kernel_call(
        ffn_body,
        (shape(TOK, 1408),) * 4 + (shape(4, TOK, 768), shape(TOK, D)),
        (hid_b, d_act, w_gate, w_up),
        [VMEM, HBM, HBM, HBM],
        [
            pltpu.VMEM((D, FF), BF),
            pltpu.VMEM((D, FF), BF),
            pltpu.VMEM((4, TOK, 1408), BF),
            pltpu.VMEM((4, TOK, 768), BF),
            pltpu.VMEM((TOK, FF), BF),
            pltpu.SemaphoreType.DMA((3,)),
            pltpu.SemaphoreType.DMA((3,)),
            pltpu.SemaphoreType.DMA((1,)),
            pltpu.SemaphoreType.DMA((5,)),
        ],
        out_specs=(HBM,) * 5 + (VMEM,),
        flops=3 * 10**10 + 2,
    )
    d_hid_b_other = step_to(d_hid_b, "mp", 1)
    act_all = swap(act, "y")
    ffn = kernel_call(
        down_body,
        shape(TOK, D),
        (act, w_down),
        [VMEM, HBM],
        [pltpu.VMEM((FF, D), BF), pltpu.SemaphoreType.DMA((4,))],
        after=(d_hid_b, cot_all),
    )
    flag, d_gu[2:] = fence((ffn, *hid_b_all[1:]), tuple(d_gu[2:]))
    d_gu = deal(d_gu, "z")
    (d_middle, d_middle_b, d_attn), (held_ffn,) = kernel_call(
        back_body,
        (shape(TOK, D, dtype=F32), shape(TOK, D), shape(TOK, 1024)),
        (cotangent, d_hid_b, d_hid_b_other, middle, gain_b, w_out),
        [VMEM] * 5 + [HBM],
        [
            pltpu.VMEM((1024, D), BF),
            pltpu.VMEM((TOK, D), F32),
            pltpu.VMEM((TOK, D), BF),
            pltpu.SemaphoreType.DMA((3,)),
        ],
        after=(flag,),
        carry=(ffn,),
        out_specs=(HBM, HBM, VMEM),
    )
    d_query, d_far, d_near, d_own, part_a = kernel_call(
        attend_back_body,
        (
            shape(TOK, 1024),
            shape(256, 256),
            shape(256, 256),
            shape(256, 256, dtype=F32),
            shape(TOK, D),
        ),
        (
            first, seq_lengths, pad_counts, query, far, near, shared, attn, d_attn, lse,
            cos_table, sin_table, w_query,
        ),
        [SMEM] * 3 + [VMEM] * 9 + [HBM],
        keys_scratch
        + [
            pltpu.VMEM((1024, 640), BF),
            pltpu.VMEM((1024, 640), BF),
            pltpu.VMEM((1024, HD), BF),
            pltpu.VMEM((1024, HD), BF),
            pltpu.VMEM((768, 256), F32),
            pltpu.VMEM((D, 1024), BF),
            pltpu.SemaphoreType.DMA((1,)),
        ],
    )
    def side_by_side(groups, after=(), flops=1000):
        n = sum(group[0].shape[-1] for group in groups)
        flat = [a for group in groups for a in group]
        return kernel_call(
            functools.partial(sum_body, [len(group) for group in groups]),
            shape(TOK, n),
            flat,
            [VMEM] * len(flat),
            after=after,
            flops=flops,
        )

    g_out = grad("y", pair_each, [d_middle_b], [attn], 1024, after=(part_a,))
    out_got = step_to(g_out[1], "c", 1)
    g_down = grad("z", pair_stacks, [cot_all], [act_all], 768, after=(g_out[0],))
    down_got = step_to(g_down[1], "c", 1)
    ready, _ = fence((g_down[0], *d_gu[1:]))
    local = kernel_call(
        local_body,
        shape(TOK, 256),
        (d_own, shifted(d_near, -1), shifted(d_far, -2)),
        [VMEM] * 3,
        after=(ready,),
    )
    g_gu = grad("y", pair_each, hid_b_all, d_gu, 1408, after=(local, out_got, down_got))
    gu_got = step_to(g_gu[1], "c", 1)
    shared_grad, d_keyval, d_half = kernel_call(
        key_body,
        (shape(TOK, 256, dtype=F32), shape(TOK, 256), shape(TOK, HD)),
        (local, step_to(local, "mp", 1), next_kv_grad, cos_table, sin_table),
        [VMEM] * 5,
        after=(g_gu[0],),
    )
    g_qkv = grad("z", pair_two, [hid_a], [d_query, d_half], 1152, after=(g_gu[0],), flops=3 * 10**10 + 1)
    qkv_got = step_to(g_qkv[1], "c", 1)
    y_sums, (part_a, held_ffn) = add_cores(
        [(g_gu[0], gu_got), (g_out[0], out_got)], after=(g_qkv[0],), carry=(part_a, held_ffn), near=True
    )
    y_parts = swap(y_sums, "y")
    z_sums = add_cores(
        [(g_down[0], down_got), (g_qkv[0], qkv_got)], "z", after=(y_sums,), flops=10**11 + 1
    )
    z_parts = deal(z_sums, "z")
    part_a_other = step_to(part_a, "mp", 1)
    ffn_other = step_to(held_ffn, "mp", 1)
    mixed = kernel_call(
        mixed_body, shape(TOK, D), (middle, held_ffn, ffn_other), [VMEM] * 3, after=(z_parts[0],)
    )
    input_grad = kernel_call(
        last_body,
        shape(TOK, D),
        (tokens, d_middle, part_a, part_a_other, d_keyval, w_keyval, gain_a),
        [VMEM] * 7,
        after=(mixed,),
    )
    in_y = side_by_side([[y_parts]], after=(input_grad,))
    from_xz = scatter(in_y, ("xl", "z"))
    z_spread = kernel_call(
        spread_body,
        (shape(32, 1920),) * 8,
        z_parts,
        [VMEM] * 4,
        [pltpu.VMEM((8, 32, 1920), BF), pltpu.SemaphoreType.DMA((8,))],
        after=(in_y,),
        out_specs=(HBM,) * 8,
        flops=10**11,
    )
    s_gate, s_up, s_out, sum_b = kernel_call(
        finish_y_body,
        (
            shape(32, FF, dtype=F32),
            shape(32, FF, dtype=F32),
            shape(32, 1024, dtype=F32),
            shape(32, 128, dtype=F32),
        ),
        (from_xz, w_gate, w_up),
        [VMEM, HBM, HBM],
        [pltpu.VMEM((32, FF), BF), pltpu.VMEM((32, FF), BF), pltpu.SemaphoreType.DMA((2,))],
    )
    from_xy = [z_spread[0]] + [around(z_spread[k], k // 4, k % 4) for k in range(1, 8)]
    s_down, s_query, sums = kernel_call(
        finish_body,
        (
            shape(32, FF, dtype=F32),
            shape(32, 1024, dtype=F32),
            shape(32, 256, dtype=F32),
        ),
        (*from_xy, sum_b, w_query, w_keyval),
        [VMEM] * 9 + [HBM] * 2,
        [
            pltpu.VMEM((4, 32, 768), F32),
            pltpu.VMEM((32, 1024), BF),
            pltpu.VMEM((32, 256), BF),
            pltpu.SemaphoreType.DMA((2,)),
        ],
    )
    s_down = lax.optimization_barrier(s_down).T
    s_out = lax.optimization_barrier(s_out).T

    mine = place_in_seq * 32
    others = step_to(sums, "mp", 1)
    both = sums[:, :128] + others[:, :128]
    first = lax.axis_index("mp") == 0
    keys, values = jnp.where(first, sums, others), jnp.where(first, others, sums)
    s_keyval = jnp.concatenate([keys[:, 128:], values[:, 128:]], axis=1)
    s_gain_a = both[:, 0] / lax.dynamic_slice_in_dim(norm_attn, mine, 32, 0)
    s_gain_b = both[:, 1] / lax.dynamic_slice_in_dim(norm_ffn, mine, 32, 0)
    return (
        mixed,
        input_grad,
        shared,
        shared_grad,
        s_gain_a,
        s_gain_b,
        s_query,
        s_keyval,
        s_out,
        s_gate,
        s_up,
        s_down,
    )


def solution(mesh):
    fine = Mesh(mesh.devices.reshape(2, 4, 4, 2, 2), SEQ + ("mp",))
    rows = P(SEQ, None)
    placed = (
        rows,
        rows,
        rows,
        P(),
        P(),
        P(),
        P(),
        P(None, "mp"),
        P(),
        P("mp", None),
        P(None, "mp"),
        P(None, "mp"),
        P("mp", None),
    )
    return jax.shard_map(
        shards,
        mesh=fine,
        in_specs=placed,
        out_specs=(
            rows,
            rows,
            rows,
            rows,
            P(SEQ),
            P(SEQ),
            P(SEQ, "mp"),
            rows,
            P("mp", SEQ),
            P(SEQ, "mp"),
            P(SEQ, "mp"),
            P("mp", SEQ),
        ),
        check_vma=False,
    )
```

```python
import functools

import jax
import jax.numpy as jnp
from jax import lax
from jax.experimental import pallas as pl
from jax.experimental.pallas import tpu as pltpu
from jax.sharding import Mesh, PartitionSpec as P

HD = 128
WINDOW = 512
EPSILON = 1e-05
THETA = 10000.0
MASKED = -1e30
SEQ = ("xl", "y", "z", "c")
SIZES = {"xl": 2, "y": 4, "z": 4, "c": 2, "mp": 2}
BF = jnp.bfloat16
F32 = jnp.float32
TOK = 256
D = 2048
HEADS = 8
FF = 2816
SCALE = HD ** (-0.5)
LOG2E = 1.4426950408889634
VMEM = pl.BlockSpec(memory_space=pltpu.VMEM)
SMEM = pl.BlockSpec(memory_space=pltpu.SMEM)
HBM = pl.BlockSpec(memory_space=pl.ANY)
MIB = 2**20


def nn(left, right):
    return jnp.dot(left, right, preferred_element_type=F32)


def nt(left, right):
    return lax.dot_general(left, right, (((1,), (1,)), ((), ())), preferred_element_type=F32)


def tn(left, right):
    return lax.dot_general(left, right, (((0,), (0,)), ((), ())), preferred_element_type=F32)


def shape(*dims, dtype=BF):
    return jax.ShapeDtypeStruct(dims, dtype)


def kernel_call(body, outs, args, specs, scratch=(), vmem=56, after=(), carry=(), out_specs=None, flops=1000):
    single = not isinstance(outs, tuple)
    outs = (outs,) if single else outs
    if out_specs is None:
        out_specs = (VMEM,) * len(outs)
    given, extra, passed = len(args), len(after), len(carry)

    def run(*refs):
        rest = refs[given + extra + passed :]
        body(*refs[:given], *rest[: len(outs)], *rest[len(outs) + passed :])

    result = pl.pallas_call(
        run,
        out_shape=outs + tuple(shape(*c.shape, dtype=c.dtype) for c in carry),
        in_specs=list(specs) + [HBM] * (extra + passed),
        out_specs=tuple(out_specs) + (HBM,) * passed,
        scratch_shapes=list(scratch),
        input_output_aliases={given + extra + i: len(outs) + i for i in range(passed)},
        compiler_params=pltpu.CompilerParams(vmem_limit_bytes=vmem * MIB),
        cost_estimate=pl.CostEstimate(flops=flops, bytes_accessed=1000, transcendentals=0),
    )(*args, *map(in_hbm, after), *map(in_hbm, carry))
    main = result[0] if single else result[: len(outs)]
    return (main, result[len(outs) :]) if carry else main


def in_vmem(value):
    return pltpu.with_memory_space_constraint(value, pltpu.VMEM)


def in_hbm(value):
    return pltpu.with_memory_space_constraint(value, pltpu.HBM)


def fetch(source, target, sems, pieces):
    copies = [
        pltpu.make_async_copy(source.at[piece], target.at[piece], sems.at[i])
        for i, piece in enumerate(pieces)
    ]
    for copy in copies:
        copy.start()
    return copies


def columns(count, width):
    return [(slice(None), pl.ds(i * width, width)) for i in range(count)]


def row_blocks(count, height):
    return [(pl.ds(i * height, height), slice(None)) for i in range(count)]


def turn(value, cos_table, sin_table):
    swapped = jnp.concatenate([value[:, HD // 2 :], value[:, : HD // 2]], axis=1)
    return value * cos_table + swapped * sin_table


def norm_kv_body(
    first_ref, lengths_ref, x_ref, gain_ref, w_ref, freq_ref, hid_ref, kv_ref, cos_ref, sin_ref
):
    index = lax.broadcasted_iota(jnp.int32, (TOK, 1), 0) + first_ref[0]
    place, start = index, jnp.int32(0)
    for s in range(lengths_ref.shape[0]):
        place = jnp.where(index >= start, index - start, place)
        start = start + lengths_ref[s]
    angle = place.astype(F32) * freq_ref[...]
    cos_ref[...] = jnp.cos(angle)
    sin = jnp.sin(angle)
    sin_ref[...] = jnp.where(lax.broadcasted_iota(jnp.int32, (TOK, HD), 1) < HD // 2, -sin, sin)
    x = x_ref[...].astype(F32)
    inv = lax.rsqrt(jnp.mean(x * x, axis=1, keepdims=True) + EPSILON)
    hid = (x * inv * gain_ref[...]).astype(BF)
    hid_ref[...] = hid
    kv = nn(hid, w_ref[...])
    kv_ref[:, :HD] = turn(kv[:, :HD], cos_ref[...], sin_ref[...]).astype(BF)
    kv_ref[:, HD:] = kv[:, HD:].astype(BF)


def query_body(hid_ref, cos_ref, sin_ref, w_ref, q_ref, buf, hid_buf, cos_buf, sin_buf, sems):
    pieces = columns(2, 512)
    weights = [pltpu.make_async_copy(w_ref.at[p], buf.at[p], sems.at[i]) for i, p in enumerate(pieces)]
    pairs = ((hid_ref, hid_buf), (cos_ref, cos_buf), (sin_ref, sin_buf))
    others = [pltpu.make_async_copy(a, b, sems.at[2 + i]) for i, (a, b) in enumerate(pairs)]
    for copy in (others[0], weights[0], others[1], others[2], weights[1]):
        copy.start()
    for copy in others:
        copy.wait()
    hid, cos_table, sin_table = hid_buf[...], cos_buf[...], sin_buf[...]
    for j in range(2):
        weights[j].wait()
        part = nn(hid, buf[:, j * 512 : j * 512 + 512])
        for h in range(4):
            q_ref[:, j * 512 + h * HD : j * 512 + h * HD + HD] = turn(
                part[:, h * HD : h * HD + HD], cos_table, sin_table
            ).astype(BF)


def local_body(own_ref, near_ref, far_ref, out_ref):
    total = own_ref[...] + near_ref[...].astype(F32) + far_ref[...].astype(F32)
    out_ref[...] = total.astype(BF)


def copies_body(in_ref, out_ref, sems):
    copies = [pltpu.make_async_copy(in_ref, out_ref.at[k], sems.at[k]) for k in range(4)]
    for copy in copies:
        copy.start()
    for copy in copies:
        copy.wait()


def add_body(pairs, places, *refs):
    sources = refs[: 2 * pairs]
    outs = refs[2 * pairs : 2 * pairs + (1 if places is None else 4)]
    buf, out_sems, in_sems, *held = refs[2 * pairs + len(outs) :]
    i = 0 if places is None else lax.axis_index(places)
    loads, sends = [], []
    for k in range(4):
        chunk = k if places is None else (i + k) % 4
        loads.append(
            [
                pltpu.make_async_copy(a.at[chunk], b.at[k], in_sems.at[4 * p + k])
                for p, (a, b) in enumerate(zip(sources, held))
            ]
        )
        out = outs[0].at[k] if places is None else outs[k]
        sends.append(pltpu.make_async_copy(buf.at[k], out, out_sems.at[k]))
    for chunk_loads in loads:
        for load in chunk_loads:
            load.start()
    for k in range(4):
        for load in loads[k]:
            load.wait()
        at = 0
        for p in range(pairs):
            total = held[2 * p][k].astype(F32) + held[2 * p + 1][k].astype(F32)
            buf[k, :, at : at + total.shape[1]] = total.astype(BF)
            at += total.shape[1]
        sends[k].start()
    for send in sends:
        send.wait()


def key_body(a_ref, b_ref, next_ref, cos_ref, sin_ref, grad_ref, d_ref, half_ref):
    total = a_ref[...].astype(F32) + b_ref[...].astype(F32) + next_ref[...].astype(F32)
    grad_ref[...] = total
    d_key = turn(total[:, :HD], cos_ref[...], -sin_ref[...]).astype(BF)
    d_value = total[:, HD:].astype(BF)
    d_ref[:, :HD] = d_key
    d_ref[:, HD:] = d_value
    first = lax.axis_index("mp") == 0
    half_ref[...] = jnp.where(first, d_key.astype(F32), d_value.astype(F32)).astype(BF)


def mixed_body(mid_ref, a_ref, b_ref, out_ref):
    out_ref[...] = (mid_ref[...] + (a_ref[...].astype(F32) + b_ref[...].astype(F32))).astype(BF)


def fence_body(out_ref):
    pass


def sum_body(groups, *refs):
    out_ref, at = refs[-1], 0
    for count in groups:
        group, refs = refs[:count], refs[count:]
        stacked = count == 1 and len(group[0].shape) == 3
        pieces = [group[0].at[k] for k in range(4)] if stacked else group
        total = sum(p[...].astype(F32) for p in pieces)
        out_ref[:, at : at + total.shape[1]] = total.astype(BF)
        at += total.shape[1]


def stack_sum_body(in_ref, out_ref, held, total, in_sems, out_sems):
    rows = [pl.ds(r * 64, 64) for r in range(4)]
    loads = [
        [pltpu.make_async_copy(in_ref.at[k, r], held.at[k, r], in_sems.at[4 * i + k]) for k in range(4)]
        for i, r in enumerate(rows)
    ]
    sends = [
        pltpu.make_async_copy(total.at[r], out_ref.at[r], out_sems.at[i]) for i, r in enumerate(rows)
    ]
    for group in loads:
        for load in group:
            load.start()
    for group, r, send in zip(loads, rows, sends):
        for load in group:
            load.wait()
        total[r] = sum(held[k, r].astype(F32) for k in range(4)).astype(BF)
        send.start()
    for send in sends:
        send.wait()


def spread_body(a_ref, b_ref, c_ref, d_ref, *refs):
    outs, buf, sems = refs[:8], refs[8], refs[9]
    total = a_ref[...].astype(F32) + b_ref[...].astype(F32)
    total = (total + c_ref[...].astype(F32) + d_ref[...].astype(F32)).astype(BF)
    for k in range(8):
        buf[k] = total[k * 32 : k * 32 + 32]
    xl, y = lax.axis_index("xl"), lax.axis_index("y")
    sends = []
    for k, out in enumerate(outs):
        place = (xl + k // 4) % 2 * 4 + (y + k % 4) % 4
        sends.append(pltpu.make_async_copy(buf.at[place], out, sems.at[k]))
    for send in sends:
        send.start()
    for send in sends:
        send.wait()


def my_rows(copies, arrays, bufs, sems):
    place = 0
    for axis in SEQ:
        place = place * SIZES[axis] + lax.axis_index(axis)
    rows = pl.ds(pl.multiple_of(place * 32, 32), 32)
    for i, (array, buf) in enumerate(zip(arrays, bufs)):
        copies.append(pltpu.make_async_copy(array.at[rows], buf, sems.at[i]))
        copies[-1].start()
    return copies


def row_sums(weights, grads):
    return jnp.sum(weights[...].astype(F32) * grads, axis=1, keepdims=True)


def finish_y_body(got_ref, wg_ref, wu_ref, gate_ref, up_ref, out_ref, sum_ref, wg, wu, sems):
    copies = my_rows([], (wg_ref, wu_ref), (wg, wu), sems)
    both = got_ref[0:128].astype(F32) + got_ref[128:256].astype(F32)
    part = [both[z * 32 : z * 32 + 32] for z in range(4)]
    out_ref[...] = part[0][:, 1408:] + part[1][:, 1408:] + part[2][:, 1408:] + part[3][:, 1408:]
    for copy in copies:
        copy.wait()
    total = jnp.zeros((32, 1), F32)
    for ref, weights, z in ((gate_ref, wg, 0), (up_ref, wu, 2)):
        for half in range(2):
            grads = part[z + half][:, :1408]
            lanes = slice(half * 1408, half * 1408 + 1408)
            ref[:, lanes] = grads
            total += row_sums(weights[:, lanes], grads)
    sum_ref[...] = jnp.broadcast_to(total, (32, 128))


def finish_body(*refs):
    pieces, (sum_b_ref, wq_ref, wk_ref, down_ref, query_ref, sum_ref, parts, wq, wk, sems) = (
        refs[:8],
        refs[8:],
    )
    copies = my_rows([], (wq_ref, wk_ref), (wq, wk), sems)
    rest = sum(p[:, 768:].astype(F32) for p in pieces)
    query_ref[...] = rest[:, :1024]
    y = lax.axis_index("y")
    for dy in range(4):
        part = pieces[dy][:, :768].astype(F32) + pieces[4 + dy][:, :768].astype(F32)
        parts[(y + 4 - dy) % 4] = part
    for i in range(4):
        low, high = ACT_STARTS[i] * 128, ACT_STARTS[i + 1] * 128
        down_ref[:, low:high] = parts[i][:, : high - low]
    for copy in copies:
        copy.wait()
    lane = lax.broadcasted_iota(jnp.int32, (32, 128), 1)
    keys = rest[:, 1024:]
    key_weights = wk[:, pl.ds(pl.multiple_of(lax.axis_index("mp") * HD, HD), HD)]
    sum_a = row_sums(wq, rest[:, :1024]) + row_sums(key_weights, keys)
    sum_ref[:, :128] = jnp.where(lane == 1, sum_b_ref[...], sum_a)
    sum_ref[:, 128:] = keys


def fill_bias(first_ref, lengths_ref, pads_ref, bias):
    first = first_ref[0]
    count = lengths_ref.shape[0]
    starts, lives = [], []
    begin = jnp.int32(0)
    for s in range(count):
        starts.append(begin)
        lives.append(begin + lengths_ref[s] - pads_ref[s])
        begin = begin + lengths_ref[s]
    for b in range(2):
        row = lax.broadcasted_iota(jnp.int32, (128, 1), 0) + b * 128
        col = lax.broadcasted_iota(jnp.int32, (1, 640), 1) + b * 128
        query = row + first
        key = col + (first - WINDOW)
        low = jnp.zeros((128, 1), jnp.int32)
        real = jnp.zeros((1, 640), jnp.int32)
        for s in range(count):
            low = jnp.where(query >= starts[s], starts[s], low)
            real = jnp.where((key >= starts[s]) & (key < lives[s]), 1, real)
        low = jnp.maximum(low, query - (WINDOW - 1))
        here = lax.broadcasted_iota(jnp.int32, (128, 640), 1) + b * 128 + (first - WINDOW)
        when = lax.broadcasted_iota(jnp.int32, (128, 640), 0) + b * 128 + first
        seen = jnp.where(jnp.broadcast_to(real, (128, 640)) > 0, here, when + 1)
        ok = (here == when) | ((here >= low) & (seen <= when))
        bias[b] = jnp.where(ok, 0.0, MASKED)


def two_heads(ref, b, pair):
    rows = slice(b * 128, b * 128 + 128)
    return jnp.concatenate(
        [ref[rows, h * HD : h * HD + HD] for h in (2 * pair, 2 * pair + 1)], axis=0
    )


def attend_body(
    first_ref, lengths_ref, pads_ref, q_ref, far_ref, near_ref, kv_ref, w_ref,
    attn_ref, lse_ref, out_ref, bias, keys, buf, sem,
):
    copy = pltpu.make_async_copy(w_ref, buf, sem.at[0])
    copy.start()
    fill_bias(first_ref, lengths_ref, pads_ref, bias)
    keys[0:256] = far_ref[...]
    keys[256:512] = near_ref[...]
    keys[512:768] = kv_ref[...]
    for b in range(2):
        k = keys[b * 128 : b * 128 + 640, :HD]
        v = keys[b * 128 : b * 128 + 640, HD:]
        for pair in range(4):
            scores = nt(two_heads(q_ref, b, pair), k) * (SCALE * LOG2E)
            scores = scores + jnp.concatenate([bias[b], bias[b]], axis=0)
            top = jnp.max(scores, axis=1, keepdims=True)
            exps = jnp.exp2(scores - top)
            total = jnp.sum(exps, axis=1, keepdims=True)
            out = nn(exps.astype(BF), v) / total
            lse_ref[b * 4 + pair] = top + jnp.log2(total)
            for h in range(2):
                lanes = slice((2 * pair + h) * HD, (2 * pair + h) * HD + HD)
                attn_ref[b * 128 : b * 128 + 128, lanes] = out[h * 128 : h * 128 + 128].astype(BF)
    copy.wait()
    attn = attn_ref[...]
    for j in range(4):
        out_ref[:, j * 512 : j * 512 + 512] = nn(attn, buf[:, j * 512 : j * 512 + 512]).astype(BF)


def d_act_body(cot_ref, w_ref, out_ref, flag_ref, buf, sems):
    copies = fetch(w_ref, buf, sems, row_blocks(2, 1408))
    cot = cot_ref[...]
    for j in range(2):
        copies[j].wait()
        rows = slice(j * 1408, j * 1408 + 1408)
        out_ref[:, rows] = nt(cot, buf[rows]).astype(BF)
    flag_ref[...] = cot[0:16, 0:128]


def middle_body(x_ref, a_ref, b_ref, gain_ref, mid_ref, hid_ref):
    mid = x_ref[...].astype(F32) + (a_ref[...].astype(F32) + b_ref[...].astype(F32))
    mid_ref[...] = mid
    inv = lax.rsqrt(jnp.mean(mid * mid, axis=1, keepdims=True) + EPSILON)
    hid = (mid * inv * gain_ref[...]).astype(BF)
    hid_ref[...] = hid


ACT_STARTS = (0, 6, 12, 17, 22)


def act_place(tile):
    part = max(i for i in range(4) if ACT_STARTS[i] <= tile)
    return part, (tile - ACT_STARTS[part]) * 128


FFN_STARTS = (0, 4, 12, 22)


def ffn_body(
    hid_ref, d_act_ref, wg_ref, wu_ref,
    d0, d1, d2, d3, act_out, out_ref,
    bufg, bufu, d_buf, act_buf, d_act_buf, semg, semu, sem_in, sem_out,
):
    pieces = [
        (slice(None), pl.ds(low * 128, (high - low) * 128))
        for low, high in zip(FFN_STARTS, FFN_STARTS[1:])
    ]
    gates = [pltpu.make_async_copy(wg_ref.at[p], bufg.at[p], semg.at[i]) for i, p in enumerate(pieces)]
    ups = [pltpu.make_async_copy(wu_ref.at[p], bufu.at[p], semu.at[i]) for i, p in enumerate(pieces)]
    d_act_in = pltpu.make_async_copy(d_act_ref, d_act_buf, sem_in.at[0])
    gates[0].start()
    ups[0].start()
    d_act_in.start()
    for g, u in zip(gates[1:], ups[1:]):
        g.start()
        u.start()
    hid = hid_ref[...]
    for j in range(3):
        low, high = FFN_STARTS[j], FFN_STARTS[j + 1]
        cols = slice(low * 128, high * 128)
        gates[j].wait()
        gate = nn(hid, bufg[:, cols])
        ups[j].wait()
        up = nn(hid, bufu[:, cols])
        if j == 0:
            d_act_in.wait()
        sigm = 1.0 / (1.0 + jnp.exp(-gate))
        silu = gate * sigm
        d_act = d_act_buf[:, cols].astype(F32)
        act = (silu * up).astype(BF)
        d_up = (d_act * silu).astype(BF)
        d_gate = (d_act * up * (sigm + silu * (1.0 - sigm))).astype(BF)
        for tile in range(low, high):
            lanes = slice((tile - low) * 128, (tile - low) * 128 + 128)
            part, at = act_place(tile)
            act_buf[part, :, at : at + 128] = act[:, lanes]
            quarter, at = tile // 11, (tile % 11) * 128
            d_buf[quarter, :, at : at + 128] = d_gate[:, lanes]
            d_buf[2 + quarter, :, at : at + 128] = d_up[:, lanes]
    for part in (2, 3):
        act_buf[part, :, 640:768] = jnp.zeros((TOK, 128), BF)
    z = lax.axis_index("z")
    sends = [pltpu.make_async_copy(act_buf, act_out, sem_out.at[4])]
    for k, d_out in enumerate((d0, d1, d2, d3)):
        sends.append(pltpu.make_async_copy(d_buf.at[(z + k) % 4], d_out, sem_out.at[k]))
    for send in sends:
        send.start()
    for i in range(2):
        rows = slice(i * 1024, i * 1024 + 1024)
        total = nt(d_buf[0], bufg[rows, :1408]) + nt(d_buf[1], bufg[rows, 1408:])
        total += nt(d_buf[2], bufu[rows, :1408]) + nt(d_buf[3], bufu[rows, 1408:])
        out_ref[:, rows] = total.astype(BF)
    for send in sends:
        send.wait()


def down_body(act_ref, w_ref, out_ref, buf, sems):
    copies = fetch(w_ref, buf, sems, columns(4, 512))
    for i in range(4):
        copies[i].wait()
        cols = slice(i * 512, i * 512 + 512)
        total = jnp.zeros((TOK, 512), F32)
        for part in range(4):
            low, high = ACT_STARTS[part] * 128, ACT_STARTS[part + 1] * 128
            total += nn(act_ref[part, :, : high - low], buf[low:high, cols])
        out_ref[:, cols] = total.astype(BF)


def back_body(
    cot_ref, a_ref, b_ref, mid_ref, gain_ref, w_ref,
    d_mid_ref, low_ref, d_attn_ref, buf, d_mid_buf, low_buf, sem,
):
    copy = pltpu.make_async_copy(w_ref, buf, sem.at[0])
    copy.start()
    mid = mid_ref[...]
    inv = lax.rsqrt(jnp.mean(mid * mid, axis=1, keepdims=True) + EPSILON)
    normed = mid * inv
    e = (a_ref[...].astype(F32) + b_ref[...].astype(F32)) * gain_ref[...]
    d_mid = cot_ref[...].astype(F32) + inv * (
        e - normed * jnp.mean(e * normed, axis=1, keepdims=True)
    )
    d_mid_buf[...] = d_mid
    low = d_mid.astype(BF)
    low_buf[...] = low
    sends = [
        pltpu.make_async_copy(d_mid_buf, d_mid_ref, sem.at[1]),
        pltpu.make_async_copy(low_buf, low_ref, sem.at[2]),
    ]
    for send in sends:
        send.start()
    copy.wait()
    d_attn_ref[...] = nt(low, buf[...]).astype(BF)
    for send in sends:
        send.wait()


def attend_back_body(
    first_ref, lengths_ref, pads_ref, q_ref, far_ref, near_ref, kv_ref, attn_ref, d_attn_ref, lse_ref,
    cos_ref, sin_ref, w_ref,
    dq_ref, d_far_ref, d_near_ref, d_own_ref, out_ref,
    bias, keys, stack_p, stack_d, stack_q, stack_o, total, buf, sem,
):
    copy = pltpu.make_async_copy(w_ref, buf, sem.at[0])
    copy.start()
    fill_bias(first_ref, lengths_ref, pads_ref, bias)
    keys[0:256] = far_ref[...]
    keys[256:512] = near_ref[...]
    keys[512:768] = kv_ref[...]
    total[...] = jnp.zeros_like(total)
    for b in range(2):
        window = slice(b * 128, b * 128 + 640)
        rows = slice(b * 128, b * 128 + 128)
        k = keys[window, :HD]
        v = keys[window, HD:]
        for pair in range(4):
            here = slice(pair * 256, pair * 256 + 256)
            q2 = two_heads(q_ref, b, pair)
            do2 = two_heads(d_attn_ref, b, pair)
            o2 = two_heads(attn_ref, b, pair)
            stack_q[here] = q2
            stack_o[here] = do2
            delta = jnp.sum(do2.astype(F32) * o2.astype(F32), axis=1, keepdims=True)
            scores = nt(q2, k) * (SCALE * LOG2E) + jnp.concatenate([bias[b], bias[b]], axis=0)
            prob = jnp.exp2(scores - lse_ref[b * 4 + pair])
            stack_p[here] = prob.astype(BF)
            d_score = (prob * (nt(do2, v) - delta)).astype(BF)
            stack_d[here] = d_score
            dq = nn(d_score, k) * SCALE
            for h in range(2):
                lanes = slice((2 * pair + h) * HD, (2 * pair + h) * HD + HD)
                dq_ref[rows, lanes] = turn(
                    dq[h * 128 : h * 128 + 128], cos_ref[rows], -sin_ref[rows]
                ).astype(BF)
        total[window, :HD] += tn(stack_d[...], stack_q[...]) * SCALE
        total[window, HD:] += tn(stack_p[...], stack_o[...])
    d_far_ref[...] = total[0:256].astype(BF)
    d_near_ref[...] = total[256:512].astype(BF)
    d_own_ref[...] = total[512:768]
    copy.wait()
    dq = dq_ref[...]
    for j in range(4):
        rows = slice(j * 512, j * 512 + 512)
        out_ref[:, rows] = nt(dq, buf[rows]).astype(BF)


def last_body(x_ref, d_mid_ref, a_ref, b_ref, d_kv_ref, w_ref, gain_ref, out_ref):
    x = x_ref[...].astype(F32)
    inv = lax.rsqrt(jnp.mean(x * x, axis=1, keepdims=True) + EPSILON)
    normed = x * inv
    d_hid = a_ref[...].astype(F32) + b_ref[...].astype(F32) + nt(d_kv_ref[...], w_ref[...])
    e = d_hid * gain_ref[...]
    out = d_mid_ref[...] + inv * (e - normed * jnp.mean(e * normed, axis=1, keepdims=True))
    out_ref[...] = out.astype(BF)


def pair_each(lefts, rights):
    return [list(zip(lefts, rights, strict=True))]


def pair_stacks(lefts, rights):
    return [[(lefts[0].at[k], rights[0].at[k]) for k in range(4)]]


def pair_two(lefts, rights):
    return [[(lefts[0], right)] for right in rights]


def grad_body(axis, pairing, lefts, rights, *refs):
    sources, outs = refs[: lefts + rights], refs[lefts + rights : lefts + rights + 2]
    buf, out_sems, in_sems, *held = refs[lefts + rights + 2 :]
    stacked = len(sources[0].shape) == 3
    pieces = [(a, b) for a, b in zip(sources, held)]
    if stacked:
        pieces = [(a.at[k], b.at[k]) for a, b in pieces for k in range(4)]
    count = 4 if stacked else lefts
    loads = [pltpu.make_async_copy(a, b, in_sems.at[i]) for i, (a, b) in enumerate(pieces)]
    for i in range(max(count, len(loads) - count)):
        for load in loads[:count][i : i + 1] + loads[count:][i : i + 1]:
            load.start()
    groups = pairing(held[:lefts], held[lefts:])
    if count == 1:
        for load in loads:
            load.wait()
    me = lax.axis_index("c")
    sends = []
    for step in range(8):
        xl, y = step % 2, step // 2
        block = xl * 4 + y
        cols = slice(block * 256, block * 256 + 256)
        at = 0
        for group in groups:
            total = None
            for i, (left, right) in enumerate(group):
                if step == 0 and count > 1:
                    loads[i].wait()
                    loads[count + i].wait()
                part = tn(left[:, cols], right[...])
                total = part if total is None else total + part
            total = total.astype(BF)
            lanes = slice(at, at + total.shape[1])
            at += total.shape[1]
            for z in range(4):
                chunk, row = (y, xl * 128 + z * 32) if axis == "y" else (z, xl * 128 + y * 32)
                for core in range(2):
                    rows = total[z * 64 + core * 32 : z * 64 + core * 32 + 32]
                    buf[(me + core) % 2, chunk, row : row + 32, lanes] = rows
        if axis == "y" and xl == 1:
            sends += [
                pltpu.make_async_copy(buf.at[k, y], out.at[y], out_sems.at[4 * k + y])
                for k, out in enumerate(outs)
            ]
            for send in sends[-2:]:
                send.start()
        if axis == "z":
            rows = pl.ds(xl * 128 + y * 32, 32)
            sends += [
                pltpu.make_async_copy(buf.at[k, :, rows], out.at[:, rows], out_sems.at[8 * k + step])
                for k, out in enumerate(outs)
            ]
            for send in sends[-2:]:
                send.start()
    for send in sends:
        send.wait()


def grad(axis, pairing, lefts, rights, n, after=(), carry=(), flops=1000):
    args = tuple(map(in_hbm, (*lefts, *rights)))
    return kernel_call(
        functools.partial(grad_body, axis, pairing, len(lefts), len(rights)),
        (shape(4, 256, n),) * 2,
        args,
        [HBM] * len(args),
        [
            pltpu.VMEM((2, 4, 256, n), BF),
            pltpu.SemaphoreType.DMA((16,)),
            pltpu.SemaphoreType.DMA((8 if args[0].ndim == 3 else len(args),)),
            *[pltpu.VMEM(a.shape, BF) for a in args],
        ],
        flops=flops,
        after=after,
        carry=carry,
        out_specs=(HBM,) * 2,
    )


def step_to(value, axis, steps):
    count = SIZES[axis]
    return lax.ppermute(value, axis, [(i, (i + steps) % count) for i in range(count)])


def shifted(value, steps):
    count = 64
    first, last = max(0, -steps), min(count, count - steps)
    return lax.ppermute(value, SEQ, [(i, i + steps) for i in range(first, last)])


def pick(stack, index):
    return lax.dynamic_index_in_dim(stack, index, 0, keepdims=False)


def fence(after, carry=()):
    result = kernel_call(
        fence_body, shape(8, 128, dtype=F32), (), [], after=after, carry=carry, flops=3 * 10**10, out_specs=(HBM,)
    )
    return result if carry else (result, ())


def from_others(value, axis):
    return [value] + [step_to(value, axis, k) for k in (1, 2, 3)]


def deal(parts, axis):
    return [parts[0]] + [step_to(parts[k], axis, k) for k in (1, 2, 3)]


def add_cores(pairs, axis=None, after=(), carry=(), flops=1000, near=False):
    rows, n = pairs[0][0].shape[1], sum(own.shape[2] for own, _ in pairs)
    args = tuple(a for pair in pairs for a in (in_hbm(pair[0]), (in_vmem if near else in_hbm)(pair[1])))
    outs = shape(4, rows, n) if axis is None else (shape(rows, n),) * 4
    return kernel_call(
        functools.partial(add_body, len(pairs), axis),
        outs,
        args,
        [HBM] * len(args),
        [
            pltpu.VMEM((4, rows, n), BF),
            pltpu.SemaphoreType.DMA((4,)),
            pltpu.SemaphoreType.DMA((4 * len(args),)),
            *[pltpu.VMEM(a.shape, BF) for a in args],
        ],
        after=after,
        carry=carry,
        out_specs=(HBM,) if axis is None else (HBM,) * 4,
        flops=flops,
    )


def swap(parts, axis):
    return lax.all_to_all(parts, axis, 0, 0, tiled=True)


def around(value, dx, dy):
    moves = [(a * 4 + b, (a + dx) % 2 * 4 + (b + dy) % 4) for a in range(2) for b in range(4)]
    return lax.ppermute(value, ("xl", "y"), moves)


def scatter(value, axes):
    return lax.all_to_all(value, axes, 0, 0, tiled=True)


def shards(
    tokens,
    cotangent,
    next_kv_grad,
    seq_lengths,
    pad_counts,
    norm_attn,
    norm_ffn,
    w_query,
    w_keyval,
    w_out,
    w_gate,
    w_up,
    w_down,
):
    place_in_seq = lax.axis_index(SEQ)
    first = (place_in_seq * TOK).astype(jnp.int32)
    half = HD // 2
    freqs = jnp.exp(-jnp.log(THETA) * jnp.arange(half, dtype=F32) * 2.0 / HD)
    freqs = jnp.concatenate([freqs, freqs])[None]
    first = first[None]

    gain_a, gain_b = norm_attn[None], norm_ffn[None]

    hid_a, shared, cos_table, sin_table = kernel_call(
        norm_kv_body,
        (shape(TOK, D), shape(TOK, 256), shape(TOK, HD, dtype=F32), shape(TOK, HD, dtype=F32)),
        (first, seq_lengths, tokens, gain_a, w_keyval, freqs),
        [SMEM] * 2 + [VMEM] * 4,
    )
    near, far = shifted(shared, 1), shifted(shared, 2)
    query = kernel_call(
        query_body,
        shape(TOK, 1024),
        (hid_a, cos_table, sin_table, w_query),
        [HBM] * 4,
        [
            pltpu.VMEM((D, 1024), BF),
            pltpu.VMEM((TOK, D), BF),
            pltpu.VMEM((TOK, HD), F32),
            pltpu.VMEM((TOK, HD), F32),
            pltpu.SemaphoreType.DMA((5,)),
        ],
    )
    keys_scratch = [pltpu.VMEM((2, 128, 640), F32), pltpu.VMEM((768, 256), BF)]
    attn, lse, branch = kernel_call(
        attend_body,
        (shape(TOK, 1024), shape(8, 256, 1, dtype=F32), shape(TOK, D)),
        (first, seq_lengths, pad_counts, query, far, near, shared, w_out),
        [SMEM] * 3 + [VMEM] * 4 + [HBM],
        keys_scratch + [pltpu.VMEM((1024, D), BF), pltpu.SemaphoreType.DMA((1,))],
    )
    branch_other = step_to(branch, "mp", 1)
    copies = kernel_call(
        copies_body,
        shape(4, TOK, D),
        (cotangent,),
        [VMEM],
        [pltpu.SemaphoreType.DMA((4,))],
        after=(branch,),
        out_specs=(HBM,),
    )
    cot_all = swap(copies, "y")
    d_act, d_act_flag = kernel_call(
        d_act_body,
        (shape(TOK, FF), shape(16, 128)),
        (cotangent, w_down),
        [VMEM, HBM],
        [pltpu.VMEM((FF, D), BF), pltpu.SemaphoreType.DMA((2,))],
        after=(copies,),
    )
    middle, hid_b = kernel_call(
        middle_body,
        (shape(TOK, D, dtype=F32), shape(TOK, D)),
        (tokens, branch, in_vmem(branch_other), gain_b),
        [VMEM] * 4,
        vmem=32,
        after=(d_act_flag,),
    )
    hid_b_all = from_others(hid_b, "z")
    *d_gu, act, d_hid_b = kernel_call(
        ffn_body,
        (shape(TOK, 1408),) * 4 + (shape(4, TOK, 768), shape(TOK, D)),
        (hid_b, d_act, w_gate, w_up),
        [VMEM, HBM, HBM, HBM],
        [
            pltpu.VMEM((D, FF), BF),
            pltpu.VMEM((D, FF), BF),
            pltpu.VMEM((4, TOK, 1408), BF),
            pltpu.VMEM((4, TOK, 768), BF),
            pltpu.VMEM((TOK, FF), BF),
            pltpu.SemaphoreType.DMA((3,)),
            pltpu.SemaphoreType.DMA((3,)),
            pltpu.SemaphoreType.DMA((1,)),
            pltpu.SemaphoreType.DMA((5,)),
        ],
        out_specs=(HBM,) * 5 + (VMEM,),
        flops=3 * 10**10 + 2,
    )
    d_hid_b_other = step_to(d_hid_b, "mp", 1)
    act_all = swap(act, "y")
    ffn = kernel_call(
        down_body,
        shape(TOK, D),
        (act, w_down),
        [VMEM, HBM],
        [pltpu.VMEM((FF, D), BF), pltpu.SemaphoreType.DMA((4,))],
        after=(d_hid_b, cot_all),
    )
    flag, d_gu[2:] = fence((ffn, *hid_b_all[1:]), tuple(d_gu[2:]))
    d_gu = deal(d_gu, "z")
    (d_middle, d_middle_b, d_attn), (held_ffn,) = kernel_call(
        back_body,
        (shape(TOK, D, dtype=F32), shape(TOK, D), shape(TOK, 1024)),
        (cotangent, d_hid_b, d_hid_b_other, middle, gain_b, w_out),
        [VMEM] * 5 + [HBM],
        [
            pltpu.VMEM((1024, D), BF),
            pltpu.VMEM((TOK, D), F32),
            pltpu.VMEM((TOK, D), BF),
            pltpu.SemaphoreType.DMA((3,)),
        ],
        after=(flag,),
        carry=(ffn,),
        out_specs=(HBM, HBM, VMEM),
    )
    d_query, d_far, d_near, d_own, part_a = kernel_call(
        attend_back_body,
        (
            shape(TOK, 1024),
            shape(256, 256),
            shape(256, 256),
            shape(256, 256, dtype=F32),
            shape(TOK, D),
        ),
        (
            first, seq_lengths, pad_counts, query, far, near, shared, attn, d_attn, lse,
            cos_table, sin_table, w_query,
        ),
        [SMEM] * 3 + [VMEM] * 9 + [HBM],
        keys_scratch
        + [
            pltpu.VMEM((1024, 640), BF),
            pltpu.VMEM((1024, 640), BF),
            pltpu.VMEM((1024, HD), BF),
            pltpu.VMEM((1024, HD), BF),
            pltpu.VMEM((768, 256), F32),
            pltpu.VMEM((D, 1024), BF),
            pltpu.SemaphoreType.DMA((1,)),
        ],
    )
    def side_by_side(groups, after=(), flops=1000):
        n = sum(group[0].shape[-1] for group in groups)
        flat = [a for group in groups for a in group]
        return kernel_call(
            functools.partial(sum_body, [len(group) for group in groups]),
            shape(TOK, n),
            flat,
            [VMEM] * len(flat),
            after=after,
            flops=flops,
        )

    g_out = grad("y", pair_each, [d_middle_b], [attn], 1024, after=(part_a,))
    out_got = step_to(g_out[1], "c", 1)
    g_down = grad("z", pair_stacks, [cot_all], [act_all], 768, after=(g_out[0],))
    down_got = step_to(g_down[1], "c", 1)
    ready, _ = fence((g_down[0], *d_gu[1:]))
    local = kernel_call(
        local_body,
        shape(TOK, 256),
        (d_own, shifted(d_near, -1), shifted(d_far, -2)),
        [VMEM] * 3,
        after=(ready,),
    )
    g_gu = grad("y", pair_each, hid_b_all, d_gu, 1408, after=(local, out_got, down_got))
    gu_got = step_to(g_gu[1], "c", 1)
    shared_grad, d_keyval, d_half = kernel_call(
        key_body,
        (shape(TOK, 256, dtype=F32), shape(TOK, 256), shape(TOK, HD)),
        (local, step_to(local, "mp", 1), next_kv_grad, cos_table, sin_table),
        [VMEM] * 5,
        after=(g_gu[0],),
    )
    g_qkv = grad("z", pair_two, [hid_a], [d_query, d_half], 1152, after=(g_gu[0],), flops=3 * 10**10 + 1)
    qkv_got = step_to(g_qkv[1], "c", 1)
    y_sums, (part_a, held_ffn) = add_cores(
        [(g_gu[0], gu_got), (g_out[0], out_got)], after=(g_qkv[0],), carry=(part_a, held_ffn), near=True
    )
    y_parts = swap(y_sums, "y")
    z_sums = add_cores(
        [(g_down[0], down_got), (g_qkv[0], qkv_got)], "z", after=(y_sums,), flops=10**11 + 1
    )
    z_parts = deal(z_sums, "z")
    part_a_other = step_to(part_a, "mp", 1)
    ffn_other = step_to(held_ffn, "mp", 1)
    mixed = kernel_call(
        mixed_body, shape(TOK, D), (middle, held_ffn, ffn_other), [VMEM] * 3, after=(z_parts[0],)
    )
    input_grad = kernel_call(
        last_body,
        shape(TOK, D),
        (tokens, d_middle, part_a, part_a_other, d_keyval, w_keyval, gain_a),
        [VMEM] * 7,
        after=(mixed,),
    )
    in_y = kernel_call(
        stack_sum_body,
        shape(TOK, y_parts.shape[2]),
        (in_hbm(y_parts),),
        [HBM],
        [
            pltpu.VMEM(y_parts.shape, BF),
            pltpu.VMEM((TOK, y_parts.shape[2]), BF),
            pltpu.SemaphoreType.DMA((16,)),
            pltpu.SemaphoreType.DMA((4,)),
        ],
        after=(input_grad,),
        out_specs=(HBM,),
    )
    from_xz = scatter(in_y, ("xl", "z"))
    z_spread = kernel_call(
        spread_body,
        (shape(32, 1920),) * 8,
        z_parts,
        [VMEM] * 4,
        [pltpu.VMEM((8, 32, 1920), BF), pltpu.SemaphoreType.DMA((8,))],
        after=(in_y,),
        out_specs=(HBM,) * 8,
        flops=10**11,
    )
    s_gate, s_up, s_out, sum_b = kernel_call(
        finish_y_body,
        (
            shape(32, FF, dtype=F32),
            shape(32, FF, dtype=F32),
            shape(32, 1024, dtype=F32),
            shape(32, 128, dtype=F32),
        ),
        (from_xz, w_gate, w_up),
        [VMEM, HBM, HBM],
        [pltpu.VMEM((32, FF), BF), pltpu.VMEM((32, FF), BF), pltpu.SemaphoreType.DMA((2,))],
    )
    from_xy = [z_spread[0]] + [around(z_spread[k], k // 4, k % 4) for k in range(1, 8)]
    s_down, s_query, sums = kernel_call(
        finish_body,
        (
            shape(32, FF, dtype=F32),
            shape(32, 1024, dtype=F32),
            shape(32, 256, dtype=F32),
        ),
        (*from_xy, sum_b, w_query, w_keyval),
        [VMEM] * 9 + [HBM] * 2,
        [
            pltpu.VMEM((4, 32, 768), F32),
            pltpu.VMEM((32, 1024), BF),
            pltpu.VMEM((32, 256), BF),
            pltpu.SemaphoreType.DMA((2,)),
        ],
    )
    s_down = lax.optimization_barrier(s_down).T
    s_out = lax.optimization_barrier(s_out).T

    mine = place_in_seq * 32
    others = step_to(sums, "mp", 1)
    both = sums[:, :128] + others[:, :128]
    first = lax.axis_index("mp") == 0
    keys, values = jnp.where(first, sums, others), jnp.where(first, others, sums)
    s_keyval = jnp.concatenate([keys[:, 128:], values[:, 128:]], axis=1)
    s_gain_a = both[:, 0] / lax.dynamic_slice_in_dim(norm_attn, mine, 32, 0)
    s_gain_b = both[:, 1] / lax.dynamic_slice_in_dim(norm_ffn, mine, 32, 0)
    return (
        mixed,
        input_grad,
        shared,
        shared_grad,
        s_gain_a,
        s_gain_b,
        s_query,
        s_keyval,
        s_out,
        s_gate,
        s_up,
        s_down,
    )


def solution(mesh):
    fine = Mesh(mesh.devices.reshape(2, 4, 4, 2, 2), SEQ + ("mp",))
    rows = P(SEQ, None)
    placed = (
        rows,
        rows,
        rows,
        P(),
        P(),
        P(),
        P(),
        P(None, "mp"),
        P(),
        P("mp", None),
        P(None, "mp"),
        P(None, "mp"),
        P("mp", None),
    )
    return jax.shard_map(
        shards,
        mesh=fine,
        in_specs=placed,
        out_specs=(
            rows,
            rows,
            rows,
            rows,
            P(SEQ),
            P(SEQ),
            P(SEQ, "mp"),
            rows,
            P("mp", SEQ),
            P(SEQ, "mp"),
            P(SEQ, "mp"),
            P("mp", SEQ),
        ),
        check_vma=False,
    )
```
